128 devices in a mesh: dp: 8 (over z, x_hi), fsdp: 16 (over x_lo, y, core).
Axes of the slice: x: 4 (x_hi: 2, x_lo: 2; x = x_hi * 2 + x_lo), y: 4, z: 4, core: 2. Of those that a mesh axis runs over, the one named last changes fastest.
Arguments:
- tokens: bfloat16 [65536, 768], P(('dp', 'fsdp')), may hold values from -6 to 6
- chip_lengths: int32 [256], P(('dp', 'fsdp')), may hold values from 64 to 256, as said below
- chip_ids: int32 [256], P(('dp', 'fsdp')), may hold values from 0 to 31, as said below
- positions: int32 [65536], P(('dp', 'fsdp')), may hold values from -1 to 1023, as said below
- ln1_gain: bfloat16 [768], P(('dp', 'fsdp')), may hold values from 0.099609375 to 1.8984375
- ln1_bias: bfloat16 [768], P(('dp', 'fsdp')), may hold values from -3 to 3
- qkv_weight: bfloat16 [768, 2304], P(('dp', 'fsdp')), may hold values from -0.21875 to 0.21875
- out_weight: bfloat16 [768, 768], P(('dp', 'fsdp')), may hold values from -0.875 to 0.875
- ln2_gain: bfloat16 [768], P(('dp', 'fsdp')), may hold values from 0.099609375 to 1.8984375
- ln2_bias: bfloat16 [768], P(('dp', 'fsdp')), may hold values from -3 to 3
- fc1_weight: bfloat16 [768, 3072], P(('dp', 'fsdp')), may hold values from -0.21875 to 0.21875
- fc1_bias: bfloat16 [3072], P(('dp', 'fsdp')), may hold values from -3 to 3
- fc2_weight: bfloat16 [3072, 768], P(('dp', 'fsdp')), may hold values from -0.109375 to 0.109375
- fc2_bias: bfloat16 [768], P(('dp', 'fsdp')), may hold values from -3 to 3
- dec_weight: bfloat16 [768, 512], P(('dp', 'fsdp')), may hold values from -0.21875 to 0.21875
- dec_bias: bfloat16 [512], P(('dp', 'fsdp')), may hold values from -3 to 3
- mask_token: bfloat16 [512], P(('dp', 'fsdp')), may hold values from -4 to 4
- grid_cotangent: bfloat16 [256, 1024, 512], P('dp', 'fsdp'), may hold values from -6 to 6
Outputs:
- full_grid: bfloat16 [256, 1024, 512], P('dp', 'fsdp')
- tokens_grad: float32 [65536, 768], P(('dp', 'fsdp'))
- ln1_gain_grad: float32 [768], P(('dp', 'fsdp'))
- ln1_bias_grad: float32 [768], P(('dp', 'fsdp'))
- qkv_weight_grad: float32 [768, 2304], P(('dp', 'fsdp'))
- out_weight_grad: float32 [768, 768], P(('dp', 'fsdp'))
- ln2_gain_grad: float32 [768], P(('dp', 'fsdp'))
- ln2_bias_grad: float32 [768], P(('dp', 'fsdp'))
- fc1_weight_grad: float32 [768, 3072], P(('dp', 'fsdp'))
- fc1_bias_grad: float32 [3072], P(('dp', 'fsdp'))
- fc2_weight_grad: float32 [3072, 768], P(('dp', 'fsdp'))
- fc2_bias_grad: float32 [768], P(('dp', 'fsdp'))
- dec_weight_grad: float32 [768, 512], P(('dp', 'fsdp'))
- dec_bias_grad: float32 [512], P(('dp', 'fsdp'))
- mask_token_grad: float32 [512], P(('dp', 'fsdp'))
The draws below stay inside these ranges and needn't reach their ends.
Inputs may be any that keep to these rules, and one draw needn't show every extreme that they name: `chip_lengths`: each slot holds one chip of 256 or 64 visible patches; every pack has at least one of each kind; a chip's rows are 2 plus its visible patches. `chip_ids`: within each group of 32 slots (one index of dp) the values are a permutation. `positions`: each chip's first two rows (class and time-location tokens) and the padding rows after the last chip have -1; the other rows of a chip hold distinct cells below 4 times its length.
All inputs are finite; a program needn't handle non-finite values.
Results may differ from the reference program's by a relative error of at most 0.018.
Values may be sent and summed in bfloat16 or wider, within the bound.
A program may use at most 192 MiB of HBM per device.

```python
import jax
import jax.numpy as jnp
from jax import lax

D = 768
HEADS = 12
HEAD_DIM = 64
FF = 3072
DEC = 512
GRID = 1024
SLOTS_DEV = 2
PACK = 512
TOKENS = 65536
CHIPS = 256
GROUP_CHIPS = 32


def chip_layout(key):
    device_count = TOKENS // PACK
    device_keys = jax.random.split(jax.random.fold_in(key, 11), device_count)

    def per_device(dkey):
        count_key, order_key, cell_key = jax.random.split(dkey, 3)
        big_count = jax.random.randint(count_key, (), max(SLOTS_DEV // 4, 1), SLOTS_DEV // 2 + 1)
        order = jax.random.permutation(order_key, SLOTS_DEV)
        lengths = jnp.where(order < big_count, GRID // 4, GRID // 16).astype(jnp.int32)
        cell_ranks = jax.vmap(lambda kk: jax.random.permutation(kk, GRID))(jax.random.split(cell_key, SLOTS_DEV))
        cell_ranks = cell_ranks.astype(jnp.int32)
        outside = (cell_ranks >= (4 * lengths)[:, None]).astype(jnp.int32)
        arrange = jnp.argsort(outside, axis=1, stable=True)
        chosen = jnp.take_along_axis(cell_ranks, arrange, axis=1)
        ends = jnp.cumsum(lengths + 2)
        starts = ends - (lengths + 2)
        row_index = jnp.arange(PACK, dtype=jnp.int32)
        segment = jnp.sum((row_index[:, None] >= ends[None, :]).astype(jnp.int32), axis=1)
        clipped = jnp.minimum(segment, SLOTS_DEV - 1)
        inner = row_index - starts[clipped] - 2
        live = (segment < SLOTS_DEV) & (inner >= 0)
        picked = chosen[clipped, jnp.clip(inner, 0, GRID - 1)]
        cells = jnp.where(live, picked, -1).astype(jnp.int32)
        return (lengths, cells)
    lengths, cells = jax.vmap(per_device)(device_keys)
    group_count = CHIPS // GROUP_CHIPS
    group_keys = jax.random.split(jax.random.fold_in(key, 23), group_count)
    chip_rows = jax.vmap(lambda kk: jax.random.permutation(kk, GROUP_CHIPS))(group_keys)
    return (lengths.reshape(-1), chip_rows.reshape(-1).astype(jnp.int32), cells.reshape(-1))


def draw_chip_lengths(key, part):
    return chip_layout(key)[0]


def draw_chip_ids(key, part):
    return chip_layout(key)[1]


def draw_positions(key, part):
    return chip_layout(key)[2]


def steps_of(stream_key, dims, cuts, least, top_value):
    level, own = 1.0, jax.random.fold_in(stream_key, 6)
    for dim, parts in cuts:
        draws = jnp.exp(jax.random.uniform(jax.random.fold_in(own, dim), (parts,), jnp.float32, least / len(cuts), top_value / len(cuts)))
        level = level * jnp.repeat(draws, dims[dim] // parts).reshape([-1 if axis == dim else 1 for axis in range(len(dims))])
    return level


def centred(key, extent, width, bound, shards=(), kind=jnp.bfloat16):
    values = width * jax.random.normal(key, extent, jnp.float32)
    if shards:
        values = values * steps_of(key, extent, shards, -0.22, 0.18)
    return jnp.clip(values, -bound, bound).astype(kind)


def setup_inputs(seed: int = 0) -> dict:
    key_of = jax.random.split(jax.random.key(seed), 19)
    tokens = centred(key_of[0], (TOKENS, D), 1.0, 6.0, ((0, 128),))
    chip_lengths = draw_chip_lengths(jax.random.fold_in(key_of[18], 71), 0)
    chip_ids = draw_chip_ids(jax.random.fold_in(key_of[18], 71), 0)
    positions = draw_positions(jax.random.fold_in(key_of[18], 71), 0)
    ln1_gain = jnp.clip(1.0 + 0.18 * jax.random.normal(key_of[4], (D,), jnp.float32), 0.099609375, 1.8984375).astype(jnp.bfloat16)
    ln1_bias = centred(key_of[5], (D,), 0.3, 3.0, ((0, 128),))
    qkv_weight = centred(key_of[6], (D, 3 * D), D ** -0.5, 0.21875, ((0, 128),))
    out_weight = centred(key_of[7], (D, D), (D // 16) ** -0.5, 0.875, ((0, 128),))
    ln2_gain = jnp.clip(1.0 + 0.18 * jax.random.normal(key_of[8], (D,), jnp.float32), 0.099609375, 1.8984375).astype(jnp.bfloat16)
    ln2_bias = centred(key_of[9], (D,), 0.3, 3.0, ((0, 128),))
    fc1_weight = centred(key_of[10], (D, FF), D ** -0.5, 0.21875, ((0, 128),))
    fc1_bias = centred(key_of[11], (FF,), 0.3, 3.0, ((0, 128),))
    fc2_weight = centred(key_of[12], (FF, D), FF ** -0.5, 0.109375, ((0, 128),))
    fc2_bias = centred(key_of[13], (D,), 0.3, 3.0, ((0, 128),))
    dec_weight = centred(key_of[14], (D, DEC), D ** -0.5, 0.21875, ((0, 128),))
    dec_bias = centred(key_of[15], (DEC,), 0.5, 3.0, ((0, 128),))
    mask_token = centred(key_of[16], (DEC,), 1.0, 4.0, ((0, 128),))
    grid_cotangent = centred(key_of[17], (CHIPS, GRID, DEC), 1.0, 6.0, ((0, 8), (1, 16)))
    return dict(tokens=tokens, chip_lengths=chip_lengths, chip_ids=chip_ids, positions=positions, ln1_gain=ln1_gain, ln1_bias=ln1_bias, qkv_weight=qkv_weight, out_weight=out_weight, ln2_gain=ln2_gain, ln2_bias=ln2_bias, fc1_weight=fc1_weight, fc1_bias=fc1_bias, fc2_weight=fc2_weight, fc2_bias=fc2_bias, dec_weight=dec_weight, dec_bias=dec_bias, mask_token=mask_token, grid_cotangent=grid_cotangent)


@jax.custom_vjp
def low(v):
    return lax.optimization_barrier(v.astype(jnp.bfloat16)).astype(jnp.float32)

@jax.custom_vjp
def low_back(v):
    return v

def low_keep(v):
    return (low(v), None)

def low_pass(kept, grad):
    return (grad,)

def back_keep(v):
    return (v, None)

def back_low(kept, grad):
    return (low(grad),)
low.defvjp(low_keep, low_pass)
low_back.defvjp(back_keep, back_low)
NORM_EPS = 1e-06
precise = lax.Precision.HIGHEST

def matmul_hi(left, right):
    return jnp.dot(left, right, precision=precise, preferred_element_type=jnp.float32)

def normalize(values):
    center = values - lax.optimization_barrier(jnp.mean(values, axis=-1, keepdims=True))
    spread = lax.optimization_barrier(jnp.mean(center * center, axis=-1, keepdims=True))
    return center * lax.rsqrt(spread + NORM_EPS)

def pack_layout(lengths, cells_of_rows):
    ends = jnp.cumsum(lengths + 2)
    row_index = jnp.arange(PACK, dtype=jnp.int32)
    segment = lax.optimization_barrier(jnp.sum((row_index[:, None] >= ends[None, :]).astype(jnp.int32), axis=1))
    target = jnp.where(cells_of_rows >= 0, segment * GRID + cells_of_rows, -1)
    cell_index = jnp.arange(SLOTS_DEV * GRID, dtype=jnp.int32)
    fill_table = (cell_index[:, None] == target[None, :]).astype(jnp.float32)
    covered = lax.optimization_barrier(jnp.sum(fill_table, axis=1))
    limits = jnp.repeat(4 * lengths, GRID)
    valid = cell_index % GRID < limits
    empty_cells = jnp.where(valid, 1.0 - covered, 0.0).astype(jnp.float32)
    return (segment, fill_table, empty_cells)

def layer_forward(params, inputs, segment, fill_table, empty_cells):
    ln1_gain, ln1_bias, qkv_weight, out_weight, ln2_gain, ln2_bias, fc1_weight, fc1_bias, fc2_weight, fc2_bias, dec_weight, dec_bias, mask_token = params
    token_count = inputs.shape[0]
    normed = low(normalize(inputs) * ln1_gain + ln1_bias)
    packed_qkv = low(low_back(matmul_hi(normed, qkv_weight)))
    queries = packed_qkv[:, :D].reshape(token_count, HEADS, HEAD_DIM)
    key_heads = packed_qkv[:, D:2 * D].reshape(token_count, HEADS, HEAD_DIM)
    value_heads = packed_qkv[:, 2 * D:].reshape(token_count, HEADS, HEAD_DIM)
    scores = jnp.einsum('qhd,khd->hqk', queries, key_heads, precision=precise) * HEAD_DIM ** (-0.5)
    scores = low_back(scores)
    same_chip = segment[:, None] == segment[None, :]
    scores = jnp.where(same_chip[None], scores, -1e+30)
    attn_probs = jax.nn.softmax(scores, axis=-1)
    mixed = jnp.einsum('hqk,khd->qhd', low(attn_probs), value_heads, precision=precise)
    mixed = low(low_back(mixed.reshape(token_count, D)))
    after_attn = inputs + low_back(matmul_hi(mixed, out_weight))
    normed_two = low(normalize(after_attn) * ln2_gain + ln2_bias)
    pre_act = low_back(matmul_hi(normed_two, fc1_weight) + fc1_bias)
    activated = low(jax.nn.gelu(pre_act, approximate=False))
    after_mlp = after_attn + low_back(matmul_hi(activated, fc2_weight) + fc2_bias)
    projected = low(matmul_hi(low(after_mlp), dec_weight) + dec_bias)
    grid_vals = matmul_hi(fill_table, projected) + empty_cells[:, None] * mask_token[None, :]
    return grid_vals.reshape(SLOTS_DEV, GRID, DEC)

def reference(tokens, chip_lengths, chip_ids, positions, ln1_gain, ln1_bias, qkv_weight, out_weight, ln2_gain, ln2_bias, fc1_weight, fc1_bias, fc2_weight, fc2_bias, dec_weight, dec_bias, mask_token, grid_cotangent):
    device_count = TOKENS // PACK
    lengths = chip_lengths.reshape(device_count, SLOTS_DEV)
    cell_rows = positions.reshape(device_count, PACK)
    params = (ln1_gain.astype(jnp.float32), ln1_bias.astype(jnp.float32), qkv_weight.astype(jnp.float32), out_weight.astype(jnp.float32), ln2_gain.astype(jnp.float32), ln2_bias.astype(jnp.float32), fc1_weight.astype(jnp.float32), fc1_bias.astype(jnp.float32), fc2_weight.astype(jnp.float32), fc2_bias.astype(jnp.float32), dec_weight.astype(jnp.float32), dec_bias.astype(jnp.float32), mask_token.astype(jnp.float32))
    inputs = tokens.astype(jnp.float32).reshape(device_count, PACK, D)
    slot_index = jnp.arange(CHIPS, dtype=jnp.int32)
    global_ids = slot_index // GROUP_CHIPS * GROUP_CHIPS + chip_ids
    inverse = jnp.argsort(global_ids)

    def forward(weights, packs):

        def per_pack(items):
            pack_rows, pack_lengths, pack_cells = items
            segment, fill_table, empty_cells = pack_layout(pack_lengths, pack_cells)
            return layer_forward(weights, pack_rows, segment, fill_table, empty_cells)
        grids = lax.map(jax.checkpoint(per_pack), (packs, lengths, cell_rows))
        return grids.reshape(CHIPS, GRID, DEC)[inverse]
    result, pull = jax.vjp(forward, params, inputs)
    grads, input_grad = pull(grid_cotangent.astype(jnp.float32))
    return (result.astype(jnp.bfloat16), input_grad.reshape(TOKENS, D), grads[0], grads[1], grads[2], grads[3], grads[4], grads[5], grads[6], grads[7], grads[8], grads[9], grads[10], grads[11], grads[12])
```

```python
import functools
import numpy as np
import jax, jax.numpy as jnp
from jax import lax
from jax.experimental import pallas as pl
from jax.experimental.pallas import tpu as pltpu
from jax.sharding import PartitionSpec as P

from functools import partial

ROWS = 336
D = 768
HEADS = 12
HEAD_DIM = 64
DEC = 512
GRID = 1024


NORM_EPS = 1e-06


def normalize(values):
    center = values - jnp.mean(values, axis=-1, keepdims=True)
    spread = jnp.mean(center * center, axis=-1, keepdims=True)
    return center * lax.rsqrt(spread + NORM_EPS)


def ln_affine(values, gain, bias):
    return normalize(values) * gain + bias


def left_product(left, right):
    return lax.dot_general(
        left, right, (((0,), (0,)), ((), ())), preferred_element_type=jnp.float32
    )


def right_product(left, right):
    return lax.dot_general(
        left, right, (((1,), (1,)), ((), ())), preferred_element_type=jnp.float32
    )


def pack_layout(chip_lengths, positions):
    row_count = positions.shape[0]
    slot_count = chip_lengths.shape[0]
    first = chip_lengths[0] + 2
    ends = jnp.stack([first, first + chip_lengths[1] + 2])
    row_index = jnp.arange(row_count, dtype=jnp.int32)
    segment = jnp.sum((row_index[:, None] >= ends[None, :]).astype(jnp.int32), axis=1)
    target = jnp.where(positions >= 0, segment * GRID + positions, -1)
    cell_index = jnp.arange(slot_count * GRID, dtype=jnp.int32)
    hits = cell_index[:, None] == target[None, :]
    fill_table = hits.astype(jnp.bfloat16)
    covered = jnp.any(hits, axis=1)
    valid = cell_index % GRID < jnp.repeat(4 * chip_lengths, GRID)
    empty_cells = (valid & jnp.logical_not(covered)).astype(jnp.bfloat16)
    return (segment, fill_table, empty_cells)


def layer_forward(weights, tokens, segment):
    gain_one = weights[0].astype(jnp.float32)
    bias_one = weights[1].astype(jnp.float32)
    gain_two = weights[4].astype(jnp.float32)
    bias_two = weights[5].astype(jnp.float32)
    inputs = tokens.astype(jnp.float32)
    token_count = tokens.shape[0]
    normed = ln_affine(inputs, gain_one, bias_one).astype(jnp.bfloat16)
    packed_qkv = jnp.dot(normed, weights[2], preferred_element_type=jnp.float32).astype(
        jnp.bfloat16
    )
    queries = packed_qkv[:, :D].reshape(token_count, HEADS, HEAD_DIM)
    key_heads = packed_qkv[:, D : 2 * D].reshape(token_count, HEADS, HEAD_DIM)
    value_heads = packed_qkv[:, 2 * D :].reshape(token_count, HEADS, HEAD_DIM)
    scores = jnp.einsum(
        "qhd,khd->hqk", queries, key_heads, preferred_element_type=jnp.float32
    ) * HEAD_DIM ** (-0.5)
    same_chip = segment[:, None] == segment[None, :]
    scores = jnp.where(same_chip[None], scores, -1e30)
    peak = jnp.max(scores, axis=-1, keepdims=True)
    raised = jnp.exp(scores - peak)
    attn_probs = raised / jnp.sum(raised, axis=-1, keepdims=True)
    probs_low = attn_probs.astype(jnp.bfloat16)
    mixed = jnp.einsum("hqk,khd->qhd", probs_low, value_heads, preferred_element_type=jnp.float32)
    mixed = mixed.reshape(token_count, D).astype(jnp.bfloat16)
    after_attn = inputs + jnp.dot(mixed, weights[3], preferred_element_type=jnp.float32)
    normed_two = ln_affine(after_attn, gain_two, bias_two).astype(jnp.bfloat16)
    pre_act = jnp.dot(normed_two, weights[6], preferred_element_type=jnp.float32) + weights[
        7
    ].astype(jnp.float32)
    activated = jax.nn.gelu(pre_act, approximate=False).astype(jnp.bfloat16)
    after_mlp = (
        after_attn
        + jnp.dot(activated, weights[8], preferred_element_type=jnp.float32)
        + weights[9].astype(jnp.float32)
    )
    return (
        inputs,
        normed,
        queries,
        key_heads,
        value_heads,
        attn_probs,
        probs_low,
        mixed,
        after_attn,
        normed_two,
        pre_act,
        activated,
        after_mlp,
    )


MESH = pl.DeviceIdType.MESH
LW = 384
SROWS = 80

def coords():
    dp = lax.axis_index("dp"); fs = lax.axis_index("fsdp")
    z = dp // 2
    x = (dp % 2) * 2 + fs // 8
    y = (fs % 8) // 2
    c = fs % 2
    return z, x, y, c

def dev(z, x, y, c):
    return (z * 2 + x // 2, (x % 2) * 8 + y * 2 + c)

def perm_matrix():
    m = np.zeros((624, 640), np.float32)
    for d in range(8):
        for u in range(8):
            for j in range(6):
                m[48 * u + 6 * d + j, d * 80 + 6 * u + j] = 1
        for j in range(6):
            m[48 * 8 + 6 * d + j, d * 80 + 72 + j] = 1
        for i in range(24):
            m[432 + 24 * d + i, d * 80 + 48 + i] = 1
    return m

ALL = slice(None)

def ag_chunks():
    return [
        [("g", "zx", (0, 2), (0, 1), (1, 2)), ("g", "xz", (2, 4), (2, 3), (3, 4))],
        [("g", "zx", (4, 6), (4, 5), (5, 6)), ("g", "xz", (6, 8), (6, 7), (7, 8))],
        [("g2", "zx", (0, 96), (0, 48), (48, 96)), ("g2", "xz", (96, 192), (96, 144), (144, 192))],
        [("g", "zx", (8, 9), (8, 9), None)],
    ]

def ag_kernel(s_ref, p_ref, g_ref, g2_ref, s1, ss1, rs1, loc, ssem, rsem):
    z, x, y, c = coords()
    zp, zm, zo = (z + 1) % 4, (z + 3) % 4, (z + 2) % 4
    xp, xm, xo = (x + 1) % 4, (x + 3) % 4, (x + 2) % 4
    o = 1 - c
    bar = pltpu.get_barrier_semaphore()
    targets = [dev(zp, x, y, c), dev(zm, x, y, c), dev(z, xp, y, c), dev(z, xm, y, c)]
    group = []
    for dy in range(4):
        for dc in range(2):
            if dy or dc:
                group.append((dy, dc, dev(z, x, (y + dy) % 4, (c + dc) % 2)))
    for t in targets + [g[2] for g in group]:
        pl.semaphore_signal(bar, inc=1, device_id=t, device_id_type=MESH)
    pl.semaphore_wait(bar, len(targets) + len(group))

    me = 2 * y + c
    own = pltpu.make_async_copy(s_ref.at[c], s1.at[me], loc)
    own.start()
    firsts = []
    for i, (dy, dc, t) in enumerate(group):
        cp = pltpu.make_async_remote_copy(s_ref.at[(c + dc) % 2], s1.at[me], ss1.at[i], rs1.at[i], device_id=t, device_id_type=MESH)
        cp.start()
        src = 2 * ((y + 4 - dy) % 4) + (c + dc) % 2
        rc = pltpu.make_async_remote_copy(s_ref.at[c], s1.at[src], ss1.at[i], rs1.at[i], device_id=t, device_id_type=MESH)
        firsts.append((cp, rc))
    own.wait()
    for cp, rc in firsts:
        rc.wait_recv()

    flat = s1[...].reshape(640, LW)
    def relay(lo, hi):
        r = jnp.dot(p_ref[lo:hi, :], flat, preferred_element_type=jnp.float32)
        return r.astype(jnp.bfloat16)

    def place(p):
        if p == 0: g_ref[c, 0:4, z, x] = relay(0, 192).reshape(4, 48, LW)
        if p == 1: g_ref[c, 4:8, z, x] = relay(192, 384).reshape(4, 48, LW)
        if p == 2: g2_ref[c, z, x] = relay(432, 624)
        if p == 3: g_ref[c, 8, z, x] = relay(384, 432)

    def view(arr, h, part, zs, xs):
        if arr == "g":
            return g_ref.at[h, part[0]:part[1], zs, xs]
        return g2_ref.at[h, zs, xs, part[0]:part[1]]

    sends = []
    def mk(k, i, src, dst, to):
        return pltpu.make_async_remote_copy(src, dst, ssem.at[k, i], rsem.at[k, i], device_id=to, device_id_type=MESH)
    def send(k, i, v, to):
        cp = mk(k, i, v, v, to); cp.start(); sends.append(cp)
    def recv(k, i, v):
        mk(k, i, v, v, dev(z, x, y, o)).wait_recv()

    def steps(k, chunk):
        arr, order, full, fa, fb = chunk
        if order == "zx":
            d1p, d1m, d2p, d2m = targets
            p1, m1, o1, p2, m2, o2, s1_, s2_ = zp, zm, zo, xp, xm, xo, z, x
            V = lambda part, a, b, h=c: view(arr, h, part, a, b)
        else:
            d2p, d2m, d1p, d1m = targets
            p1, m1, o1, p2, m2, o2, s1_, s2_ = xp, xm, xo, zp, zm, zo, x, z
            V = lambda part, a, b, h=c: view(arr, h, part, b, a)
        sib = dev(z, x, y, o)
        def st0():
            send(k, 0, V(full, s1_, s2_), d1p)
            send(k, 1, V(full, s1_, s2_), d1m)
        def st1():
            recv(k, 0, V(full, m1, s2_))
            send(k, 2, V(fa, m1, s2_), d1p)
            recv(k, 1, V(full, p1, s2_))
            if fb is not None: send(k, 3, V(fb, p1, s2_), d1m)
        def st2():
            recv(k, 2, V(fa, o1, s2_))
            if fb is not None: recv(k, 3, V(fb, o1, s2_))
            send(k, 4, V(full, ALL, s2_), d2p)
            send(k, 5, V(full, ALL, s2_), d2m)
            send(k, 8, V(full, ALL, s2_), sib)
        def st3():
            recv(k, 4, V(full, ALL, m2))
            send(k, 6, V(fa, ALL, m2), d2p)
            send(k, 9, V(full, ALL, m2), sib)
            recv(k, 5, V(full, ALL, p2))
            if fb is not None: send(k, 7, V(fb, ALL, p2), d2m)
            send(k, 10, V(full, ALL, p2), sib)
        def st4():
            recv(k, 6, V(fa, ALL, o2))
            if fb is not None: recv(k, 7, V(fb, ALL, o2))
            send(k, 11, V(full, ALL, o2), sib)
        def st5():
            recv(k, 8, V(full, ALL, s2_, o))
            recv(k, 9, V(full, ALL, m2, o))
            recv(k, 10, V(full, ALL, p2, o))
            recv(k, 11, V(full, ALL, o2, o))
        return [st0, st1, st2, st3, st4, st5]

    pieces = []
    k = 0
    for p, cl in enumerate(ag_chunks()):
        lst = []
        for ch in cl:
            lst.append(steps(k, ch)); k += 1
        pieces.append(lst)
    for t in range(len(pieces) + 5):
        for p, lst in enumerate(pieces):
            s = t - p
            if s == 0: place(p)
            if 0 <= s < 6:
                for ch in lst: ch[s]()
    for cp, rc in firsts: cp.wait_send()
    for cp in sends: cp.wait_send()

def ag_call(s, pm):
    nk = sum(len(c) for c in ag_chunks())
    return pl.pallas_call(
        ag_kernel,
        out_shape=(jax.ShapeDtypeStruct((2, 9, 4, 4, 48, LW), jnp.bfloat16), jax.ShapeDtypeStruct((2, 4, 4, 192, LW), jnp.bfloat16)),
        in_specs=[pl.BlockSpec(memory_space=pltpu.VMEM)] * 2,
        out_specs=[pl.BlockSpec(memory_space=pltpu.VMEM)] * 2,
        scratch_shapes=[
            pltpu.VMEM((8, SROWS, LW), jnp.bfloat16),
            pltpu.SemaphoreType.DMA((7,)), pltpu.SemaphoreType.DMA((7,)), pltpu.SemaphoreType.DMA(()),
            pltpu.SemaphoreType.DMA((nk, 12)), pltpu.SemaphoreType.DMA((nk, 12)),
        ],
        compiler_params=pltpu.CompilerParams(collective_id=0, has_side_effects=True, vmem_limit_bytes=58 * 2**20),
        cost_estimate=pl.CostEstimate(flops=10**9, bytes_accessed=3 * 10**7, transcendentals=0),
        name="gather_weights",
    )(s, pm)

def half_split(w, h):
    n = w.shape[1] // 2
    return w[:, h * n:(h + 1) * n]

def pack_half(h, qkv, out, fc1, fc2, dec, vec):
    def units(w):
        n = w.shape[1] // LW
        return w.reshape(6, n, LW).transpose(1, 0, 2).reshape(6 * n, LW)
    rows = [units(half_split(qkv, h)), units(half_split(out, h)), units(half_split(fc1, h)), half_split(fc2, h),
            jnp.concatenate([half_split(dec, h), vec[h]], axis=1), jnp.zeros((2, LW), jnp.bfloat16)]
    return jnp.concatenate(rows, axis=0)

def pack_vec(ln1_g, ln1_b, ln2_g, ln2_b, fc2_b, fc1_b, dec_b, mask):
    cols = [ln1_g[:, None], ln1_b[:, None], ln2_g[:, None], ln2_b[:, None], fc2_b[:, None], fc1_b.reshape(6, 4),
            jnp.pad(dec_b, (0, 2))[:, None], jnp.pad(mask, (0, 2))[:, None]]
    v = jnp.concatenate(cols, axis=1)
    return jnp.pad(v, ((0, 0), (0, 128 - v.shape[1])))

def unpack_weights(g, g2):
    def w(u0, u1):
        a = g[:, u0:u1].reshape(2, u1 - u0, 768, LW)
        return a.transpose(2, 0, 1, 3).reshape(768, 2 * (u1 - u0) * LW)
    qkv, out, fc1 = w(0, 3), w(3, 4), w(4, 8)
    fc2 = g2.reshape(2, 3072, LW).transpose(1, 0, 2).reshape(3072, 768)
    dv = g[:, 8].reshape(2, 768, LW)
    dec = dv[:, :, :256].transpose(1, 0, 2).reshape(768, 512)
    v = dv[0, :, 256:]
    vecs = (v[:, 0], v[:, 1], v[:, 2], v[:, 3], v[:, 4], v[:, 5:9].reshape(3072),
            v[:, 9].reshape(128, 6)[:, :4].reshape(512), v[:, 10].reshape(128, 6)[:, :4].reshape(512))
    return qkv, out, fc1, fc2, dec, vecs


def rs_kernel(g_ref, g2_ref, pt_ref, o_ref, sg, sg2, acc, acc2, xa, xa2, xb, xb2, fs, f1, ssem, rsem, ss1, rs1, loc):
    z, x, y, c = coords()
    zp, zm, zo = (z + 1) % 4, (z + 3) % 4, (z + 2) % 4
    xp, xm, xo = (x + 1) % 4, (x + 3) % 4, (x + 2) % 4
    o = 1 - c
    bar = pltpu.get_barrier_semaphore()
    targets = [dev(zp, x, y, c), dev(zm, x, y, c), dev(z, xp, y, c), dev(z, xm, y, c)]
    sib = dev(z, x, y, o)
    group = []
    for dy in range(4):
        for dc in range(2):
            if dy or dc:
                group.append((dy, dc, dev(z, x, (y + dy) % 4, (c + dc) % 2)))
    for t in targets + [g[2] for g in group]:
        pl.semaphore_signal(bar, inc=1, device_id=t, device_id_type=MESH)
    pl.semaphore_wait(bar, len(targets) + len(group))

    sends = []
    def send(k, i, src, dst, to):
        cp = pltpu.make_async_remote_copy(src, dst, ssem.at[k, i], rsem.at[k, i], device_id=to, device_id_type=MESH)
        cp.start(); sends.append(cp)
    def recv(k, i, v):
        pltpu.make_async_remote_copy(v, v, ssem.at[k, i], rsem.at[k, i], device_id=sib, device_id_type=MESH).wait_recv()
    f32, bf = jnp.float32, jnp.bfloat16

    def steps(k, chunk):
        arr, order, full, fa, fb = chunk
        zx = order == "zx"
        if zx:
            d1p, d1m, d2p, d2m = targets
            p1, m1, o1, p2, m2, o2, s1_, s2_ = zp, zm, zo, xp, xm, xo, z, x
        else:
            d2p, d2m, d1p, d1m = targets
            p1, m1, o1, p2, m2, o2, s1_, s2_ = xp, xm, xo, zp, zm, zo, x, z
        def idx(part, a, b):
            zs, xs = (a, b) if zx else (b, a)
            r = pl.ds(part[0], part[1] - part[0])
            return (r, zs, xs) if arr == "g" else (zs, xs, r)
        A = acc if arr == "g" else acc2
        def inp(h, part, a, b):
            src = g_ref if arr == "g" else g2_ref
            return src.at[(h,) + idx(part, a, b)]
        SG = sg if arr == "g" else sg2
        def xav(way, part):
            r = slice(part[0], part[1])
            return xa.at[way, r] if arr == "g" else xa2.at[way, :, r]
        def xbv(way, part):
            r = slice(part[0], part[1])
            return xb.at[way, r] if arr == "g" else xb2.at[way, r]
        def add(part, a, b, recvd):
            i = idx(part, a, b)
            A[i] = (A[i].astype(f32) + recvd[...].astype(f32)).astype(bf)
        def st0():
            send(k, 8, inp(o, full, ALL, ALL), SG.at[idx(full, ALL, ALL)], sib)
        def st1():
            recv(k, 8, SG.at[idx(full, ALL, ALL)])
            def one(j, _):
                i = idx(full, j, ALL)
                A[i] = (inp(c, full, j, ALL)[...].astype(f32) + SG[i].astype(f32)).astype(bf)
                return 0
            lax.fori_loop(0, 4, one, 0)
            send(k, 0, A.at[idx(fa, ALL, o2)], xav(0, fa), d2p)
            if fb is not None: send(k, 1, A.at[idx(fb, ALL, o2)], xav(0, fb), d2m)
        def st2():
            recv(k, 0, xav(0, fa)); add(fa, ALL, p2, xav(0, fa))
            send(k, 2, A.at[idx(full, ALL, p2)], xav(1, full), d2p)
            if fb is not None:
                recv(k, 1, xav(0, fb)); add(fb, ALL, m2, xav(0, fb))
            send(k, 3, A.at[idx(full, ALL, m2)], xav(2, full), d2m)
        def st3():
            recv(k, 2, xav(1, full)); recv(k, 3, xav(2, full))
            i = idx(full, ALL, s2_)
            A[i] = (A[i].astype(f32) + xav(1, full)[...].astype(f32) + xav(2, full)[...].astype(f32)).astype(bf)
            send(k, 4, A.at[idx(fa, o1, s2_)], xbv(0, fa), d1p)
            if fb is not None: send(k, 5, A.at[idx(fb, o1, s2_)], xbv(0, fb), d1m)
        def st4():
            recv(k, 4, xbv(0, fa)); add(fa, p1, s2_, xbv(0, fa))
            send(k, 6, A.at[idx(full, p1, s2_)], xbv(1, full), d1p)
            if fb is not None:
                recv(k, 5, xbv(0, fb)); add(fb, m1, s2_, xbv(0, fb))
            send(k, 7, A.at[idx(full, m1, s2_)], xbv(2, full), d1m)
        def st5():
            recv(k, 6, xbv(1, full)); recv(k, 7, xbv(2, full))
            i = idx(full, s1_, s2_)
            A[i] = (A[i].astype(f32) + xbv(1, full)[...].astype(f32) + xbv(2, full)[...].astype(f32)).astype(bf)
        return [st0, st1, st2, st3, st4, st5]

    pieces = []
    k = 0
    for cl in ag_chunks():
        lst = []
        for ch in cl:
            lst.append(steps(k, ch)); k += 1
        pieces.append(lst)
    pieces = pieces[::-1]
    for t in range(len(pieces) + 5):
        for p, lst in enumerate(pieces):
            s = t - p
            if 0 <= s < 6:
                for ch in lst: ch[s]()
    blk = jnp.concatenate([acc[:, z, x].reshape(432, LW), acc2[z, x]], axis=0)
    r = jnp.dot(pt_ref[...], blk, preferred_element_type=f32).astype(bf)
    fs[...] = r.reshape(8, SROWS, LW)
    me = 2 * y + c
    own = pltpu.make_async_copy(fs.at[me], f1.at[me], loc)
    own.start()
    lasts = []
    for i, (dy, dc, t) in enumerate(group):
        dst = 2 * ((y + dy) % 4) + (c + dc) % 2
        cp = pltpu.make_async_remote_copy(fs.at[dst], f1.at[me], ss1.at[i], rs1.at[i], device_id=t, device_id_type=MESH)
        cp.start()
        src = 2 * ((y + 4 - dy) % 4) + (c + dc) % 2
        rc = pltpu.make_async_remote_copy(fs.at[me], f1.at[src], ss1.at[i], rs1.at[i], device_id=t, device_id_type=MESH)
        lasts.append((cp, rc))
    own.wait()
    for cp, rc in lasts: rc.wait_recv()
    for h in range(2):
        t = f1[h].astype(f32)
        for yy in range(1, 4): t = t + f1[2 * yy + h].astype(f32)
        o_ref[h] = t
    for cp, rc in lasts: cp.wait_send()
    for cp in sends: cp.wait_send()

def rs_call(g, g2, pt):
    nk = sum(len(c) for c in ag_chunks())
    V, bf = pltpu.VMEM, jnp.bfloat16
    return pl.pallas_call(
        rs_kernel,
        out_shape=jax.ShapeDtypeStruct((2, SROWS, LW), jnp.float32),
        in_specs=[pl.BlockSpec(memory_space=pltpu.VMEM)] * 3,
        out_specs=pl.BlockSpec(memory_space=pltpu.VMEM),
        scratch_shapes=[
            V((9, 4, 4, 48, LW), bf), V((4, 4, 192, LW), bf),
            V((9, 4, 4, 48, LW), bf), V((4, 4, 192, LW), bf),
            V((3, 9, 4, 48, LW), bf), V((3, 4, 192, LW), bf),
            V((3, 9, 48, LW), bf), V((3, 192, LW), bf),
            V((8, SROWS, LW), bf), V((8, SROWS, LW), bf),
            pltpu.SemaphoreType.DMA((nk, 9)), pltpu.SemaphoreType.DMA((nk, 9)),
            pltpu.SemaphoreType.DMA((7,)), pltpu.SemaphoreType.DMA((7,)), pltpu.SemaphoreType.DMA(()),
        ],
        compiler_params=pltpu.CompilerParams(collective_id=1, has_side_effects=True, vmem_limit_bytes=60 * 2**20),
        cost_estimate=pl.CostEstimate(flops=10**9, bytes_accessed=3 * 10**7, transcendentals=0),
        name="scatter_grads",
    )(g, g2, pt)

def pack_grads(qkv, out, fc1, fc2, dec, vec):
    bf = jnp.bfloat16
    def u(w):
        w = w.astype(bf)
        n = w.shape[1] // LW // 2
        return w.reshape(768, 2, n, LW).transpose(1, 2, 0, 3)
    d = dec.astype(bf).reshape(768, 2, 256).transpose(1, 0, 2)
    v = jnp.stack([vec.astype(bf), jnp.zeros_like(vec, bf)])
    dv = jnp.concatenate([d, v], axis=2)[:, None]
    g = jnp.concatenate([u(qkv), u(out), u(fc1), dv], axis=1).reshape(2, 9, 4, 4, 48, LW)
    g2 = fc2.astype(bf).reshape(3072, 2, LW).transpose(1, 0, 2).reshape(2, 4, 4, 192, LW)
    return g, g2

def pack_vec_full(ln1_g, ln1_b, ln2_g, ln2_b, fc2_b, fc1_b, dec_b, mask):
    p4 = lambda v: jnp.pad(v.reshape(128, 4), ((0, 0), (0, 2))).reshape(768, 1)
    cols = [ln1_g[:, None], ln1_b[:, None], ln2_g[:, None], ln2_b[:, None], fc2_b[:, None], fc1_b.reshape(768, 4), p4(dec_b), p4(mask)]
    v = jnp.concatenate(cols, axis=1)
    return jnp.pad(v, ((0, 0), (0, 128 - v.shape[1])))

def unpack_grads(r):
    def u(a, n):
        return a.reshape(2, n, 6, LW).transpose(2, 0, 1, 3).reshape(6, 2 * n * LW)
    qkv, out, fc1 = u(r[:, 0:18], 3), u(r[:, 18:24], 1), u(r[:, 24:48], 4)
    fc2 = r[:, 48:72].transpose(1, 0, 2).reshape(24, 768)
    dec = r[:, 72:78, :256].transpose(1, 0, 2).reshape(6, 512)
    v = r[0, 72:78, 256:]
    return qkv, out, fc1, fc2, dec, (v[:, 0], v[:, 1], v[:, 2], v[:, 3], v[:, 4], v[:, 5:9].reshape(24), v[:4, 9], v[:4, 10])


def body(
    tokens,
    chip_lengths,
    chip_ids,
    positions,
    ln1_gain,
    ln1_bias,
    qkv_weight,
    out_weight,
    ln2_gain,
    ln2_bias,
    fc1_weight,
    fc1_bias,
    fc2_weight,
    fc2_bias,
    dec_weight,
    dec_bias,
    mask_token,
    grid_cotangent,
):
    all_tokens = tokens
    tokens = tokens[:ROWS]
    positions = positions[:ROWS]
    vec = pack_vec(ln1_gain, ln1_bias, ln2_gain, ln2_bias, fc2_bias, fc1_bias, dec_bias, mask_token)
    packed = jnp.stack(
        [pack_half(h, qkv_weight, out_weight, fc1_weight, fc2_weight, dec_weight, [vec, jnp.zeros_like(vec)]) for h in range(2)]
    )
    perm = jnp.asarray(perm_matrix(), jnp.bfloat16)
    w_qkv, w_out, w_fc1, w_fc2, w_dec, vecs = unpack_weights(*ag_call(packed, perm))
    gathered = (
        vecs[0], vecs[1], w_qkv, w_out, vecs[2], vecs[3], w_fc1, vecs[5], w_fc2, vecs[4], w_dec, vecs[6], vecs[7],
    )
    segment, fill_table, empty_cells = pack_layout(chip_lengths, positions)
    forward_saved = layer_forward(gathered, tokens, segment)
    dec_input = forward_saved[12].astype(jnp.bfloat16)
    projected = (
        jnp.dot(dec_input, gathered[10], preferred_element_type=jnp.float32)
        + gathered[11].astype(jnp.float32)
    ).astype(jnp.bfloat16)
    cell_values = jnp.dot(fill_table, projected, preferred_element_type=jnp.float32)
    cell_values = (
        cell_values
        + empty_cells.astype(jnp.float32)[:, None] * gathered[12].astype(jnp.float32)[None, :]
    )
    slot_count = chip_lengths.shape[0]
    cell_values = cell_values.astype(jnp.bfloat16).reshape(slot_count, GRID, DEC)
    fsdp_size = lax.axis_size("fsdp")
    chip_tags = jnp.broadcast_to(chip_ids.astype(jnp.bfloat16)[:, None], (slot_count, fsdp_size))
    arrived, arrived_tags = (
        lax.all_to_all(cell_values, "fsdp", split_axis=1, concat_axis=0, tiled=True),
        lax.all_to_all(chip_tags, "fsdp", split_axis=1, concat_axis=0, tiled=True),
    )
    group_size = arrived.shape[0]
    owner_rows = arrived_tags[:, 0].astype(jnp.int32)
    placement = (jnp.arange(group_size, dtype=jnp.int32)[:, None] == owner_rows[None, :]).astype(
        jnp.bfloat16
    )
    full_grid = jnp.dot(
        placement, arrived.reshape(group_size, -1), preferred_element_type=jnp.float32
    )
    full_grid = full_grid.astype(jnp.bfloat16).reshape(arrived.shape)
    returned = left_product(placement, grid_cotangent.reshape(group_size, -1))
    returned = returned.astype(jnp.bfloat16).reshape(grid_cotangent.shape)
    grid_grad = lax.all_to_all(returned, "fsdp", split_axis=0, concat_axis=1, tiled=True)
    weights = gathered
    (
        inputs,
        normed,
        queries,
        key_heads,
        value_heads,
        attn_probs,
        probs_low,
        mixed,
        after_attn,
        normed_two,
        pre_act,
        activated,
        after_mlp,
    ) = forward_saved
    token_count = tokens.shape[0]
    gain_one = weights[0].astype(jnp.float32)
    bias_one = weights[1].astype(jnp.float32)
    gain_two = weights[4].astype(jnp.float32)
    bias_two = weights[5].astype(jnp.float32)
    flat_grad = grid_grad.reshape(slot_count * GRID, DEC)
    proj_grad = left_product(fill_table, flat_grad).astype(jnp.bfloat16)
    mask_grad = jnp.dot(empty_cells, flat_grad, preferred_element_type=jnp.float32)
    dec_w_grad = left_product(after_mlp.astype(jnp.bfloat16), proj_grad)
    dec_b_grad = jnp.sum(proj_grad.astype(jnp.float32), axis=0)
    mlp_grad = right_product(proj_grad, weights[10])
    fc2_input = mlp_grad.astype(jnp.bfloat16)
    fc2_w_grad = left_product(activated, fc2_input)
    fc2_b_grad = jnp.sum(fc2_input.astype(jnp.float32), axis=0)
    act_grad = right_product(fc2_input, weights[8])
    unused_value, gelu_pull = jax.vjp(partial(jax.nn.gelu, approximate=False), pre_act)
    pre_grad = gelu_pull(act_grad)[0].astype(jnp.bfloat16)
    fc1_w_grad = left_product(normed_two, pre_grad)
    fc1_b_grad = jnp.sum(pre_grad.astype(jnp.float32), axis=0)
    norm_two_grad = right_product(pre_grad, weights[6])
    unused_two, norm_two_pull = jax.vjp(ln_affine, after_attn, gain_two, bias_two)
    attn_res_grad, ln2_g_grad, ln2_b_grad = norm_two_pull(norm_two_grad)
    resid_grad = mlp_grad + attn_res_grad
    out_input = resid_grad.astype(jnp.bfloat16)
    out_w_grad = left_product(mixed, out_input)
    mixed_grad = (
        right_product(out_input, weights[3])
        .astype(jnp.bfloat16)
        .reshape(token_count, HEADS, HEAD_DIM)
    )
    prob_grad = jnp.einsum(
        "qhd,khd->hqk", mixed_grad, value_heads, preferred_element_type=jnp.float32
    )
    value_grad = jnp.einsum(
        "hqk,qhd->khd", probs_low, mixed_grad, preferred_element_type=jnp.float32
    )
    inner_sum = jnp.sum(prob_grad * attn_probs, axis=-1, keepdims=True)
    score_grad = (attn_probs * (prob_grad - inner_sum)).astype(jnp.bfloat16)
    scale_factor = HEAD_DIM ** (-0.5)
    query_grad = scale_factor * jnp.einsum(
        "hqk,khd->qhd", score_grad, key_heads, preferred_element_type=jnp.float32
    )
    key_grad = scale_factor * jnp.einsum(
        "hqk,qhd->khd", score_grad, queries, preferred_element_type=jnp.float32
    )
    qkv_grad = jnp.concatenate(
        [
            query_grad.reshape(token_count, D),
            key_grad.reshape(token_count, D),
            value_grad.reshape(token_count, D),
        ],
        axis=1,
    ).astype(jnp.bfloat16)
    qkv_w_grad = left_product(normed, qkv_grad)
    normed_grad = right_product(qkv_grad, weights[2])
    unused_one, norm_one_pull = jax.vjp(ln_affine, inputs, gain_one, bias_one)
    input_part, ln1_g_grad, ln1_b_grad = norm_one_pull(normed_grad)
    tokens_grad = resid_grad + input_part
    tokens_grad = jnp.pad(tokens_grad, ((0, all_tokens.shape[0] - ROWS), (0, 0)))
    vec_grad = pack_vec_full(ln1_g_grad, ln1_b_grad, ln2_g_grad, ln2_b_grad, fc2_b_grad, fc1_b_grad, dec_b_grad, mask_grad)
    g, g2 = pack_grads(qkv_w_grad, out_w_grad, fc1_w_grad, fc2_w_grad, dec_w_grad, vec_grad)
    s_qkv, s_out, s_fc1, s_fc2, s_dec, s_vec = unpack_grads(rs_call(g, g2, perm.T))
    return (
        full_grid,
        tokens_grad,
        s_vec[0],
        s_vec[1],
        s_qkv,
        s_out,
        s_vec[2],
        s_vec[3],
        s_fc1,
        s_vec[5],
        s_fc2,
        s_vec[4],
        s_dec,
        s_vec[6],
        s_vec[7],
    )


def solution(mesh):
    placed = (
        P(("dp", "fsdp"), None),
        P(("dp", "fsdp")),
        P(("dp", "fsdp")),
        P(("dp", "fsdp")),
        P(("dp", "fsdp")),
        P(("dp", "fsdp")),
        P(("dp", "fsdp"), None),
        P(("dp", "fsdp"), None),
        P(("dp", "fsdp")),
        P(("dp", "fsdp")),
        P(("dp", "fsdp"), None),
        P(("dp", "fsdp")),
        P(("dp", "fsdp"), None),
        P(("dp", "fsdp")),
        P(("dp", "fsdp"), None),
        P(("dp", "fsdp")),
        P(("dp", "fsdp")),
        P("dp", "fsdp", None),
    )
    return jax.shard_map(
        body,
        mesh=mesh,
        in_specs=placed,
        out_specs=(
            P("dp", "fsdp", None),
            P(("dp", "fsdp"), None),
            P(("dp", "fsdp")),
            P(("dp", "fsdp")),
            P(("dp", "fsdp"), None),
            P(("dp", "fsdp"), None),
            P(("dp", "fsdp")),
            P(("dp", "fsdp")),
            P(("dp", "fsdp"), None),
            P(("dp", "fsdp")),
            P(("dp", "fsdp"), None),
            P(("dp", "fsdp")),
            P(("dp", "fsdp"), None),
            P(("dp", "fsdp")),
            P(("dp", "fsdp")),
        ),
        check_vma=False,
    )
```

```python
import functools
import numpy as np
import jax, jax.numpy as jnp
from jax import lax
from jax.experimental import pallas as pl
from jax.experimental.pallas import tpu as pltpu
from jax.sharding import PartitionSpec as P

MESH = pl.DeviceIdType.MESH
LW = 384
SROWS = 80

def coords():
    dp = lax.axis_index("dp"); fs = lax.axis_index("fsdp")
    z = dp // 2
    x = (dp % 2) * 2 + fs // 8
    y = (fs % 8) // 2
    c = fs % 2
    return z, x, y, c

def dev(z, x, y, c):
    return (z * 2 + x // 2, (x % 2) * 8 + y * 2 + c)

def perm_matrix():
    m = np.zeros((624, 640), np.float32)
    for d in range(8):
        for u in range(8):
            for j in range(6):
                m[48 * u + 6 * d + j, d * 80 + 6 * u + j] = 1
        for j in range(6):
            m[48 * 8 + 6 * d + j, d * 80 + 72 + j] = 1
        for i in range(24):
            m[432 + 24 * d + i, d * 80 + 48 + i] = 1
    return m

ALL = slice(None)

def ag_chunks():
    return [
        [("g", "zx", (0, 2), (0, 1), (1, 2)), ("g", "xz", (2, 4), (2, 3), (3, 4))],
        [("g", "zx", (4, 6), (4, 5), (5, 6)), ("g", "xz", (6, 8), (6, 7), (7, 8))],
        [("g2", "zx", (0, 96), (0, 48), (48, 96)), ("g2", "xz", (96, 192), (96, 144), (144, 192))],
        [("g", "zx", (8, 9), (8, 9), None)],
    ]


def pack_vec(ln1_g, ln1_b, ln2_g, ln2_b, fc2_b, fc1_b, dec_b, mask):
    cols = [ln1_g[:, None], ln1_b[:, None], ln2_g[:, None], ln2_b[:, None], fc2_b[:, None], fc1_b.reshape(6, 4),
            jnp.pad(dec_b, (0, 2))[:, None], jnp.pad(mask, (0, 2))[:, None]]
    v = jnp.concatenate(cols, axis=1)
    return jnp.pad(v, ((0, 0), (0, 128 - v.shape[1])))


ROWS = 336
HEADS_PAIRS = 6
D = 768
NT = (((1,), (1,)), ((), ()))
TN = (((0,), (0,)), ((), ()))
f32, bf16 = jnp.float32, jnp.bfloat16


def cell_spread():
    m = np.zeros((768, 512), np.float32)
    for d in range(128):
        for j in range(4):
            m[6 * d + j, 4 * d + j] = 1
    return m


def quad_spread():
    m = np.zeros((192, 768), np.float32)
    m[np.arange(768) // 4, np.arange(768)] = 1
    return m


def stats(v):
    mean = jnp.mean(v, axis=-1, keepdims=True)
    center = v - mean
    rstd = lax.rsqrt(jnp.mean(center * center, axis=-1, keepdims=True) + 1e-6)
    return center * rstd, rstd


def gelu_pair(f):
    cdf = 0.5 * (1.0 + lax.erf(f * 0.7071067811865476))
    pdf = 0.3989422804014327 * jnp.exp(-0.5 * f * f)
    return f * cdf, cdf + f * pdf


def k1_kernel(tok, lens, pos, vec6, qkv_s, out_s, fc1_s, fc2_s, dec_s, p_ref, m2_ref, m4_ref,
              g_hbm, g2_hbm, rows_ref, a_ref, qkv_ref, p_out, o_ref, x2_ref, h2_ref, act_ref, dact_ref, e_ref, cells_ref,
              g_ref, g2_ref, sp, s_ref, s1, z_ref, ss1, rs1, loc, ssem, rsem, wsem):
    z, x, y, c = coords()
    zp, zm, zo = (z + 1) % 4, (z + 3) % 4, (z + 2) % 4
    xp, xm, xo = (x + 1) % 4, (x + 3) % 4, (x + 2) % 4
    o = 1 - c
    bar = pltpu.get_barrier_semaphore()
    targets = [dev(zp, x, y, c), dev(zm, x, y, c), dev(z, xp, y, c), dev(z, xm, y, c)]
    group = []
    for dy in range(4):
        for dc in range(2):
            if dy or dc:
                group.append((dy, dc, dev(z, x, (y + dy) % 4, (c + dc) % 2)))
    for t in targets + [g[2] for g in group]:
        pl.semaphore_signal(bar, inc=1, device_id=t, device_id_type=MESH)

    sp[...] = jnp.zeros_like(sp)
    for h in range(2):
        for u in range(3):
            sp[h, 6 * u:6 * u + 6, :] = qkv_s[:, h * 1152 + u * LW:h * 1152 + (u + 1) * LW].astype(f32)
        sp[h, 18:24, :] = out_s[:, h * LW:(h + 1) * LW].astype(f32)
        for u in range(4):
            sp[h, 24 + 6 * u:30 + 6 * u, :] = fc1_s[:, h * 1536 + u * LW:h * 1536 + (u + 1) * LW].astype(f32)
        sp[h, 48:72, :] = fc2_s[:, h * LW:(h + 1) * LW].astype(f32)
        sp[h, 72:78, 0:256] = dec_s[:, h * 256:(h + 1) * 256].astype(f32)
    sp[0, 72:78, 256:384] = vec6[...].astype(f32)
    s_ref[...] = sp[...].astype(bf16)
    pl.semaphore_wait(bar, len(targets) + len(group))

    me = 2 * y + c
    own = pltpu.make_async_copy(s_ref.at[c], s1.at[me], loc)
    own.start()
    firsts = []
    for i, (dy, dc, t) in enumerate(group):
        cp = pltpu.make_async_remote_copy(s_ref.at[(c + dc) % 2], s1.at[me], ss1.at[i], rs1.at[i], device_id=t, device_id_type=MESH)
        cp.start()
        src = 2 * ((y + 4 - dy) % 4) + (c + dc) % 2
        rc = pltpu.make_async_remote_copy(s_ref.at[c], s1.at[src], ss1.at[i], rs1.at[i], device_id=t, device_id_type=MESH)
        firsts.append((cp, rc))

    own.wait()
    for cp, rc in firsts:
        rc.wait_recv()

    def relay(lo, hi):
        flat = s1[...].reshape(640, LW)
        r = jnp.dot(p_ref[lo:hi, :], flat, preferred_element_type=f32)
        return r.astype(bf16)

    def place(p):
        if p == 0: g_ref[c, 0:4, z, x] = relay(0, 192).reshape(4, 48, LW)
        if p == 1: g_ref[c, 4:8, z, x] = relay(192, 384).reshape(4, 48, LW)
        if p == 2: g2_ref[c, z, x] = relay(432, 624)
        if p == 3: g_ref[c, 8, z, x] = relay(384, 432)

    def view(arr, h, part, zs, xs):
        if arr == "g":
            return g_ref.at[h, part[0]:part[1], zs, xs]
        return g2_ref.at[h, zs, xs, part[0]:part[1]]

    sends = []
    def mk(k, i, src, dst, to):
        return pltpu.make_async_remote_copy(src, dst, ssem.at[k, i], rsem.at[k, i], device_id=to, device_id_type=MESH)
    def send(k, i, v, to):
        cp = mk(k, i, v, v, to); cp.start(); sends.append(cp)
    def recv(k, i, v):
        mk(k, i, v, v, dev(z, x, y, o)).wait_recv()

    def steps(k, chunk):
        arr, order, full, fa, fb = chunk
        if order == "zx":
            d1p, d1m, d2p, d2m = targets
            p1, m1, o1, p2, m2, o2, s1_, s2_ = zp, zm, zo, xp, xm, xo, z, x
            V = lambda part, a, b, h=c: view(arr, h, part, a, b)
        else:
            d2p, d2m, d1p, d1m = targets
            p1, m1, o1, p2, m2, o2, s1_, s2_ = xp, xm, xo, zp, zm, zo, x, z
            V = lambda part, a, b, h=c: view(arr, h, part, b, a)
        sib = dev(z, x, y, o)
        def st0():
            send(k, 0, V(full, s1_, s2_), d1p)
            send(k, 1, V(full, s1_, s2_), d1m)
        def st1():
            recv(k, 0, V(full, m1, s2_))
            send(k, 2, V(fa, m1, s2_), d1p)
            recv(k, 1, V(full, p1, s2_))
            if fb is not None: send(k, 3, V(fb, p1, s2_), d1m)
        def st2():
            recv(k, 2, V(fa, o1, s2_))
            if fb is not None: recv(k, 3, V(fb, o1, s2_))
            send(k, 4, V(full, ALL, s2_), d2p)
            send(k, 5, V(full, ALL, s2_), d2m)
            send(k, 8, V(full, ALL, s2_), sib)
        def st3():
            recv(k, 4, V(full, ALL, m2))
            send(k, 6, V(fa, ALL, m2), d2p)
            send(k, 9, V(full, ALL, m2), sib)
            recv(k, 5, V(full, ALL, p2))
            if fb is not None: send(k, 7, V(fb, ALL, p2), d2m)
            send(k, 10, V(full, ALL, p2), sib)
        def st4():
            recv(k, 6, V(fa, ALL, o2))
            if fb is not None: recv(k, 7, V(fb, ALL, o2))
            send(k, 11, V(full, ALL, o2), sib)
        def st5():
            recv(k, 8, V(full, ALL, s2_, o))
            recv(k, 9, V(full, ALL, m2, o))
            recv(k, 10, V(full, ALL, p2, o))
            recv(k, 11, V(full, ALL, o2, o))
        return [st0, st1, st2, st3, st4, st5]

    outs = []
    def to_hbm(p):
        if p == 2: cp = pltpu.make_async_copy(g2_ref, g2_hbm, wsem.at[p])
        else:
            u0, u1 = ((0, 4), (4, 8), None, (8, 9))[p]
            cp = pltpu.make_async_copy(g_ref.at[:, u0:u1], g_hbm.at[:, u0:u1], wsem.at[p])
        cp.start(); outs.append(cp)

    def blocks(body, n=7):
        def step(i, _):
            body(pl.ds(pl.multiple_of(i * 48, 48), 48)); return 0
        lax.fori_loop(0, n, step, 0)

    def w(h, u):
        return g_ref[h, u].reshape(768, LW)

    def rows_of():
        v = jnp.concatenate([g_ref[0, 8, zz, xx, :, 256:384] for zz in range(4) for xx in range(4)], axis=0)
        vt = v.astype(f32).T
        rows_ref[0:5, 0:768] = vt[0:5]
        md = lax.dot_general(v, m2_ref[...], TN, preferred_element_type=f32)
        rows_ref[6:8, 0:512] = md[9:11]
        lane = lax.broadcasted_iota(jnp.int32, (8, 768), 1) % 4
        row = lax.broadcasted_iota(jnp.int32, (8, 768), 0)
        for s in range(4):
            q = lax.dot_general(v[192 * s:192 * s + 192], m4_ref[...], TN, preferred_element_type=f32)
            q = jnp.where(row == lane, q[5:13], 0.0)
            rows_ref[5:6, 768 * s:768 * s + 768] = jnp.sum(q, axis=0, keepdims=True)

    def ln1():
        def body(r):
            n, _ = stats(tok[r, :].astype(f32))
            a_ref[r, :] = (n * rows_ref[0:1, 0:768] + rows_ref[1:2, 0:768]).astype(bf16)
        blocks(body)

    def qkv():
        for h in range(2):
            wt = jnp.concatenate([w(h, u) for u in range(3)], axis=1)
            qkv_ref[:, h * 1152:(h + 1) * 1152] = jnp.dot(a_ref[...], wt, preferred_element_type=f32).astype(bf16)

    ends0 = lens[0] + 2
    ends1 = ends0 + lens[1] + 2
    def seg(shape, axis):
        r = lax.broadcasted_iota(jnp.int32, shape, axis)
        return (r >= ends0).astype(jnp.int32) + (r >= ends1).astype(jnp.int32)

    def attention():
        low = lax.broadcasted_iota(jnp.int32, (1, 128), 1) < 64
        same = seg((ROWS, 1), 0) == seg((1, ROWS), 1)
        bias = jnp.where(same, 0.0, -1e30)
        def pair(i, _):
            def cols(base):
                return qkv_ref[:, pl.ds(pl.multiple_of(base + i * 128, 128), 128)]
            q, k, v = cols(0), cols(768), cols(1536)
            outs_ = []
            for t in range(2):
                keep = low if t == 0 else jnp.logical_not(low)
                s = lax.dot_general(jnp.where(keep, q, jnp.zeros_like(q)), k, NT, preferred_element_type=f32)
                s = jnp.where(same, s * 0.125, -1e30)
                m = jnp.max(s, axis=-1, keepdims=True)
                ex = jnp.exp(s - m)
                pr = (ex / jnp.sum(ex, axis=-1, keepdims=True)).astype(bf16)
                p_out[2 * i + t] = pr
                outs_.append(jnp.dot(pr, v, preferred_element_type=f32))
            o_ref[:, pl.ds(pl.multiple_of(i * 128, 128), 128)] = jnp.where(low, outs_[0], outs_[1]).astype(bf16)
            return 0
        lax.fori_loop(0, HEADS_PAIRS, pair, 0)

    def out_proj():
        for h in range(2):
            cs = slice(h * LW, (h + 1) * LW)
            x2_ref[:, cs] = tok[0:ROWS, cs].astype(f32) + jnp.dot(o_ref[...], w(h, 3), preferred_element_type=f32)
        def body(r):
            n, _ = stats(x2_ref[r, :])
            h2_ref[r, :] = (n * rows_ref[2:3, 0:768] + rows_ref[3:4, 0:768]).astype(bf16)
        blocks(body)

    def fc1():
        for h in range(2):
            def unit(u, _):
                cs = pl.ds(pl.multiple_of(h * 1536 + u * LW, LW), LW)
                f = jnp.dot(h2_ref[...], w(h, 4 + u), preferred_element_type=f32) + rows_ref[5:6, cs]
                g, dg = gelu_pair(f)
                act_ref[:, cs] = g.astype(bf16)
                dact_ref[:, cs] = dg.astype(bf16)
                return 0
            lax.fori_loop(0, 4, unit, 0)

    def fc2():
        for h in range(2):
            cs = slice(h * LW, (h + 1) * LW)
            t = jnp.dot(act_ref[...], g2_ref[h].reshape(3072, LW), preferred_element_type=f32)
            e_ref[:, cs] = (x2_ref[:, cs] + t + rows_ref[4:5, cs]).astype(bf16)

    def dec():
        for h in range(2):
            cs = slice(h * 256, (h + 1) * 256)
            t = jnp.dot(e_ref[...], g_ref[h, 8, :, :, :, 0:256].reshape(768, 256), preferred_element_type=f32)
            z_ref[:, cs] = (t + rows_ref[6:7, cs]).astype(bf16)
        z_ref[:, 512:640] = jnp.ones((ROWS, 128), bf16)
        p_ = pos[0:1, 0:ROWS]
        target = jnp.where(p_ >= 0, seg((1, ROWS), 1) * 1024 + p_, -1)
        def block(i, _):
            slot = i // 4
            first = i * 256
            cell = first + lax.broadcasted_iota(jnp.int32, (256, 1), 0)
            fill = (cell == target).astype(f32).astype(bf16)
            r = jnp.dot(fill, z_ref[...], preferred_element_type=f32)
            limit = 4 * jnp.where(slot == 0, lens[0], lens[1])
            valid = (cell - slot * 1024 < limit).astype(f32)
            empty = jnp.where(valid > 0.0, 1.0 - r[:, 512:640], 0.0)
            for t in range(4):
                cs = slice(128 * t, 128 * t + 128)
                val = r[:, cs] + empty * rows_ref[7:8, cs]
                cells_ref[pl.ds(4 * (i % 4), 4), slot, :, cs] = val.astype(bf16).reshape(4, 64, 128)
            return 0
        lax.fori_loop(0, 8, block, 0)

    after = AFTER(dict(rows_of=rows_of, ln1=ln1, qkv=qkv, attention=attention, out_proj=out_proj, fc1=fc1, fc2=fc2, dec=dec))
    order = PIECE_ORDER
    pieces = [None] * 4
    k = 0
    for p, cl in enumerate(ag_chunks()):
        lst = []
        for ch in cl:
            lst.append(steps(k, ch)); k += 1
        pieces[p] = lst
    for t in range(len(pieces) + 5):
        for pos_, p in enumerate(order):
            s = t - pos_
            if s == 0: place(p)
            if 0 <= s < 6:
                for ch in pieces[p]: ch[s]()
            if s == 5: to_hbm(p)
        for fn in after.get(t, []): fn()
    for fn in after.get("end", []): fn()
    for cp, rc in firsts: cp.wait_send()
    for cp in sends: cp.wait_send()
    for cp in outs: cp.wait()

PIECE_ORDER = [3, 0, 1, 2]

def AFTER(f):
    return {"end": [f[n] for n in ("rows_of", "ln1", "qkv", "attention", "out_proj", "fc1", "fc2", "dec")]}

def k1_call(tok, lens, pos, vec6, qkv_s, out_s, fc1_s, fc2_s, dec_s):
    nk = sum(len(c) for c in ag_chunks())
    S = jax.ShapeDtypeStruct
    vm = pl.BlockSpec(memory_space=pltpu.VMEM)
    anyspec = pl.BlockSpec(memory_space=pl.ANY)
    V = pltpu.VMEM
    outs = (
        S((2, 9, 4, 4, 48, LW), bf16), S((2, 4, 4, 192, LW), bf16), S((8, 3072), f32), S((ROWS, 768), bf16),
        S((ROWS, 2304), bf16), S((12, ROWS, ROWS), bf16), S((ROWS, 768), bf16), S((ROWS, 768), f32),
        S((ROWS, 768), bf16), S((ROWS, 3072), bf16), S((ROWS, 3072), bf16), S((ROWS, 768), bf16), S((16, 2, 64, 512), bf16),
    )
    return pl.pallas_call(
        k1_kernel,
        out_shape=outs,
        in_specs=[vm, pl.BlockSpec(memory_space=pltpu.SMEM)] + [vm] * 10,
        out_specs=[anyspec, anyspec] + [vm] * 11,
        scratch_shapes=[
            V((2, 9, 4, 4, 48, LW), bf16), V((2, 4, 4, 192, LW), bf16),
            V((2, SROWS, LW), f32), V((2, SROWS, LW), bf16), V((8, SROWS, LW), bf16), V((ROWS, 640), bf16),
            pltpu.SemaphoreType.DMA((7,)), pltpu.SemaphoreType.DMA((7,)), pltpu.SemaphoreType.DMA(()),
            pltpu.SemaphoreType.DMA((nk, 12)), pltpu.SemaphoreType.DMA((nk, 12)), pltpu.SemaphoreType.DMA((4,)),
        ],
        compiler_params=pltpu.CompilerParams(collective_id=0, has_side_effects=True, vmem_limit_bytes=60 * 2**20),
        cost_estimate=pl.CostEstimate(flops=6 * 10**9, bytes_accessed=5 * 10**7, transcendentals=0),
        name="forward",
    )(tok, lens, pos, vec6, qkv_s, out_s, fc1_s, fc2_s, dec_s,
      jnp.asarray(perm_matrix(), bf16), jnp.asarray(cell_spread(), bf16), jnp.asarray(quad_spread(), bf16))


def k2_kernel(lens, g_hbm, g2_hbm, rows_ref, tok, a_ref, qkv_ref, p_hbm, o_ref, x2_ref, h2_ref, act_ref, dact_ref, e_ref,
              pos, dc_ref, pt_ref, m2_ref, m4_ref,
              tg_ref, oq_ref, oo_ref, of1_ref, of2_ref, od_ref, ov_ref,
              wd, wa, wb, sta, sta2, stc, sg, sg2, acc, acc2, xa, xa2, xb, xb2,
              dz, dx, dh, dm, df, dqkv, vsum, pb, db, fs, f1, fo, ssem, rsem, ss1, rs1, loc, wsem, psem, tsem, dsem):
    z, x, y, c = coords()
    zp, zm, zo = (z + 1) % 4, (z + 3) % 4, (z + 2) % 4
    xp, xm, xo = (x + 1) % 4, (x + 3) % 4, (x + 2) % 4
    o = 1 - c
    bar = pltpu.get_barrier_semaphore()
    targets = [dev(zp, x, y, c), dev(zm, x, y, c), dev(z, xp, y, c), dev(z, xm, y, c)]
    sib = dev(z, x, y, o)
    group = []
    for dy in range(4):
        for dc in range(2):
            if dy or dc:
                group.append((dy, dc, dev(z, x, (y + dy) % 4, (c + dc) % 2)))
    for t in targets + [g[2] for g in group]:
        pl.semaphore_signal(bar, inc=1, device_id=t, device_id_type=MESH)
    ld_d = pltpu.make_async_copy(g_hbm.at[:, 8], wd, wsem.at[0])
    ld_a = pltpu.make_async_copy(g2_hbm, wa, wsem.at[1])
    ld_b = pltpu.make_async_copy(g_hbm.at[:, 4:8], wb, wsem.at[2])
    ld_c = pltpu.make_async_copy(g_hbm.at[:, 0:4], wb, wsem.at[3])
    for l in (ld_d, ld_a, ld_b): l.start()
    pl.semaphore_wait(bar, len(targets) + len(group))

    sends = {}
    def send(k, i, src, dst, to):
        cp = pltpu.make_async_remote_copy(src, dst, ssem.at[k, i], rsem.at[k, i], device_id=to, device_id_type=MESH)
        cp.start(); sends[k, i] = cp
    def recv(k, i, v):
        pltpu.make_async_remote_copy(v, v, ssem.at[k, i], rsem.at[k, i], device_id=sib, device_id_type=MESH).wait_recv()

    def steps(k, piece, chunk):
        arr, order, full, fa, fb = chunk
        zx = order == "zx"
        if zx:
            d1p, d1m, d2p, d2m = targets
            p1, m1, o1, p2, m2, o2, s1_, s2_ = zp, zm, zo, xp, xm, xo, z, x
        else:
            d2p, d2m, d1p, d1m = targets
            p1, m1, o1, p2, m2, o2, s1_, s2_ = xp, xm, xo, zp, zm, zo, x, z
        def idx(part, a, b):
            zs, xs = (a, b) if zx else (b, a)
            r = pl.ds(part[0], part[1] - part[0])
            return (r, zs, xs) if arr == "g" else (zs, xs, r)
        A = acc if arr == "g" else acc2
        SG = sg if arr == "g" else sg2
        def stage(part):
            if piece == 2: return sta2.at[:, :, pl.ds(part[0], part[1] - part[0])]
            if piece == 3: return stc
            u = 4 * piece
            return sta.at[pl.ds(part[0] - u, part[1] - part[0])]
        def xav(way, part):
            r = slice(part[0], part[1])
            return xa.at[way, r] if arr == "g" else xa2.at[way, :, r]
        def xbv(way, part):
            r = slice(part[0], part[1])
            return xb.at[way, r] if arr == "g" else xb2.at[way, r]
        def add(part, a, b, *recvd):
            i = idx(part, a, b)
            t = A[i].astype(f32)
            for r in recvd: t = t + r[...].astype(f32)
            A[i] = t.astype(bf16)
        def st0():
            send(k, 8, stage(full), SG.at[idx(full, ALL, ALL)], sib)
        def st1():
            recv(k, 8, SG.at[idx(full, ALL, ALL)])
            def one(j, _):
                i = idx(full, j, ALL)
                A[i] = (A[i].astype(f32) + SG[i].astype(f32)).astype(bf16)
                return 0
            lax.fori_loop(0, 4, one, 0)
            send(k, 0, A.at[idx(fa, ALL, o2)], xav(0, fa), d2p)
            if fb is not None: send(k, 1, A.at[idx(fb, ALL, o2)], xav(0, fb), d2m)
        def st2():
            recv(k, 0, xav(0, fa)); add(fa, ALL, p2, xav(0, fa))
            send(k, 2, A.at[idx(full, ALL, p2)], xav(1, full), d2p)
            if fb is not None:
                recv(k, 1, xav(0, fb)); add(fb, ALL, m2, xav(0, fb))
            send(k, 3, A.at[idx(full, ALL, m2)], xav(2, full), d2m)
        def st3():
            recv(k, 2, xav(1, full)); recv(k, 3, xav(2, full))
            add(full, ALL, s2_, xav(1, full), xav(2, full))
            send(k, 4, A.at[idx(fa, o1, s2_)], xbv(0, fa), d1p)
            if fb is not None: send(k, 5, A.at[idx(fb, o1, s2_)], xbv(0, fb), d1m)
        def st4():
            recv(k, 4, xbv(0, fa)); add(fa, p1, s2_, xbv(0, fa))
            send(k, 6, A.at[idx(full, p1, s2_)], xbv(1, full), d1p)
            if fb is not None:
                recv(k, 5, xbv(0, fb)); add(fb, m1, s2_, xbv(0, fb))
            send(k, 7, A.at[idx(full, m1, s2_)], xbv(2, full), d1m)
        def st5():
            recv(k, 6, xbv(1, full)); recv(k, 7, xbv(2, full))
            add(full, s1_, s2_, xbv(1, full), xbv(2, full))
        return [st0, st1, st2, st3, st4, st5]

    table = {}
    keys = {}
    k = 0
    for p, cl in enumerate(ag_chunks()):
        lst = []
        for ch in cl:
            lst.append(steps(k, p, ch)); keys.setdefault(p, []).append(k); k += 1
        table[p] = lst
    def st(p, s):
        for ch in table[p]: ch[s]()

    def blocks(body, n=7):
        def step(i, _):
            body(pl.ds(pl.multiple_of(i * 48, 48), 48)); return 0
        lax.fori_loop(0, n, step, 0)
    ends0 = lens[0] + 2
    ends1 = ends0 + lens[1] + 2
    def col(base, width, unit):
        return pl.ds(pl.multiple_of(base, unit), width)

    def start_grads():
        p_ = jnp.broadcast_to(pos[0:1, 0:384], (8, 384)).astype(f32)
        r_ = lax.broadcasted_iota(jnp.int32, (8, 384), 1)
        seg = ((r_ >= ends0).astype(jnp.int32) + (r_ >= ends1).astype(jnp.int32)).astype(f32)
        target = jnp.where(p_ >= 0.0, seg * 1024.0 + p_, -1.0).T[0:ROWS, 0:1].astype(jnp.int32)
        dx[:, 0:512] = jnp.zeros((ROWS, 512), f32)
        vsum[...] = jnp.zeros_like(vsum)
        def load(i):
            return pltpu.make_async_copy(dc_ref.at[pl.ds(4 * (i % 4), 4), i // 4], db.at[i % 2], dsem.at[i % 2])
        load(0).start()
        def block(i, _):
            load(i).wait()
            pl.when(i < 7)(lambda: load(i + 1).start())
            slot = i // 4
            cell = i * 256 + lax.broadcasted_iota(jnp.int32, (1, 256), 1)
            hit = (target == cell).astype(f32)
            dcb = db[i % 2].reshape(256, 512)
            dx[:, 0:512] += jnp.dot(hit.astype(bf16), dcb, preferred_element_type=f32)
            limit = 4 * jnp.where(slot == 0, lens[0], lens[1])
            empty = jnp.where(cell - slot * 1024 < limit, 1.0 - jnp.sum(hit, axis=0, keepdims=True), 0.0)
            em = jnp.dot(jnp.broadcast_to(empty, (16, 256)).astype(bf16), dcb, preferred_element_type=f32)
            vsum[10:11, 0:512] += em[0:1]
            return 0
        lax.fori_loop(0, 8, block, 0)
        dz[...] = dx[:, 0:512].astype(bf16)
        vsum[9:10, 0:512] = jnp.sum(dz[...].astype(f32), axis=0, keepdims=True)

    def wdec(h):
        return wd[h, :, :, :, 0:256].reshape(768, 256)
    def dec_back():
        for n in range(2):
            rs = slice(n * 384, (n + 1) * 384)
            t = lax.dot_general(dz[:, 0:256], wdec(0)[rs], NT, preferred_element_type=f32)
            t = t + lax.dot_general(dz[:, 256:512], wdec(1)[rs], NT, preferred_element_type=f32)
            dx[:, rs] = t
            dm[:, rs] = t.astype(bf16)
        vsum[4:5, 0:768] = jnp.sum(dm[...].astype(f32), axis=0, keepdims=True)

    def grad_fc2(h, dst):
        def part(i, _):
            t = lax.dot_general(act_ref[:, col(i * 768, 768, 768)], dm[:, col(h * LW, LW, LW)], TN, preferred_element_type=f32)
            dst[i] = t.astype(bf16).reshape(4, 192, LW)
            return 0
        lax.fori_loop(0, 4, part, 0)

    def fc2_back():
        def part(i, _):
            cs = col(i * 768, 768, 768)
            t = lax.dot_general(dm[:, 0:LW], wa[0, i].reshape(768, LW), NT, preferred_element_type=f32)
            t = t + lax.dot_general(dm[:, LW:768], wa[1, i].reshape(768, LW), NT, preferred_element_type=f32)
            t = (t * dact_ref[:, cs].astype(f32)).astype(bf16)
            df[:, cs] = t
            vsum[5:6, cs] = jnp.sum(t.astype(f32), axis=0, keepdims=True)
            return 0
        lax.fori_loop(0, 4, part, 0)

    def wunit(h, u):
        return wb[h, u].reshape(768, LW)
    def fc1_back():
        for h in range(2):
            wt = lambda r: jnp.concatenate([wunit(h, u)[r] for u in range(4)], axis=1)
            for n in range(2):
                rs = slice(n * 384, (n + 1) * 384)
                t = lax.dot_general(df[:, h * 1536:(h + 1) * 1536], wt(rs), NT, preferred_element_type=f32)
                dh[:, rs] = t if h == 0 else dh[:, rs] + t

    def grad_fc1(h, dst, base):
        def part(u, _):
            t = lax.dot_general(h2_ref[...], df[:, col(h * 1536 + u * LW, LW, LW)], TN, preferred_element_type=f32)
            dst[base + u] = t.astype(bf16).reshape(4, 4, 48, LW)
            return 0
        lax.fori_loop(0, 4, part, 0)

    def norm_back(src, gain_row, into, out_lo, base):
        gain = rows_ref[gain_row:gain_row + 1, 0:768]
        def body(r):
            n, rstd = stats(src[r, :].astype(f32))
            d = dh[r, :]
            vsum[base:base + 1, 0:768] += jnp.sum(d * n, axis=0, keepdims=True)
            vsum[base + 1:base + 2, 0:768] += jnp.sum(d, axis=0, keepdims=True)
            dn = d * gain
            t = rstd * (dn - jnp.mean(dn, axis=-1, keepdims=True) - n * jnp.mean(dn * n, axis=-1, keepdims=True))
            t = dx[r, :] + t
            into[r, :] = t
            if out_lo is not None: out_lo[r, :] = t.astype(bf16)
        blocks(body)

    def out_back():
        t = lax.dot_general(dm[:, 0:LW], wunit(0, 3), NT, preferred_element_type=f32)
        t = t + lax.dot_general(dm[:, LW:768], wunit(1, 3), NT, preferred_element_type=f32)
        df[:, 0:768] = t.astype(bf16)

    def load_p(i):
        return pltpu.make_async_copy(p_hbm.at[pl.ds(2 * i, 2)], pb.at[i % 2], psem.at[i % 2])

    def attn_back(lo, hi):
        low = lax.broadcasted_iota(jnp.int32, (1, 128), 1) < 64
        def pair(i, _):
            load_p(i).wait()
            pl.when(i + 1 < HEADS_PAIRS)(lambda: load_p(i + 1).start())
            def cols(ref, base):
                return ref[:, col(base + i * 128, 128, 128)]
            q, kk, v, do = cols(qkv_ref, 0), cols(qkv_ref, 768), cols(qkv_ref, 1536), cols(df, 0)
            r = []
            for t in range(2):
                keep = low if t == 0 else jnp.logical_not(low)
                pr = pb[i % 2, t]
                dp = lax.dot_general(jnp.where(keep, do, jnp.zeros_like(do)), v, NT, preferred_element_type=f32)
                p32 = pr.astype(f32)
                ds = (p32 * (dp - jnp.sum(dp * p32, axis=-1, keepdims=True))).astype(bf16)
                dv = lax.dot_general(pr, do, TN, preferred_element_type=f32)
                dq = jnp.dot(ds, kk, preferred_element_type=f32)
                dk = lax.dot_general(ds, q, TN, preferred_element_type=f32)
                r.append((dq, dk, dv))
            dqkv[:, col(i * 128, 128, 128)] = (0.125 * jnp.where(low, r[0][0], r[1][0])).astype(bf16)
            dqkv[:, col(768 + i * 128, 128, 128)] = (0.125 * jnp.where(low, r[0][1], r[1][1])).astype(bf16)
            dqkv[:, col(1536 + i * 128, 128, 128)] = jnp.where(low, r[0][2], r[1][2]).astype(bf16)
            return 0
        lax.fori_loop(lo, hi, pair, 0)

    def qkv_back():
        for h in range(2):
            wt = lambda r: jnp.concatenate([wunit(h, u)[r] for u in range(3)], axis=1)
            for n in range(2):
                rs = slice(n * 384, (n + 1) * 384)
                t = lax.dot_general(dqkv[:, h * 1152:(h + 1) * 1152], wt(rs), NT, preferred_element_type=f32)
                dh[:, rs] = t if h == 0 else dh[:, rs] + t

    def grad_qkv(h, dst):
        def part(u, _):
            t = lax.dot_general(a_ref[...], dqkv[:, col(h * 1152 + u * LW, LW, LW)], TN, preferred_element_type=f32)
            dst[u] = t.astype(bf16).reshape(4, 4, 48, LW)
            return 0
        lax.fori_loop(0, 3, part, 0)
    def grad_out(h, dst):
        t = lax.dot_general(o_ref[...], dm[:, col(h * LW, LW, LW)], TN, preferred_element_type=f32)
        dst[3] = t.astype(bf16).reshape(4, 4, 48, LW)

    def vec_cols():
        rt = jnp.concatenate([vsum[0:8, 0:768], jnp.zeros((120, 768), f32)], axis=0)
        srow = lax.broadcasted_iota(jnp.int32, (128, 768), 0)
        rt = jnp.where(srow < 5, rt, 0.0)
        v = rt.T
        r2 = jnp.concatenate([vsum[0:16, 0:512], jnp.zeros((112, 512), f32)], axis=0)
        srow2 = lax.broadcasted_iota(jnp.int32, (128, 512), 0)
        r2 = jnp.where((srow2 == 9) | (srow2 == 10), r2, 0.0).astype(bf16)
        v = v + lax.dot_general(m2_ref[...], r2, NT, preferred_element_type=f32)
        lane = lax.broadcasted_iota(jnp.int32, (128, 768), 1) % 4
        parts = []
        for s in range(4):
            wrow = jnp.broadcast_to(vsum[5:6, 768 * s:768 * s + 768], (128, 768))
            wt = jnp.where(srow - 5 == lane, wrow, 0.0).astype(bf16)
            parts.append(lax.dot_general(m4_ref[...], wt, NT, preferred_element_type=f32))
        return (v + jnp.concatenate(parts, axis=0)).astype(bf16)

    def grad_dec(h, dst_store):
        t = lax.dot_general(e_ref[...], dz[:, col(h * 256, 256, 256)], TN, preferred_element_type=f32)
        dst_store(t.astype(bf16).reshape(4, 4, 48, 256), slice(0, 256))

    def acc8(v, cs): acc[8, :, :, :, cs] = v
    def stc8(v, cs): stc[0, :, :, :, cs] = v

    start_grads()
    ld_d.wait()
    dec_back()
    grad_fc2(o, sta2); st(2, 0)
    grad_fc2(c, acc2)
    ld_a.wait()
    fc2_back()
    st(2, 1)
    ld_b.wait()
    fc1_back()
    ld_c.start()
    load_p(0).start()
    grad_fc1(o, sta, 0); st(1, 0)
    st(2, 2)
    grad_fc1(c, acc, 4)
    norm_back(x2_ref, 2, dx, dm, 2)
    st(2, 3); st(1, 1)
    ld_c.wait()
    for kk in keys[1]: sends[kk, 8].wait_send(); del sends[kk, 8]
    grad_out(o, sta); grad_out(c, acc)
    out_back()
    st(2, 4); st(1, 2)
    attn_back(0, 3)
    st(2, 5); st(1, 3)
    attn_back(3, 6)
    st(1, 4)
    grad_qkv(o, sta)
    st(0, 0)
    grad_qkv(c, acc)
    st(1, 5)
    qkv_back()
    norm_back(tok, 0, dx, None, 0)
    dh[0:512 - ROWS, :] = jnp.zeros((512 - ROWS, 768), f32)
    tgs = [pltpu.make_async_copy(dx, tg_ref.at[0:ROWS], tsem.at[0]), pltpu.make_async_copy(dh.at[0:512 - ROWS], tg_ref.at[ROWS:512], tsem.at[1])]
    for t in tgs: t.start()
    st(0, 1)
    v = vec_cols().reshape(4, 4, 48, 128)
    zero = jnp.zeros_like(v)
    acc8(jnp.where(c == 0, v, zero), slice(256, 384)); stc8(jnp.where(c == 0, zero, v), slice(256, 384))
    grad_dec(o, stc8)
    st(3, 0)
    grad_dec(c, acc8)
    st(0, 2); st(3, 1); st(0, 3); st(3, 2); st(0, 4); st(3, 3); st(0, 5); st(3, 4); st(3, 5)

    blk = jnp.concatenate([acc[:, z, x].reshape(432, LW), acc2[z, x]], axis=0)
    fs[...] = jnp.dot(pt_ref[...], blk, preferred_element_type=f32).astype(bf16).reshape(8, SROWS, LW)
    me = 2 * y + c
    own = pltpu.make_async_copy(fs.at[me], f1.at[me], loc)
    own.start()
    lasts = []
    for i, (dy, dc, t) in enumerate(group):
        dst = 2 * ((y + dy) % 4) + (c + dc) % 2
        cp = pltpu.make_async_remote_copy(fs.at[dst], f1.at[me], ss1.at[i], rs1.at[i], device_id=t, device_id_type=MESH)
        cp.start()
        src = 2 * ((y + 4 - dy) % 4) + (c + dc) % 2
        rc = pltpu.make_async_remote_copy(fs.at[me], f1.at[src], ss1.at[i], rs1.at[i], device_id=t, device_id_type=MESH)
        lasts.append((cp, rc))
    own.wait()
    for cp, rc in lasts: rc.wait_recv()
    for h in range(2):
        t = f1[h].astype(f32)
        for yy in range(1, 4): t = t + f1[2 * yy + h].astype(f32)
        fo[h] = t
    for h in range(2):
        for u in range(3):
            oq_ref[:, h * 1152 + u * LW:h * 1152 + (u + 1) * LW] = fo[h, 6 * u:6 * u + 6, :]
        oo_ref[:, h * LW:(h + 1) * LW] = fo[h, 18:24, :]
        for u in range(4):
            of1_ref[:, h * 1536 + u * LW:h * 1536 + (u + 1) * LW] = fo[h, 24 + 6 * u:30 + 6 * u, :]
        of2_ref[:, h * LW:(h + 1) * LW] = fo[h, 48:72, :]
        od_ref[:, h * 256:(h + 1) * 256] = fo[h, 72:78, 0:256]
    ov_ref[...] = fo[0, 72:78, 256:384]
    for t in tgs: t.wait()
    for cp, rc in lasts: cp.wait_send()
    for cp in sends.values(): cp.wait_send()


def k2_call(lens, g, g2, rows, tok, a, qkv, pr, o, x2, h2, act, dact, e, pos, dc):
    nk = sum(len(c) for c in ag_chunks())
    S = jax.ShapeDtypeStruct
    vm = pl.BlockSpec(memory_space=pltpu.VMEM)
    anyspec = pl.BlockSpec(memory_space=pl.ANY)
    V, DMA = pltpu.VMEM, pltpu.SemaphoreType.DMA
    outs = (S((512, 768), f32), S((6, 2304), f32), S((6, 768), f32), S((6, 3072), f32), S((24, 768), f32), S((6, 512), f32), S((6, 128), f32))
    return pl.pallas_call(
        k2_kernel,
        out_shape=outs,
        in_specs=[pl.BlockSpec(memory_space=pltpu.SMEM), anyspec, anyspec] + [vm] * 4 + [anyspec] + [vm] * 7 + [anyspec] + [vm] * 3,
        out_specs=[anyspec] + [vm] * 6,
        scratch_shapes=[
            V((2, 4, 4, 48, LW), bf16), V((2, 4, 4, 192, LW), bf16), V((2, 4, 4, 4, 48, LW), bf16),
            V((4, 4, 4, 48, LW), bf16), V((4, 4, 192, LW), bf16), V((1, 4, 4, 48, LW), bf16),
            V((9, 4, 4, 48, LW), bf16), V((4, 4, 192, LW), bf16),
            V((9, 4, 4, 48, LW), bf16), V((4, 4, 192, LW), bf16),
            V((3, 9, 4, 48, LW), bf16), V((3, 4, 192, LW), bf16),
            V((3, 9, 48, LW), bf16), V((3, 192, LW), bf16),
            V((ROWS, 512), bf16), V((ROWS, 768), f32), V((ROWS, 768), f32), V((ROWS, 768), bf16), V((ROWS, 3072), bf16),
            V((ROWS, 2304), bf16), V((16, 3072), f32), V((2, 2, ROWS, ROWS), bf16), V((2, 4, 64, 512), bf16),
            V((8, SROWS, LW), bf16), V((8, SROWS, LW), bf16), V((2, SROWS, LW), f32),
            DMA((nk, 9)), DMA((nk, 9)), DMA((7,)), DMA((7,)), DMA(()), DMA((4,)), DMA((2,)), DMA((2,)), DMA((2,)),
        ],
        compiler_params=pltpu.CompilerParams(collective_id=1, has_side_effects=True, vmem_limit_bytes=60 * 2**20),
        cost_estimate=pl.CostEstimate(flops=12 * 10**9, bytes_accessed=5 * 10**7, transcendentals=0),
        name="backward",
    )(lens, g, g2, rows, tok, a, qkv, pr, o, x2, h2, act, dact, e, pos, dc,
      jnp.asarray(perm_matrix().T, bf16), jnp.asarray(cell_spread(), bf16), jnp.asarray(quad_spread(), bf16))


def body(tokens, chip_lengths, chip_ids, positions, ln1_gain, ln1_bias, qkv_weight, out_weight, ln2_gain, ln2_bias, fc1_weight,
         fc1_bias, fc2_weight, fc2_bias, dec_weight, dec_bias, mask_token, grid_cotangent):
    n = lax.axis_size("fsdp")
    tags = jnp.broadcast_to(chip_ids.astype(bf16)[None], (n, 2))
    owner = lax.all_to_all(tags, "fsdp", split_axis=0, concat_axis=0).reshape(32).astype(jnp.int32)
    placement = (jnp.arange(32, dtype=jnp.int32)[:, None] == owner[None, :]).astype(bf16)
    back = lax.dot_general(placement, grid_cotangent.reshape(32, -1), TN, preferred_element_type=f32).astype(bf16)
    cots = lax.all_to_all(back.reshape(16, 2, 64, 512), "fsdp", split_axis=0, concat_axis=0)
    vec = pack_vec(ln1_gain, ln1_bias, ln2_gain, ln2_bias, fc2_bias, fc1_bias, dec_bias, mask_token)
    pos = positions.reshape(1, 512)
    *saved, cells = k1_call(tokens, chip_lengths, pos, vec, qkv_weight, out_weight, fc1_weight, fc2_weight, dec_weight)
    g, g2, rows, *acts = saved
    arrived = lax.all_to_all(cells, "fsdp", split_axis=0, concat_axis=0)
    tg, dq, do, df1, df2, dd, dv = k2_call(chip_lengths, g, g2, rows, tokens, *acts, pos, cots)
    grid = jnp.dot(placement, arrived.reshape(32, -1), preferred_element_type=f32).astype(bf16).reshape(32, 64, 512)
    return (grid, tg, dv[:, 0], dv[:, 1], dq, do, dv[:, 2], dv[:, 3], df1, dv[:, 5:9].reshape(24), df2, dv[:, 4], dd,
            dv[:4, 9], dv[:4, 10])


def solution(mesh):
    both = ("dp", "fsdp")
    r1, r2, grid = P(both), P(both, None), P("dp", "fsdp", None)
    weights = (r1, r1, r2, r2, r1, r1, r2, r1, r2, r1, r2, r1, r1)
    return jax.shard_map(body, mesh=mesh, in_specs=(r2, r1, r1, r1) + weights + (grid,), out_specs=(grid, r2) + weights,
                         check_vma=False)
```

```python
import functools
import numpy as np
import jax, jax.numpy as jnp
from jax import lax
from jax.experimental import pallas as pl
from jax.experimental.pallas import tpu as pltpu
from jax.sharding import PartitionSpec as P

MESH = pl.DeviceIdType.MESH
LW = 384
SROWS = 80

def coords():
    dp = lax.axis_index("dp"); fs = lax.axis_index("fsdp")
    z = dp // 2
    x = (dp % 2) * 2 + fs // 8
    y = (fs % 8) // 2
    c = fs % 2
    return z, x, y, c

def dev(z, x, y, c):
    return (z * 2 + x // 2, (x % 2) * 8 + y * 2 + c)

def perm_matrix():
    m = np.zeros((624, 640), np.float32)
    for d in range(8):
        for u in range(8):
            for j in range(6):
                m[48 * u + 6 * d + j, d * 80 + 6 * u + j] = 1
        for j in range(6):
            m[48 * 8 + 6 * d + j, d * 80 + 72 + j] = 1
        for i in range(24):
            m[432 + 24 * d + i, d * 80 + 48 + i] = 1
    return m

ALL = slice(None)

def ag_chunks():
    return [
        [("g", "zx", (0, 2), (0, 1), (1, 2)), ("g", "xz", (2, 4), (2, 3), (3, 4))],
        [("g", "zx", (4, 6), (4, 5), (5, 6)), ("g", "xz", (6, 8), (6, 7), (7, 8))],
        [("g2", "zx", (0, 96), (0, 48), (48, 96)), ("g2", "xz", (96, 192), (96, 144), (144, 192))],
        [("g", "zx", (8, 9), (8, 9), None)],
    ]


ROWS = 336
HEADS_PAIRS = 6
D = 768
NT = (((1,), (1,)), ((), ()))
TN = (((0,), (0,)), ((), ()))
f32, bf16 = jnp.float32, jnp.bfloat16


def cell_spread():
    m = np.zeros((768, 512), np.float32)
    for d in range(128):
        for j in range(4):
            m[6 * d + j, 4 * d + j] = 1
    return m


def fc1_bias_spread():
    m = np.zeros((192, 768), np.float32)
    n = np.arange(768)
    m[6 * (n // 24) + n % 6, n] = 1
    return m


def peers(f):
    return [(r, (f + r) % 16) for r in range(1, 16)]


def greet(bar, devices):
    for t in devices:
        pl.semaphore_signal(bar, inc=1, device_id=t, device_id_type=MESH)


def stats(v):
    mean = jnp.mean(v, axis=-1, keepdims=True)
    center = v - mean
    rstd = lax.rsqrt(jnp.mean(center * center, axis=-1, keepdims=True) + 1e-6)
    return center * rstd, rstd


def gelu_pair(f):
    cdf = 0.5 * (1.0 + lax.erf(f * 0.7071067811865476))
    pdf = 0.3989422804014327 * jnp.exp(-0.5 * f * f)
    return f * cdf, cdf + f * pdf


def k1_kernel(ids, lens, pos, tok, l1g, l1b, qkv_s, out_s, l2g, l2b, fc1_s, fc1b, fc2_s, fc2b, dec_s, decb, maskt, cot_hbm,
              p_ref, m2_ref, m4_ref,
              g_hbm, g2_hbm, rows_hbm, a_hbm, qkv_hbm, p_hbm, o_hbm, x2_hbm, h2_hbm, act_hbm, dact_hbm, e_hbm, cells_hbm,
              dz_hbm, dx_hbm, dm_hbm, vs_hbm, inv_hbm,
              g_ref, g2_ref, rows_ref, a_ref, qkv_ref, p_out, o_ref, x2_ref, h2_ref, act_ref, dact_ref, e_ref, cells_ref,
              dz, dx, dm, vs, inv,
              sp, s_ref, s1, z_ref, vrow, tag, tags, idv, idm, cot, cotsend, dc, hits,
              ss1, rs1, loc, ssem, rsem, wsem, osem, tss, tsr, bss, bsr, mss, msr, lsem):
    z, x, y, c = coords()
    dp, f = lax.axis_index("dp"), lax.axis_index("fsdp")
    zp, zm, zo = (z + 1) % 4, (z + 3) % 4, (z + 2) % 4
    xp, xm, xo = (x + 1) % 4, (x + 3) % 4, (x + 2) % 4
    o = 1 - c
    bar = pltpu.get_barrier_semaphore()
    targets = [dev(zp, x, y, c), dev(zm, x, y, c), dev(z, xp, y, c), dev(z, xm, y, c)]
    group = []
    for dy in range(4):
        for dc_ in range(2):
            if dy or dc_:
                group.append((dy, dc_, dev(z, x, (y + dy) % 4, (c + dc_) % 2)))
    greeted = targets + [(dp, g) for _, g in peers(f)]
    greet(bar, greeted)
    ld_cot = pltpu.make_async_copy(cot_hbm, cot, lsem.at[0])
    ld_cot.start()

    sp[...] = jnp.zeros_like(sp)
    for h in range(2):
        for u in range(3):
            sp[h, 6 * u:6 * u + 6, :] = qkv_s[:, h * 1152 + u * LW:h * 1152 + (u + 1) * LW].astype(f32)
        sp[h, 18:24, :] = out_s[:, h * LW:(h + 1) * LW].astype(f32)
        for u in range(4):
            sp[h, 24 + 6 * u:30 + 6 * u, :] = fc1_s[:, h * 1536 + u * LW:h * 1536 + (u + 1) * LW].astype(f32)
        sp[h, 48:72, :] = fc2_s[:, h * LW:(h + 1) * LW].astype(f32)
        sp[h, 72:78, 0:256] = dec_s[:, h * 256:(h + 1) * 256].astype(f32)
    vrow[...] = jnp.zeros_like(vrow)
    for i, r in enumerate((l1g, l1b, l2g, l2b, fc2b)):
        vrow[i:i + 1, 0:6] = r[...].astype(f32)
    for q in range(4):
        vrow[5 + q:6 + q, 0:6] = fc1b[:, 6 * q:6 * q + 6].astype(f32)
    vrow[9:10, 0:4] = decb[...].astype(f32)
    vrow[10:11, 0:4] = maskt[...].astype(f32)
    sp[0, 72:78, 256:384] = vrow[...].T[0:6]
    s_ref[...] = sp[...].astype(bf16)
    first_small = lens[0] < lens[1]
    trow = lax.broadcasted_iota(jnp.int32, (8, 128), 0)
    tag[...] = jnp.where(trow == 0, jnp.where(first_small, ids[1], ids[0]), jnp.where(first_small, ids[0], ids[1]))
    pl.semaphore_wait(bar, len(greeted))

    me = 2 * y + c
    own = pltpu.make_async_copy(s_ref.at[c], s1.at[me], loc)
    own.start()
    firsts = []
    for i, (dy, dc_, t) in enumerate(group):
        cp = pltpu.make_async_remote_copy(s_ref.at[(c + dc_) % 2], s1.at[me], ss1.at[i], rs1.at[i], device_id=t, device_id_type=MESH)
        cp.start()
        src = 2 * ((y + 4 - dy) % 4) + (c + dc_) % 2
        rc = pltpu.make_async_remote_copy(s_ref.at[c], s1.at[src], ss1.at[i], rs1.at[i], device_id=t, device_id_type=MESH)
        firsts.append((cp, rc))

    tagged = []
    tags[f] = tag[...]
    for r, g in peers(f):
        cp = pltpu.make_async_remote_copy(tag, tags.at[f], tss.at[r], tsr.at[r], device_id=(dp, g), device_id_type=MESH)
        cp.start(); tagged.append(cp)
    for r, g in peers(f):
        src = (f + 16 - r) % 16
        pltpu.make_async_remote_copy(tag, tags.at[src], tss.at[r], tsr.at[r], device_id=(dp, g), device_id_type=MESH).wait_recv()
    for s in range(16):
        idv[s:s + 1, :] = tags[s, 0:1, :]
        idv[16 + s:17 + s, :] = tags[s, 1:2, :]
    ld_ids = pltpu.make_async_copy(idv, idm, lsem.at[1])
    ld_ids.start()
    srow = lax.broadcasted_iota(jnp.int32, (32, 128), 0)
    hit = idv[...] == lax.broadcasted_iota(jnp.int32, (32, 128), 1)
    place_of = jnp.where((srow >= 16) & (f >= 4), 32, srow)
    inv[...] = jnp.broadcast_to(jnp.sum(jnp.where(hit, place_of, 0), axis=0, keepdims=True), (8, 128))
    ld_ids.wait()
    ld_cot.wait()
    for s in range(32):
        cotsend[s] = cot[idm[s, 0]]

    own.wait()
    for cp, rc in firsts:
        rc.wait_recv()

    few = f < 4
    def to_peer(i, g):
        big = pltpu.make_async_remote_copy(cotsend.at[g], dc.at[f], bss.at[i], bsr.at[i], device_id=(dp, g), device_id_type=MESH)
        return big
    def small_to_peer(i, g):
        return pltpu.make_async_remote_copy(cotsend.at[16 + g], dc.at[16 + f % 4], mss.at[i], msr.at[f % 4], device_id=(dp, g), device_id_type=MESH)
    own_dc = pltpu.make_async_copy(cotsend.at[f], dc.at[f], lsem.at[2])
    own_small = pltpu.make_async_copy(cotsend.at[16 + f], dc.at[16 + f % 4], lsem.at[3])
    def send_cotangents():
        own_dc.start()
        for r, g in peers(f):
            to_peer(r, g).start()
        @pl.when(few)
        def _():
            own_small.start()
            for r, g in peers(f):
                small_to_peer(r, g).start()
    def get_cotangents():
        own_dc.wait()
        for r, g in peers(f):
            src = (f + 16 - r) % 16
            pltpu.make_async_remote_copy(cotsend.at[g], dc.at[src], bss.at[r], bsr.at[r], device_id=(dp, g), device_id_type=MESH).wait_recv()
        for s in range(4):
            @pl.when(f != s)
            def _():
                pltpu.make_async_remote_copy(cotsend.at[16], dc.at[16 + s], mss.at[0], msr.at[s], device_id=(dp, s), device_id_type=MESH).wait_recv()
        @pl.when(few)
        def _():
            own_small.wait()
    def finish_cotangents():
        for r, g in peers(f):
            to_peer(r, g).wait_send()
        @pl.when(few)
        def _():
            for r, g in peers(f):
                small_to_peer(r, g).wait_send()

    def relay(lo, hi):
        flat = s1[...].reshape(640, LW)
        r = jnp.dot(p_ref[lo:hi, :], flat, preferred_element_type=f32)
        return r.astype(bf16)

    def place(p):
        if p == 0: g_ref[c, 0:4, z, x] = relay(0, 192).reshape(4, 48, LW)
        if p == 1: g_ref[c, 4:8, z, x] = relay(192, 384).reshape(4, 48, LW)
        if p == 2: g2_ref[c, z, x] = relay(432, 624)
        if p == 3: g_ref[c, 8, z, x] = relay(384, 432)

    def view(arr, h, part, zs, xs):
        if arr == "g":
            return g_ref.at[h, part[0]:part[1], zs, xs]
        return g2_ref.at[h, zs, xs, part[0]:part[1]]

    sends = []
    def mk(k, i, src, dst, to):
        return pltpu.make_async_remote_copy(src, dst, ssem.at[k, i], rsem.at[k, i], device_id=to, device_id_type=MESH)
    def send(k, i, v, to):
        cp = mk(k, i, v, v, to); cp.start(); sends.append(cp)
    def recv(k, i, v):
        mk(k, i, v, v, dev(z, x, y, o)).wait_recv()

    def steps(k, chunk):
        arr, order, full, fa, fb = chunk
        if order == "zx":
            d1p, d1m, d2p, d2m = targets
            p1, m1, o1, p2, m2, o2, s1_, s2_ = zp, zm, zo, xp, xm, xo, z, x
            V = lambda part, a, b, h=c: view(arr, h, part, a, b)
        else:
            d2p, d2m, d1p, d1m = targets
            p1, m1, o1, p2, m2, o2, s1_, s2_ = xp, xm, xo, zp, zm, zo, x, z
            V = lambda part, a, b, h=c: view(arr, h, part, b, a)
        sib = dev(z, x, y, o)
        def st0():
            send(k, 0, V(full, s1_, s2_), d1p)
            send(k, 1, V(full, s1_, s2_), d1m)
        def st1():
            recv(k, 0, V(full, m1, s2_))
            send(k, 2, V(fa, m1, s2_), d1p)
            recv(k, 1, V(full, p1, s2_))
            if fb is not None: send(k, 3, V(fb, p1, s2_), d1m)
        def st2():
            recv(k, 2, V(fa, o1, s2_))
            if fb is not None: recv(k, 3, V(fb, o1, s2_))
            send(k, 4, V(full, ALL, s2_), d2p)
            send(k, 5, V(full, ALL, s2_), d2m)
            send(k, 8, V(full, ALL, s2_), sib)
        def st3():
            recv(k, 4, V(full, ALL, m2))
            send(k, 6, V(fa, ALL, m2), d2p)
            send(k, 9, V(full, ALL, m2), sib)
            recv(k, 5, V(full, ALL, p2))
            if fb is not None: send(k, 7, V(fb, ALL, p2), d2m)
            send(k, 10, V(full, ALL, p2), sib)
        def st4():
            recv(k, 6, V(fa, ALL, o2))
            if fb is not None: recv(k, 7, V(fb, ALL, o2))
            send(k, 11, V(full, ALL, o2), sib)
        def st5():
            recv(k, 8, V(full, ALL, s2_, o))
            recv(k, 9, V(full, ALL, m2, o))
            recv(k, 10, V(full, ALL, p2, o))
            recv(k, 11, V(full, ALL, o2, o))
        return [st0, st1, st2, st3, st4, st5]

    outs = []
    def to_hbm(p):
        if p == 2: cp = pltpu.make_async_copy(g2_ref, g2_hbm, wsem.at[p])
        else:
            u0, u1 = ((0, 4), (4, 8), None, (8, 9))[p]
            cp = pltpu.make_async_copy(g_ref.at[:, u0:u1], g_hbm.at[:, u0:u1], wsem.at[p])
        cp.start(); outs.append(cp)

    def blocks(body, n=7):
        def step(i, _):
            body(pl.ds(pl.multiple_of(i * 48, 48), 48)); return 0
        lax.fori_loop(0, n, step, 0)

    def w(h, u):
        return g_ref[h, u].reshape(768, LW)

    def rows_of():
        v = jnp.concatenate([g_ref[0, 8, zz, xx, :, 256:384] for zz in range(4) for xx in range(4)], axis=0)
        vt = v.astype(f32).T
        rows_ref[0:5, 0:768] = vt[0:5]
        md = lax.dot_general(v, m2_ref[...], TN, preferred_element_type=f32)
        rows_ref[6:8, 0:512] = md[9:11]
        lane = (lax.broadcasted_iota(jnp.int32, (8, 768), 1) % 24) // 6
        row = lax.broadcasted_iota(jnp.int32, (8, 768), 0)
        for s in range(4):
            q = lax.dot_general(v[192 * s:192 * s + 192], m4_ref[...], TN, preferred_element_type=f32)
            q = jnp.where(row == lane, q[5:13], 0.0)
            rows_ref[5:6, 768 * s:768 * s + 768] = jnp.sum(q, axis=0, keepdims=True)

    def ln1():
        def body(r):
            n, _ = stats(tok[r, :].astype(f32))
            a_ref[r, :] = (n * rows_ref[0:1, 0:768] + rows_ref[1:2, 0:768]).astype(bf16)
        blocks(body)

    def qkv():
        for h in range(2):
            wt = jnp.concatenate([w(h, u) for u in range(3)], axis=1)
            qkv_ref[:, h * 1152:(h + 1) * 1152] = jnp.dot(a_ref[...], wt, preferred_element_type=f32).astype(bf16)

    ends0 = lens[0] + 2
    ends1 = ends0 + lens[1] + 2
    def seg(shape, axis):
        r = lax.broadcasted_iota(jnp.int32, shape, axis)
        return (r >= ends0).astype(jnp.int32) + (r >= ends1).astype(jnp.int32)

    def attention(lo, hi):
        low = lax.broadcasted_iota(jnp.int32, (1, 128), 1) < 64
        same = seg((ROWS, 1), 0) == seg((1, ROWS), 1)
        bias = jnp.where(same, 0.0, -1e30)
        def pair(i, _):
            def cols(base):
                return qkv_ref[:, pl.ds(pl.multiple_of(base + i * 128, 128), 128)]
            q, k, v = cols(0), cols(768), cols(1536)
            outs_ = []
            for t in range(2):
                keep = low if t == 0 else jnp.logical_not(low)
                s = lax.dot_general(jnp.where(keep, q, jnp.zeros_like(q)), k, NT, preferred_element_type=f32)
                s = jnp.where(same, s * 0.125, -1e30)
                m = jnp.max(s, axis=-1, keepdims=True)
                ex = jnp.exp(s - m)
                pr = (ex / jnp.sum(ex, axis=-1, keepdims=True)).astype(bf16)
                p_out[2 * i + t] = pr
                outs_.append(jnp.dot(pr, v, preferred_element_type=f32))
            o_ref[:, pl.ds(pl.multiple_of(i * 128, 128), 128)] = jnp.where(low, outs_[0], outs_[1]).astype(bf16)
            return 0
        lax.fori_loop(lo, hi, pair, 0)

    def out_proj():
        for h in range(2):
            cs = slice(h * LW, (h + 1) * LW)
            x2_ref[:, cs] = tok[0:ROWS, cs].astype(f32) + jnp.dot(o_ref[...], w(h, 3), preferred_element_type=f32)
        def body(r):
            n, _ = stats(x2_ref[r, :])
            h2_ref[r, :] = (n * rows_ref[2:3, 0:768] + rows_ref[3:4, 0:768]).astype(bf16)
        blocks(body)

    def fc1():
        for h in range(2):
            def unit(u, _):
                cs = pl.ds(pl.multiple_of(h * 1536 + u * LW, LW), LW)
                f = jnp.dot(h2_ref[...], w(h, 4 + u), preferred_element_type=f32) + rows_ref[5:6, cs]
                g, dg = gelu_pair(f)
                act_ref[:, cs] = g.astype(bf16)
                dact_ref[:, cs] = dg.astype(bf16)
                return 0
            lax.fori_loop(0, 4, unit, 0)

    def fc2():
        for h in range(2):
            cs = slice(h * LW, (h + 1) * LW)
            t = jnp.dot(act_ref[...], g2_ref[h].reshape(3072, LW), preferred_element_type=f32)
            e_ref[:, cs] = (x2_ref[:, cs] + t + rows_ref[4:5, cs]).astype(bf16)

    def dec():
        for h in range(2):
            cs = slice(h * 256, (h + 1) * 256)
            t = jnp.dot(e_ref[...], g_ref[h, 8, :, :, :, 0:256].reshape(768, 256), preferred_element_type=f32)
            z_ref[:, cs] = (t + rows_ref[6:7, cs]).astype(bf16)
        z_ref[:, 512:640] = jnp.ones((ROWS, 128), bf16)
        def block(i, _):
            fill = hits[pl.ds(pl.multiple_of(i * 256, 256), 256), :]
            r = jnp.dot(fill, z_ref[...], preferred_element_type=f32)
            empty = 1.0 - r[:, 512:640]
            for t in range(4):
                cs = slice(128 * t, 128 * t + 128)
                val = r[:, cs] + empty * rows_ref[7:8, cs]
                cells_ref[pl.ds(4 * i, 4), :, cs] = val.astype(bf16).reshape(4, 64, 128)
            return 0
        lax.fori_loop(0, 5, block, 0)

    def fills():
        p_ = pos[0:1, 0:ROWS]
        large = seg((1, ROWS), 1) == jnp.where(first_small, 1, 0)
        target = jnp.where(p_ >= 0, jnp.where(large, p_, 1024 + p_), -1)
        def block(i, _):
            cell = i * 256 + lax.broadcasted_iota(jnp.int32, (256, 1), 0)
            hits[pl.ds(pl.multiple_of(i * 256, 256), 256), :] = (cell == target).astype(f32).astype(bf16)
            return 0
        lax.fori_loop(0, 5, block, 0)

    def cell_grads():
        get_cotangents()
        d = dc[...].reshape(1280, 512)
        dz[...] = lax.dot_general(hits[...], d, TN, preferred_element_type=f32).astype(bf16)
        covered = lax.dot_general(jnp.ones((16, ROWS), bf16), hits[...], NT, preferred_element_type=f32)
        vs[10:11, :] = jnp.dot((1.0 - covered).astype(bf16), d, preferred_element_type=f32)[0:1]
        vs[9:10, :] = jnp.sum(dz[...].astype(f32), axis=0, keepdims=True)
        for n in range(2):
            rs = slice(n * 384, (n + 1) * 384)
            wt = [g_ref[h, 8, :, :, :, 0:256].reshape(768, 256)[rs] for h in range(2)]
            t = lax.dot_general(dz[:, 0:256], wt[0], NT, preferred_element_type=f32)
            t = t + lax.dot_general(dz[:, 256:512], wt[1], NT, preferred_element_type=f32)
            dx[:, rs] = t
            dm[:, rs] = t.astype(bf16)

    kept = dict(rows=(rows_ref, rows_hbm), a=(a_ref, a_hbm), qkv=(qkv_ref, qkv_hbm), p=(p_out, p_hbm), o=(o_ref, o_hbm),
                x2=(x2_ref, x2_hbm), h2=(h2_ref, h2_hbm), act=(act_ref, act_hbm), dact=(dact_ref, dact_hbm), e=(e_ref, e_hbm),
                cells=(cells_ref, cells_hbm), dz=(dz, dz_hbm), dx=(dx, dx_hbm), dm=(dm, dm_hbm), vs=(vs, vs_hbm), inv=(inv, inv_hbm))
    def keep(*names):
        for n in names:
            cp = pltpu.make_async_copy(*kept[n], osem.at[list(kept).index(n)])
            cp.start(); outs.append(cp)

    vs[...] = jnp.zeros_like(vs)
    rows_ref[...] = jnp.zeros_like(rows_ref)
    after = {
        0: [send_cotangents, lambda: keep("inv"), fills],
        5: [rows_of, ln1, lambda: keep("rows", "a")],
        6: [qkv, lambda: attention(0, 3), lambda: keep("qkv")],
        7: [lambda: attention(3, 6), out_proj, lambda: keep("p", "o", "x2", "h2"), fc1, lambda: keep("act", "dact"), cell_grads,
            lambda: keep("dz", "dx", "dm", "vs")],
        8: [fc2, lambda: keep("e"), dec, lambda: keep("cells")],
    }
    order = PIECE_ORDER
    pieces = [None] * 4
    k = 0
    for p, cl in enumerate(ag_chunks()):
        lst = []
        for ch in cl:
            lst.append(steps(k, ch)); k += 1
        pieces[p] = lst
    for t in range(len(pieces) + 5):
        for pos_, p in enumerate(order):
            s = t - pos_
            if s == 0: place(p)
            if 0 <= s < 6:
                for ch in pieces[p]: ch[s]()
            if s == 5: to_hbm(p)
        for fn in after.get(t, []): fn()
    for cp, rc in firsts: cp.wait_send()
    for cp in sends: cp.wait_send()
    for cp in tagged: cp.wait_send()
    finish_cotangents()
    for cp in outs: cp.wait()

PIECE_ORDER = [3, 0, 1, 2]

def k1_call(*args):
    nk = sum(len(c) for c in ag_chunks())
    S = jax.ShapeDtypeStruct
    vm, smem = pl.BlockSpec(memory_space=pltpu.VMEM), pl.BlockSpec(memory_space=pltpu.SMEM)
    anyspec = pl.BlockSpec(memory_space=pl.ANY)
    V, DMA = pltpu.VMEM, pltpu.SemaphoreType.DMA
    outs = (
        S((2, 9, 4, 4, 48, LW), bf16), S((2, 4, 4, 192, LW), bf16), S((8, 3072), f32), S((ROWS, 768), bf16),
        S((ROWS, 2304), bf16), S((12, ROWS, ROWS), bf16), S((ROWS, 768), bf16), S((ROWS, 768), f32),
        S((ROWS, 768), bf16), S((ROWS, 3072), bf16), S((ROWS, 3072), bf16), S((ROWS, 768), bf16), S((20, 64, 512), bf16),
        S((ROWS, 512), bf16), S((ROWS, 768), f32), S((ROWS, 768), bf16), S((16, 512), f32), S((8, 128), jnp.int32),
    )
    return pl.pallas_call(
        k1_kernel,
        out_shape=outs,
        in_specs=[smem, smem] + [vm] * 15 + [anyspec] + [vm] * 3,
        out_specs=[anyspec] * 18,
        scratch_shapes=[V(t.shape, t.dtype) for t in outs] + [
            V((2, SROWS, LW), f32), V((2, SROWS, LW), bf16), V((8, SROWS, LW), bf16), V((ROWS, 640), bf16), V((128, 128), f32),
            V((8, 128), jnp.int32), V((16, 8, 128), jnp.int32), V((32, 128), jnp.int32), pltpu.SMEM((32, 128), jnp.int32),
            V((32, 64, 512), bf16), V((32, 64, 512), bf16), V((20, 64, 512), bf16), V((1280, ROWS), bf16),
            DMA((7,)), DMA((7,)), DMA(()), DMA((nk, 12)), DMA((nk, 12)), DMA((4,)), DMA((16,)), DMA((16,)), DMA((16,)),
            DMA((16,)), DMA((16,)), DMA((16,)), DMA((4,)), DMA((4,)),
        ],
        compiler_params=pltpu.CompilerParams(collective_id=0, has_side_effects=True, vmem_limit_bytes=60 * 2**20),
        cost_estimate=pl.CostEstimate(flops=6 * 10**9, bytes_accessed=5 * 10**7, transcendentals=0),
        name="forward",
    )(*args, jnp.asarray(perm_matrix(), bf16), jnp.asarray(cell_spread(), bf16), jnp.asarray(fc1_bias_spread(), bf16))


def k2_kernel(g_hbm, g2_hbm, rows_hbm, a_hbm, qkv_hbm, p_hbm, o_hbm, x2_hbm, h2_hbm, act_hbm, dact_hbm, e_hbm, cells_hbm,
              dz_hbm, dx_hbm, dm_hbm, vs_hbm, tok_hbm, pt_ref, m2_ref, m4_ref,
              tg_ref, arr, oq_ref, oo_ref, of1_ref, of2_ref, od_ref, v0_ref, v1_ref, v2_ref, v3_ref, v4_ref, vf_ref, vd_ref, vm_ref,
              rows_ref, a_ref, qkv_ref, o_ref, x2_ref, h2_ref, act_ref, dact_ref, e_ref, dz, dx, dm, vs, tok,
              wa, wb, sta, sta2, stc, sg, sg2, acc, acc2, xa, xa2, xb, xb2,
              dh, df, dqkv, vsum, pb, fs, f1, fo, zb, vt,
              ssem, rsem, ss1, rs1, loc, wsem, psem, tsem, isem, css, csr, csl):
    z, x, y, c = coords()
    dp, f = lax.axis_index("dp"), lax.axis_index("fsdp")
    zp, zm, zo = (z + 1) % 4, (z + 3) % 4, (z + 2) % 4
    xp, xm, xo = (x + 1) % 4, (x + 3) % 4, (x + 2) % 4
    o = 1 - c
    bar = pltpu.get_barrier_semaphore()
    targets = [dev(zp, x, y, c), dev(zm, x, y, c), dev(z, xp, y, c), dev(z, xm, y, c)]
    sib = dev(z, x, y, o)
    group = []
    for dy in range(4):
        for dc in range(2):
            if dy or dc:
                group.append((dy, dc, dev(z, x, (y + dy) % 4, (c + dc) % 2)))
    greeted = targets + [(dp, g) for _, g in peers(f)]
    greet(bar, greeted)
    loads = {}
    def load(name, src, dst):
        loads[name] = pltpu.make_async_copy(src, dst, isem.at[len(loads)])
        return loads[name]
    for name, src, dst in (
        ("dm", dm_hbm, dm), ("act", act_hbm, act_ref), ("fc2", g2_hbm, wa), ("dact", dact_hbm, dact_ref), ("fc1", g_hbm.at[:, 4:8], wb),
        ("h2", h2_hbm, h2_ref), ("x2", x2_hbm, x2_ref), ("dx", dx_hbm, dx), ("rows", rows_hbm, rows_ref), ("o", o_hbm, o_ref),
        ("qkv", qkv_hbm, qkv_ref), ("e", e_hbm, e_ref), ("dz", dz_hbm, dz), ("a", a_hbm, a_ref), ("tok", tok_hbm.at[0:ROWS], tok),
        ("vs", vs_hbm, vs),
    ):
        load(name, src, dst).start()
    def need(*names):
        for n in names: loads[n].wait()
    ld_c = pltpu.make_async_copy(g_hbm.at[:, 0:4], wb, wsem.at[0])
    zb[...] = jnp.zeros_like(zb)
    vt[...] = jnp.zeros_like(vt)
    vsum[...] = jnp.zeros_like(vsum)
    pl.semaphore_wait(bar, len(greeted))

    few = f < 4
    def cells_to(i, g):
        return pltpu.make_async_remote_copy(cells_hbm.at[g], arr.at[f], css.at[i], csr.at[i], device_id=(dp, g), device_id_type=MESH)
    def small_cells_to(i, g):
        return pltpu.make_async_remote_copy(cells_hbm.at[16 + g % 4], arr.at[16 + f], css.at[16 + i], csr.at[16 + i], device_id=(dp, g), device_id_type=MESH)
    locals_ = [pltpu.make_async_copy(cells_hbm.at[f], arr.at[f], csl.at[0]), pltpu.make_async_copy(zb, arr.at[32], csl.at[1])]
    own_small = pltpu.make_async_copy(cells_hbm.at[16 + f % 4], arr.at[16 + f], csl.at[2])
    for l in locals_: l.start()
    for r, g in peers(f):
        cells_to(r, g).start()
        @pl.when(g < 4)
        def _():
            small_cells_to(r, g).start()
    @pl.when(few)
    def _():
        own_small.start()
    def finish_cells():
        for l in locals_: l.wait()
        for r, g in peers(f):
            src = (f + 16 - r) % 16
            pltpu.make_async_remote_copy(cells_hbm.at[g], arr.at[src], css.at[r], csr.at[r], device_id=(dp, g), device_id_type=MESH).wait_recv()
            cells_to(r, g).wait_send()
            @pl.when(g < 4)
            def _():
                small_cells_to(r, g).wait_send()
        @pl.when(few)
        def _():
            own_small.wait()
            for r, g in peers(f):
                src = (f + 16 - r) % 16
                pltpu.make_async_remote_copy(cells_hbm.at[16], arr.at[16 + src], css.at[16 + r], csr.at[16 + r], device_id=(dp, g), device_id_type=MESH).wait_recv()

    sends = {}
    def send(k, i, src, dst, to):
        cp = pltpu.make_async_remote_copy(src, dst, ssem.at[k, i], rsem.at[k, i], device_id=to, device_id_type=MESH)
        cp.start(); sends[k, i] = cp
    def recv(k, i, v):
        pltpu.make_async_remote_copy(v, v, ssem.at[k, i], rsem.at[k, i], device_id=sib, device_id_type=MESH).wait_recv()

    def steps(k, piece, chunk):
        arr, order, full, fa, fb = chunk
        zx = order == "zx"
        if zx:
            d1p, d1m, d2p, d2m = targets
            p1, m1, o1, p2, m2, o2, s1_, s2_ = zp, zm, zo, xp, xm, xo, z, x
        else:
            d2p, d2m, d1p, d1m = targets
            p1, m1, o1, p2, m2, o2, s1_, s2_ = xp, xm, xo, zp, zm, zo, x, z
        def idx(part, a, b):
            zs, xs = (a, b) if zx else (b, a)
            r = pl.ds(part[0], part[1] - part[0])
            return (r, zs, xs) if arr == "g" else (zs, xs, r)
        A = acc if arr == "g" else acc2
        SG = sg if arr == "g" else sg2
        def stage(part):
            if piece == 2: return sta2.at[:, :, pl.ds(part[0], part[1] - part[0])]
            if piece == 3: return stc
            u = 4 * piece
            return sta.at[pl.ds(part[0] - u, part[1] - part[0])]
        def xav(way, part):
            r = slice(part[0], part[1])
            return xa.at[way, r] if arr == "g" else xa2.at[way, :, r]
        def xbv(way, part):
            r = slice(part[0], part[1])
            return xb.at[way, r] if arr == "g" else xb2.at[way, r]
        def add(part, a, b, *recvd):
            i = idx(part, a, b)
            t = A[i].astype(f32)
            for r in recvd: t = t + r[...].astype(f32)
            A[i] = t.astype(bf16)
        def st0():
            send(k, 8, stage(full), SG.at[idx(full, ALL, ALL)], sib)
        def st1():
            recv(k, 8, SG.at[idx(full, ALL, ALL)])
            def one(j, _):
                i = idx(full, j, ALL)
                A[i] = (A[i].astype(f32) + SG[i].astype(f32)).astype(bf16)
                return 0
            lax.fori_loop(0, 4, one, 0)
            send(k, 0, A.at[idx(fa, ALL, o2)], xav(0, fa), d2p)
            if fb is not None: send(k, 1, A.at[idx(fb, ALL, o2)], xav(0, fb), d2m)
        def st2():
            recv(k, 0, xav(0, fa)); add(fa, ALL, p2, xav(0, fa))
            send(k, 2, A.at[idx(full, ALL, p2)], xav(1, full), d2p)
            if fb is not None:
                recv(k, 1, xav(0, fb)); add(fb, ALL, m2, xav(0, fb))
            send(k, 3, A.at[idx(full, ALL, m2)], xav(2, full), d2m)
        def st3():
            recv(k, 2, xav(1, full)); recv(k, 3, xav(2, full))
            add(full, ALL, s2_, xav(1, full), xav(2, full))
            send(k, 4, A.at[idx(fa, o1, s2_)], xbv(0, fa), d1p)
            if fb is not None: send(k, 5, A.at[idx(fb, o1, s2_)], xbv(0, fb), d1m)
        def st4():
            recv(k, 4, xbv(0, fa)); add(fa, p1, s2_, xbv(0, fa))
            send(k, 6, A.at[idx(full, p1, s2_)], xbv(1, full), d1p)
            if fb is not None:
                recv(k, 5, xbv(0, fb)); add(fb, m1, s2_, xbv(0, fb))
            send(k, 7, A.at[idx(full, m1, s2_)], xbv(2, full), d1m)
        def st5():
            recv(k, 6, xbv(1, full)); recv(k, 7, xbv(2, full))
            add(full, s1_, s2_, xbv(1, full), xbv(2, full))
        return [st0, st1, st2, st3, st4, st5]

    table = {}
    keys = {}
    k = 0
    for p, cl in enumerate(ag_chunks()):
        lst = []
        for ch in cl:
            lst.append(steps(k, p, ch)); keys.setdefault(p, []).append(k); k += 1
        table[p] = lst
    def st(p, s):
        for ch in table[p]: ch[s]()

    def blocks(body, n=7):
        def step(i, _):
            body(pl.ds(pl.multiple_of(i * 48, 48), 48)); return 0
        lax.fori_loop(0, n, step, 0)
    def col(base, width, unit):
        return pl.ds(pl.multiple_of(base, unit), width)

    def grad_fc2(h, dst):
        def part(i, _):
            t = lax.dot_general(act_ref[:, col(i * 768, 768, 768)], dm[:, col(h * LW, LW, LW)], TN, preferred_element_type=f32)
            dst[i] = t.astype(bf16).reshape(4, 192, LW)
            return 0
        lax.fori_loop(0, 4, part, 0)

    def fc2_back():
        def part(i, _):
            cs = col(i * 768, 768, 768)
            t = lax.dot_general(dm[:, 0:LW], wa[0, i].reshape(768, LW), NT, preferred_element_type=f32)
            t = t + lax.dot_general(dm[:, LW:768], wa[1, i].reshape(768, LW), NT, preferred_element_type=f32)
            t = (t * dact_ref[:, cs].astype(f32)).astype(bf16)
            df[:, cs] = t
            vsum[5:6, cs] = jnp.sum(t.astype(f32), axis=0, keepdims=True)
            return 0
        lax.fori_loop(0, 4, part, 0)

    def wunit(h, u):
        return wb[h, u].reshape(768, LW)
    def fc1_back():
        for h in range(2):
            wt = lambda r: jnp.concatenate([wunit(h, u)[r] for u in range(4)], axis=1)
            for n in range(2):
                rs = slice(n * 384, (n + 1) * 384)
                t = lax.dot_general(df[:, h * 1536:(h + 1) * 1536], wt(rs), NT, preferred_element_type=f32)
                dh[:, rs] = t if h == 0 else dh[:, rs] + t

    def grad_fc1(h, dst, base):
        def part(u, _):
            t = lax.dot_general(h2_ref[...], df[:, col(h * 1536 + u * LW, LW, LW)], TN, preferred_element_type=f32)
            dst[base + u] = t.astype(bf16).reshape(4, 4, 48, LW)
            return 0
        lax.fori_loop(0, 4, part, 0)

    def norm_back(src, gain_row, into, out_lo, base):
        gain = rows_ref[gain_row:gain_row + 1, 0:768]
        def body(r):
            n, rstd = stats(src[r, :].astype(f32))
            d = dh[r, :]
            vsum[base:base + 1, 0:768] += jnp.sum(d * n, axis=0, keepdims=True)
            vsum[base + 1:base + 2, 0:768] += jnp.sum(d, axis=0, keepdims=True)
            dn = d * gain
            t = rstd * (dn - jnp.mean(dn, axis=-1, keepdims=True) - n * jnp.mean(dn * n, axis=-1, keepdims=True))
            t = dx[r, :] + t
            into[r, :] = t
            if out_lo is not None: out_lo[r, :] = t.astype(bf16)
        blocks(body)

    def out_back():
        t = lax.dot_general(dm[:, 0:LW], wunit(0, 3), NT, preferred_element_type=f32)
        t = t + lax.dot_general(dm[:, LW:768], wunit(1, 3), NT, preferred_element_type=f32)
        df[:, 0:768] = t.astype(bf16)

    def load_p(i):
        return pltpu.make_async_copy(p_hbm.at[pl.ds(2 * i, 2)], pb.at[i % 2], psem.at[i % 2])

    def attn_back(lo, hi):
        low = lax.broadcasted_iota(jnp.int32, (1, 128), 1) < 64
        def pair(i, _):
            load_p(i).wait()
            pl.when(i + 1 < HEADS_PAIRS)(lambda: load_p(i + 1).start())
            def cols(ref, base):
                return ref[:, col(base + i * 128, 128, 128)]
            q, kk, v, do = cols(qkv_ref, 0), cols(qkv_ref, 768), cols(qkv_ref, 1536), cols(df, 0)
            r = []
            for t in range(2):
                keep = low if t == 0 else jnp.logical_not(low)
                pr = pb[i % 2, t]
                dp = lax.dot_general(jnp.where(keep, do, jnp.zeros_like(do)), v, NT, preferred_element_type=f32)
                p32 = pr.astype(f32)
                ds = (p32 * (dp - jnp.sum(dp * p32, axis=-1, keepdims=True))).astype(bf16)
                dv = lax.dot_general(pr, do, TN, preferred_element_type=f32)
                dq = jnp.dot(ds, kk, preferred_element_type=f32)
                dk = lax.dot_general(ds, q, TN, preferred_element_type=f32)
                r.append((dq, dk, dv))
            dqkv[:, col(i * 128, 128, 128)] = (0.125 * jnp.where(low, r[0][0], r[1][0])).astype(bf16)
            dqkv[:, col(768 + i * 128, 128, 128)] = (0.125 * jnp.where(low, r[0][1], r[1][1])).astype(bf16)
            dqkv[:, col(1536 + i * 128, 128, 128)] = jnp.where(low, r[0][2], r[1][2]).astype(bf16)
            return 0
        lax.fori_loop(lo, hi, pair, 0)

    def qkv_back():
        for h in range(2):
            wt = lambda r: jnp.concatenate([wunit(h, u)[r] for u in range(3)], axis=1)
            for n in range(2):
                rs = slice(n * 384, (n + 1) * 384)
                t = lax.dot_general(dqkv[:, h * 1152:(h + 1) * 1152], wt(rs), NT, preferred_element_type=f32)
                dh[:, rs] = t if h == 0 else dh[:, rs] + t

    def grad_qkv(h, dst):
        def part(u, _):
            t = lax.dot_general(a_ref[...], dqkv[:, col(h * 1152 + u * LW, LW, LW)], TN, preferred_element_type=f32)
            dst[u] = t.astype(bf16).reshape(4, 4, 48, LW)
            return 0
        lax.fori_loop(0, 3, part, 0)
    def grad_out(h, dst):
        t = lax.dot_general(o_ref[...], dm[:, col(h * LW, LW, LW)], TN, preferred_element_type=f32)
        dst[3] = t.astype(bf16).reshape(4, 4, 48, LW)

    def vec_cols():
        rt = jnp.concatenate([vsum[0:8, 0:768], jnp.zeros((120, 768), f32)], axis=0)
        srow = lax.broadcasted_iota(jnp.int32, (128, 768), 0)
        rt = jnp.where(srow < 5, rt, 0.0)
        v = rt.T
        r2 = jnp.concatenate([vsum[0:16, 0:512], jnp.zeros((112, 512), f32)], axis=0)
        srow2 = lax.broadcasted_iota(jnp.int32, (128, 512), 0)
        r2 = jnp.where((srow2 == 9) | (srow2 == 10), r2, 0.0).astype(bf16)
        v = v + lax.dot_general(m2_ref[...], r2, NT, preferred_element_type=f32)
        lane = (lax.broadcasted_iota(jnp.int32, (128, 768), 1) % 24) // 6
        parts = []
        for s in range(4):
            wrow = jnp.broadcast_to(vsum[5:6, 768 * s:768 * s + 768], (128, 768))
            wt = jnp.where(srow - 5 == lane, wrow, 0.0).astype(bf16)
            parts.append(lax.dot_general(m4_ref[...], wt, NT, preferred_element_type=f32))
        return (v + jnp.concatenate(parts, axis=0)).astype(bf16)

    def grad_dec(h, dst_store):
        t = lax.dot_general(e_ref[...], dz[:, col(h * 256, 256, 256)], TN, preferred_element_type=f32)
        dst_store(t.astype(bf16).reshape(4, 4, 48, 256), slice(0, 256))

    def acc8(v, cs): acc[8, :, :, :, cs] = v
    def stc8(v, cs): stc[0, :, :, :, cs] = v

    need("dm", "act")
    grad_fc2(o, sta2); st(2, 0)
    grad_fc2(c, acc2)
    vsum[4:5, 0:768] = jnp.sum(dm[...].astype(f32), axis=0, keepdims=True)
    need("fc2", "dact")
    fc2_back()
    st(2, 1)
    need("fc1")
    fc1_back()
    ld_c.start()
    load_p(0).start()
    need("h2")
    grad_fc1(o, sta, 0); st(1, 0)
    st(2, 2)
    grad_fc1(c, acc, 4)
    need("x2", "dx", "rows")
    norm_back(x2_ref, 2, dx, dm, 2)
    st(2, 3); st(1, 1)
    ld_c.wait()
    for kk in keys[1]: sends[kk, 8].wait_send(); del sends[kk, 8]
    need("o", "qkv")
    grad_out(o, sta); grad_out(c, acc)
    out_back()
    st(2, 4); st(1, 2)
    attn_back(0, 3)
    st(2, 5); st(1, 3)
    attn_back(3, 6)
    st(1, 4)
    need("a")
    grad_qkv(o, sta)
    st(0, 0)
    grad_qkv(c, acc)
    st(1, 5)
    qkv_back()
    need("tok", "vs", "e", "dz")
    vsum[9:11, 0:512] = vs[9:11, :]
    norm_back(tok, 0, dx, None, 0)
    dh[0:512 - ROWS, :] = jnp.zeros((512 - ROWS, 768), f32)
    tgs = [pltpu.make_async_copy(dx, tg_ref.at[0:ROWS], tsem.at[0]), pltpu.make_async_copy(dh.at[0:512 - ROWS], tg_ref.at[ROWS:512], tsem.at[1])]
    for t in tgs: t.start()
    st(0, 1)
    v = vec_cols().reshape(4, 4, 48, 128)
    zero = jnp.zeros_like(v)
    acc8(jnp.where(c == 0, v, zero), slice(256, 384)); stc8(jnp.where(c == 0, zero, v), slice(256, 384))
    grad_dec(o, stc8)
    st(3, 0)
    grad_dec(c, acc8)
    st(0, 2); st(3, 1); st(0, 3); st(3, 2); st(0, 4); st(3, 3); st(0, 5); st(3, 4); st(3, 5)

    blk = jnp.concatenate([acc[:, z, x].reshape(432, LW), acc2[z, x]], axis=0)
    fs[...] = jnp.dot(pt_ref[...], blk, preferred_element_type=f32).astype(bf16).reshape(8, SROWS, LW)
    me = 2 * y + c
    own = pltpu.make_async_copy(fs.at[me], f1.at[me], loc)
    own.start()
    lasts = []
    for i, (dy, dc, t) in enumerate(group):
        dst = 2 * ((y + dy) % 4) + (c + dc) % 2
        cp = pltpu.make_async_remote_copy(fs.at[dst], f1.at[me], ss1.at[i], rs1.at[i], device_id=t, device_id_type=MESH)
        cp.start()
        src = 2 * ((y + 4 - dy) % 4) + (c + dc) % 2
        rc = pltpu.make_async_remote_copy(fs.at[me], f1.at[src], ss1.at[i], rs1.at[i], device_id=t, device_id_type=MESH)
        lasts.append((cp, rc))
    own.wait()
    for cp, rc in lasts: rc.wait_recv()
    for h in range(2):
        t = f1[h].astype(f32)
        for yy in range(1, 4): t = t + f1[2 * yy + h].astype(f32)
        fo[h] = t
    for h in range(2):
        for u in range(3):
            oq_ref[:, h * 1152 + u * LW:h * 1152 + (u + 1) * LW] = fo[h, 6 * u:6 * u + 6, :]
        oo_ref[:, h * LW:(h + 1) * LW] = fo[h, 18:24, :]
        for u in range(4):
            of1_ref[:, h * 1536 + u * LW:h * 1536 + (u + 1) * LW] = fo[h, 24 + 6 * u:30 + 6 * u, :]
        of2_ref[:, h * LW:(h + 1) * LW] = fo[h, 48:72, :]
        od_ref[:, h * 256:(h + 1) * 256] = fo[h, 72:78, 0:256]
    vt[0:6, :] = fo[0, 72:78, 256:384]
    vrows = vt[...].T
    for i, r in enumerate((v0_ref, v1_ref, v2_ref, v3_ref, v4_ref)):
        r[...] = vrows[i:i + 1, 0:6]
    for q in range(4):
        vf_ref[:, 6 * q:6 * q + 6] = vrows[5 + q:6 + q, 0:6]
    vd_ref[...] = vrows[9:10, 0:4]
    vm_ref[...] = vrows[10:11, 0:4]
    finish_cells()
    for t in tgs: t.wait()
    for cp, rc in lasts: cp.wait_send()
    for cp in sends.values(): cp.wait_send()


def k2_call(*args):
    nk = sum(len(c) for c in ag_chunks())
    S = jax.ShapeDtypeStruct
    vm = pl.BlockSpec(memory_space=pltpu.VMEM)
    anyspec = pl.BlockSpec(memory_space=pl.ANY)
    V, DMA = pltpu.VMEM, pltpu.SemaphoreType.DMA
    outs = (S((512, 768), f32), S((33, 64, 512), bf16), S((6, 2304), f32), S((6, 768), f32), S((6, 3072), f32), S((24, 768), f32),
            S((6, 512), f32)) + (S((1, 6), f32),) * 5 + (S((1, 24), f32), S((1, 4), f32), S((1, 4), f32))
    return pl.pallas_call(
        k2_kernel,
        out_shape=outs,
        in_specs=[anyspec] * 18 + [vm] * 3,
        out_specs=[anyspec] * 2 + [vm] * 13,
        scratch_shapes=[
            V((8, 3072), f32), V((ROWS, 768), bf16), V((ROWS, 2304), bf16), V((ROWS, 768), bf16), V((ROWS, 768), f32),
            V((ROWS, 768), bf16), V((ROWS, 3072), bf16), V((ROWS, 3072), bf16), V((ROWS, 768), bf16), V((ROWS, 512), bf16),
            V((ROWS, 768), f32), V((ROWS, 768), bf16), V((16, 512), f32), V((ROWS, 768), bf16),
            V((2, 4, 4, 192, LW), bf16), V((2, 4, 4, 4, 48, LW), bf16),
            V((4, 4, 4, 48, LW), bf16), V((4, 4, 192, LW), bf16), V((1, 4, 4, 48, LW), bf16),
            V((9, 4, 4, 48, LW), bf16), V((4, 4, 192, LW), bf16),
            V((9, 4, 4, 48, LW), bf16), V((4, 4, 192, LW), bf16),
            V((3, 9, 4, 48, LW), bf16), V((3, 4, 192, LW), bf16),
            V((3, 9, 48, LW), bf16), V((3, 192, LW), bf16),
            V((ROWS, 768), f32), V((ROWS, 3072), bf16), V((ROWS, 2304), bf16), V((16, 3072), f32), V((2, 2, ROWS, ROWS), bf16),
            V((8, SROWS, LW), bf16), V((8, SROWS, LW), bf16), V((2, SROWS, LW), f32), V((64, 512), bf16), V((128, 128), f32),
            DMA((nk, 9)), DMA((nk, 9)), DMA((7,)), DMA((7,)), DMA(()), DMA((1,)), DMA((2,)), DMA((2,)), DMA((16,)),
            DMA((32,)), DMA((32,)), DMA((3,)),
        ],
        compiler_params=pltpu.CompilerParams(collective_id=1, has_side_effects=True, vmem_limit_bytes=60 * 2**20),
        cost_estimate=pl.CostEstimate(flops=12 * 10**9, bytes_accessed=5 * 10**7, transcendentals=0),
        name="backward",
    )(*args, jnp.asarray(perm_matrix().T, bf16), jnp.asarray(cell_spread(), bf16), jnp.asarray(fc1_bias_spread(), bf16))


def k3_kernel(inv, arr, tg, *refs):
    n = len(refs) - 3
    small, (grid, tg_out, *outs), (gv, tv, sem) = refs[:13], refs[13:n], refs[n:]
    ins = [pltpu.make_async_copy(tg, tv, sem.at[0])]
    ins += [pltpu.make_async_copy(arr.at[inv[0, r]], gv.at[r], sem.at[1 + r]) for r in range(32)]
    for cp in ins: cp.start()
    for a, b in zip(small, outs): b[...] = a[...]
    back = [pltpu.make_async_copy(tv, tg_out, sem.at[33])]
    back += [pltpu.make_async_copy(gv.at[pl.ds(8 * i, 8)], grid.at[pl.ds(8 * i, 8)], sem.at[34 + i]) for i in range(4)]
    ins[0].wait()
    back[0].start()
    for i in range(4):
        for r in range(8): ins[1 + 8 * i + r].wait()
        back[1 + i].start()
    for cp in back: cp.wait()


def k3_call(inv, arr, tg, *small):
    S = jax.ShapeDtypeStruct
    vm = pl.BlockSpec(memory_space=pltpu.VMEM)
    anyspec = pl.BlockSpec(memory_space=pl.ANY)
    return pl.pallas_call(
        k3_kernel,
        out_shape=(S((32, 64, 512), bf16), S((512, 768), f32)) + tuple(S(t.shape, t.dtype) for t in small),
        in_specs=[pl.BlockSpec(memory_space=pltpu.SMEM), anyspec, anyspec] + [vm] * 13,
        out_specs=[anyspec, anyspec] + [vm] * 13,
        scratch_shapes=[pltpu.VMEM((32, 64, 512), bf16), pltpu.VMEM((512, 768), f32), pltpu.SemaphoreType.DMA((38,))],
        name="results",
    )(inv, arr, tg, *small)


def body(tokens, chip_lengths, chip_ids, positions, ln1_gain, ln1_bias, qkv_weight, out_weight, ln2_gain, ln2_bias, fc1_weight,
         fc1_bias, fc2_weight, fc2_bias, dec_weight, dec_bias, mask_token, grid_cotangent):
    row = lambda v: v.reshape(1, -1)
    *saved, inv = k1_call(chip_ids, chip_lengths, row(positions), tokens, row(ln1_gain), row(ln1_bias), qkv_weight, out_weight,
                          row(ln2_gain), row(ln2_bias), fc1_weight, row(fc1_bias), fc2_weight, row(fc2_bias), dec_weight,
                          row(dec_bias), row(mask_token), grid_cotangent)
    tg, arrived, *small = k2_call(*saved, tokens)
    grid, tg, dq, do, df1, df2, dd, *v = k3_call(inv, arrived, tg, *small)
    v = [t.reshape(-1) for t in v]
    return (grid, tg, v[0], v[1], dq, do, v[2], v[3], df1, v[5], df2, v[4], dd, v[6], v[7])


def solution(mesh):
    both = ("dp", "fsdp")
    r1, r2, grid = P(both), P(both, None), P("dp", "fsdp", None)
    weights = (r1, r1, r2, r2, r1, r1, r2, r1, r2, r1, r2, r1, r1)
    return jax.shard_map(body, mesh=mesh, in_specs=(r2, r1, r1, r1) + weights + (grid,), out_specs=(grid, r2) + weights,
                         check_vma=False)
```

```python
import functools
import numpy as np
import jax, jax.numpy as jnp
from jax import lax
from jax.experimental import pallas as pl
from jax.experimental.pallas import tpu as pltpu
from jax.sharding import PartitionSpec as P

MESH = pl.DeviceIdType.MESH
LW = 384
SROWS = 96
YROWS = 64

def coords():
    dp = lax.axis_index("dp"); fs = lax.axis_index("fsdp")
    z = dp // 2
    x = (dp % 2) * 2 + fs // 8
    y = (fs % 8) // 2
    c = fs % 2
    return z, x, y, c

def dev(z, x, y, c):
    return (z * 2 + x // 2, (x % 2) * 8 + y * 2 + c)

UNIT_ROWS = (32, 38, 44, 50, 0, 6, 12, 18, 56)
FC2_ROWS = 64


def perm_matrix():
    m = np.zeros((432, 512), np.float32)
    for u, base in enumerate(UNIT_ROWS):
        for d in range(8):
            for j in range(6):
                m[48 * u + 6 * d + j, d * 64 + base + j] = 1
    return m


def spread_matrix(units, first):
    m = perm_matrix().reshape(9, 48, 8, 64)[list(units), :, :, first:first + 32]
    return m.reshape(48 * len(units), 256).T


ALL = slice(None)


def ring_places(z, x, y, c):
    out = {}
    for name, v in (("z", z), ("x", x), ("y", y)):
        at = {0: v, 1: (v + 1) % 4, -1: (v + 3) % 4, 2: (v + 2) % 4}
        to = {k: dev(*(at[k] if n == name else w for n, w in (("z", z), ("x", x), ("y", y))), c) for k in (1, -1)}
        out[name] = (at, to)
    return out


ROWS = 336
HEADS_PAIRS = 6
D = 768
NT = (((1,), (1,)), ((), ()))
TN = (((0,), (0,)), ((), ()))
f32, bf16 = jnp.float32, jnp.bfloat16


def cell_spread():
    m = np.zeros((768, 512), np.float32)
    for d in range(128):
        for j in range(4):
            m[6 * d + j, 4 * d + j] = 1
    return m


def fc1_bias_spread():
    m = np.zeros((192, 768), np.float32)
    n = np.arange(768)
    m[6 * (n // 24) + n % 6, n] = 1
    return m


def peers(f):
    return [(r, (f + r) % 16) for r in range(1, 16)]


def greet(bar, devices):
    for t in devices:
        pl.semaphore_signal(bar, inc=1, device_id=t, device_id_type=MESH)


def stats(v):
    mean = jnp.mean(v, axis=-1, keepdims=True)
    center = v - mean
    rstd = lax.rsqrt(jnp.mean(center * center, axis=-1, keepdims=True) + 1e-6)
    return center * rstd, rstd


def gelu_pair(f):
    cdf = 0.5 * (1.0 + lax.erf(f * 0.7071067811865476))
    pdf = 0.3989422804014327 * jnp.exp(-0.5 * f * f)
    return f * cdf, cdf + f * pdf


def k1_kernel(ids, lens, pos, tok, l1g, l1b, qkv_s, out_s, l2g, l2b, fc1_s, fc1b, fc2_s, fc2b, dec_s, decb, maskt, cot_hbm,
              p1_ref, p2_ref, m2_ref, m4_ref,
              g_hbm, g2_hbm, rows_hbm, a_hbm, qkv_hbm, p_hbm, o_hbm, x2_hbm, h2_hbm, act_hbm, dact_hbm, e_hbm, cells_hbm,
              dz_hbm, dx_hbm, dm_hbm, vs_hbm, inv_hbm,
              g_ref, g2_ref, rows_ref, a_ref, qkv_ref, p_out, o_ref, x2_ref, h2_ref, act_ref, dact_ref, e_ref, cells_ref,
              dz, dx, dm, vs, inv,
              sp, s_ref, s1, s2, z_ref, vrow, tag, tags, idv, idm, cot, cotsend, dc, hits,
              ss1, rs1, loc, ssem, rsem, wsem, osem, tss, tsr, bss, bsr, mss, msr, lsem):
    z, x, y, c = coords()
    dp, f = lax.axis_index("dp"), lax.axis_index("fsdp")
    o = 1 - c
    bar = pltpu.get_barrier_semaphore()
    rings = ring_places(z, x, y, c)
    targets = [rings[a][1][d] for a in "zx" for d in (1, -1)]
    group = []
    for dy in range(4):
        for dc_ in range(2):
            if dy or dc_:
                group.append((dy, dc_, dev(z, x, (y + dy) % 4, (c + dc_) % 2)))
    greeted = targets + [(dp, g) for _, g in peers(f)]
    greet(bar, greeted)
    ld_cot = pltpu.make_async_copy(cot_hbm, cot, lsem.at[0])
    ld_cot.start()

    sp[...] = jnp.zeros_like(sp)
    for h in range(2):
        for u in range(3):
            for b in range(3):
                first = 768 * b + 128 * (3 * h + u)
                sp[h, 32 + 6 * u:38 + 6 * u, 128 * b:128 * b + 128] = qkv_s[:, first:first + 128].astype(f32)
        sp[h, 50:56, :] = out_s[:, h * LW:(h + 1) * LW].astype(f32)
        for u in range(4):
            sp[h, 6 * u:6 * u + 6, :] = fc1_s[:, h * 1536 + u * LW:h * 1536 + (u + 1) * LW].astype(f32)
        sp[h, 64:88, :] = fc2_s[:, h * LW:(h + 1) * LW].astype(f32)
        sp[h, 56:62, 0:256] = dec_s[:, h * 256:(h + 1) * 256].astype(f32)
    vrow[...] = jnp.zeros_like(vrow)
    for i, r in enumerate((l1g, l1b, l2g, l2b, fc2b)):
        vrow[i:i + 1, 0:6] = r[...].astype(f32)
    for q in range(4):
        vrow[5 + q:6 + q, 0:6] = fc1b[:, 6 * q:6 * q + 6].astype(f32)
    vrow[9:10, 0:4] = decb[...].astype(f32)
    vrow[10:11, 0:4] = maskt[...].astype(f32)
    sp[0, 56:62, 256:384] = vrow[...].T[0:6]
    s_ref[...] = sp[...].astype(bf16)
    first_small = lens[0] < lens[1]
    trow = lax.broadcasted_iota(jnp.int32, (8, 128), 0)
    tag[...] = jnp.where(trow == 0, jnp.where(first_small, ids[1], ids[0]), jnp.where(first_small, ids[0], ids[1]))
    pl.semaphore_wait(bar, len(greeted))

    me = 2 * y + c
    sib = dev(z, x, y, o)
    mate = pltpu.make_async_remote_copy(s_ref.at[o, YROWS:SROWS], s2, ss1.at[2, 0], rs1.at[2, 0], device_id=sib, device_id_type=MESH)
    mate.start()
    firsts = []
    for j, rows in enumerate((slice(32, 64), slice(0, 32))):
        own = pltpu.make_async_copy(s_ref.at[c, rows], s1.at[me, rows], loc.at[j])
        own.start()
        got = []
        for i, (dy, dc_, t) in enumerate(group):
            cp = pltpu.make_async_remote_copy(s_ref.at[(c + dc_) % 2, rows], s1.at[me, rows], ss1.at[j, i], rs1.at[j, i], device_id=t, device_id_type=MESH)
            cp.start()
            src = 2 * ((y + 4 - dy) % 4) + (c + dc_) % 2
            rc = pltpu.make_async_remote_copy(s_ref.at[c, rows], s1.at[src, rows], ss1.at[j, i], rs1.at[j, i], device_id=t, device_id_type=MESH)
            got.append((cp, rc))
        firsts.append((own, got))
    def shards(j):
        own, got = firsts[j]
        own.wait()
        for _, rc in got: rc.wait_recv()
    tagged = []
    tags[f] = tag[...]
    for r, g in peers(f):
        cp = pltpu.make_async_remote_copy(tag, tags.at[f], tss.at[r], tsr.at[r], device_id=(dp, g), device_id_type=MESH)
        cp.start(); tagged.append(cp)
    def sort_cotangents():
        for r, g in peers(f):
            src = (f + 16 - r) % 16
            pltpu.make_async_remote_copy(tag, tags.at[src], tss.at[r], tsr.at[r], device_id=(dp, g), device_id_type=MESH).wait_recv()
        for s in range(16):
            idv[s:s + 1, :] = tags[s, 0:1, :]
            idv[16 + s:17 + s, :] = tags[s, 1:2, :]
        ld_ids = pltpu.make_async_copy(idv, idm, lsem.at[1])
        ld_ids.start()
        srow = lax.broadcasted_iota(jnp.int32, (32, 128), 0)
        hit = idv[...] == lax.broadcasted_iota(jnp.int32, (32, 128), 1)
        place_of = jnp.where((srow >= 16) & (f >= 4), 32, srow)
        inv[...] = jnp.broadcast_to(jnp.sum(jnp.where(hit, place_of, 0), axis=0, keepdims=True), (8, 128))
        ld_ids.wait()
        ld_cot.wait()
        for s in range(32):
            cotsend[s] = cot[idm[s, 0]]

    few = f < 4
    def to_peer(i, g):
        big = pltpu.make_async_remote_copy(cotsend.at[g], dc.at[f], bss.at[i], bsr.at[i], device_id=(dp, g), device_id_type=MESH)
        return big
    def small_to_peer(i, g):
        return pltpu.make_async_remote_copy(cotsend.at[16 + g], dc.at[16 + f % 4], mss.at[i], msr.at[f % 4], device_id=(dp, g), device_id_type=MESH)
    own_dc = pltpu.make_async_copy(cotsend.at[f], dc.at[f], lsem.at[2])
    own_small = pltpu.make_async_copy(cotsend.at[16 + f], dc.at[16 + f % 4], lsem.at[3])
    def send_cotangents():
        own_dc.start()
        for r, g in peers(f):
            to_peer(r, g).start()
        @pl.when(few)
        def _():
            own_small.start()
            for r, g in peers(f):
                small_to_peer(r, g).start()
    def get_cotangents():
        own_dc.wait()
        for r, g in peers(f):
            src = (f + 16 - r) % 16
            pltpu.make_async_remote_copy(cotsend.at[g], dc.at[src], bss.at[r], bsr.at[r], device_id=(dp, g), device_id_type=MESH).wait_recv()
        for s in range(4):
            @pl.when(f != s)
            def _():
                pltpu.make_async_remote_copy(cotsend.at[16], dc.at[16 + s], mss.at[0], msr.at[s], device_id=(dp, s), device_id_type=MESH).wait_recv()
        @pl.when(few)
        def _():
            own_small.wait()
    def finish_cotangents():
        for r, g in peers(f):
            to_peer(r, g).wait_send()
        @pl.when(few)
        def _():
            for r, g in peers(f):
                small_to_peer(r, g).wait_send()

    def relay(perm, rows, lo, hi):
        flat = s1[:, rows].reshape(256, LW)
        r = jnp.dot(perm[lo:hi, :], flat, preferred_element_type=f32)
        return r.astype(bf16)

    def place(p):
        if p == 0: g_ref[c, 0:4, z, x] = relay(p2_ref, slice(32, 64), 0, 192).reshape(4, 48, LW)
        if p == 1: g_ref[c, 4:8, z, x] = relay(p1_ref, slice(0, 32), 0, 192).reshape(4, 48, LW)
        if p == 2:
            mate.wait_recv()
            both = [s_ref[c, YROWS:SROWS].astype(f32)[0:24], s2[...].astype(f32)[0:24]]
            both = [jnp.where(c == k, both[0], both[1]) for k in range(2)]
            g2_ref[c, z, x, y] = jnp.concatenate(both, axis=0).astype(bf16)
        if p == 3: g_ref[c, 8, z, x] = relay(p2_ref, slice(32, 64), 192, 240)

    sends = []
    def mk(k, i, v, to):
        return pltpu.make_async_remote_copy(v, v, ssem.at[k, i], rsem.at[k, i], device_id=to, device_id_type=MESH)
    def send(k, i, v, to):
        cp = mk(k, i, v, to); cp.start(); sends.append(cp)
    def recv(k, i, v):
        mk(k, i, v, sib).wait_recv()

    def steps(k, axes, view, parts):
        last = len(axes) - 1
        def opposite(l):
            at, _ = rings[axes[l]]
            _, fa, fb = parts[l]
            recv(k, 4 * l + 2, view(l, at[2], fa, c))
            if fb is not None: recv(k, 4 * l + 3, view(l, at[2], fb, c))
        def first(l):
            at, to = rings[axes[l]]
            full = parts[l][0]
            if l: opposite(l - 1)
            for i, d in enumerate((1, -1)): send(k, 4 * l + i, view(l, at[0], full, c), to[d])
            if l == last: send(k, 12, view(l, at[0], full, c), sib)
        def second(l):
            at, to = rings[axes[l]]
            full, fa, fb = parts[l]
            recv(k, 4 * l, view(l, at[-1], full, c))
            send(k, 4 * l + 2, view(l, at[-1], fa, c), to[1])
            if l == last: send(k, 13, view(l, at[-1], full, c), sib)
            recv(k, 4 * l + 1, view(l, at[1], full, c))
            if fb is not None: send(k, 4 * l + 3, view(l, at[1], fb, c), to[-1])
            if l == last: send(k, 14, view(l, at[1], full, c), sib)
        def third():
            at, _ = rings[axes[last]]
            opposite(last)
            send(k, 15, view(last, at[2], parts[last][0], c), sib)
        def fourth():
            at, _ = rings[axes[last]]
            for i, d in enumerate((0, -1, 1, 2)): recv(k, 12 + i, view(last, at[d], parts[last][0], o))
        out = []
        for l in range(last + 1):
            out += [functools.partial(first, l), functools.partial(second, l)]
        return out + [third, fourth]

    def unit_chunk(k, axes, *parts):
        def view(l, at, part, h):
            u0, u1, l0, l1 = part
            zs, xs = [(z, at), (at, ALL)][l] if axes == "xz" else [(at, x), (ALL, at)][l]
            return g_ref.at[h, u0:u1, zs, xs, :, l0:l1]
        return steps(k, axes, view, [parts, parts])
    def fc2_chunk(k):
        def view(l, at, part, h):
            a, b = part
            if l == 0: return g2_ref.at[h, z, at, y, a:b]
            if l == 1: return g2_ref.at[h, at, a:b, y]
            return g2_ref.at[h, a:b, :, at]
        ring = ((0, 4), (0, 2), (2, 4))
        return steps(k, "xzy", view, [((0, 48), (0, 32), (32, 48)), ring, ring])

    outs = []
    def to_hbm(p):
        if p == 2: cp = pltpu.make_async_copy(g2_ref, g2_hbm, wsem.at[p])
        else:
            u0, u1 = ((0, 4), (4, 8), None, (8, 9))[p]
            cp = pltpu.make_async_copy(g_ref.at[:, u0:u1], g_hbm.at[:, u0:u1], wsem.at[p])
        cp.start(); outs.append(cp)

    def blocks(body, n=7):
        def step(i, _):
            body(pl.ds(pl.multiple_of(i * 48, 48), 48)); return 0
        lax.fori_loop(0, n, step, 0)

    def w(h, u):
        return g_ref[h, u].reshape(768, LW)

    def rows_of():
        v = jnp.concatenate([g_ref[0, 8, zz, xx, :, 256:384] for zz in range(4) for xx in range(4)], axis=0)
        vt = v.astype(f32).T
        rows_ref[0:5, 0:768] = vt[0:5]
        md = lax.dot_general(v, m2_ref[...], TN, preferred_element_type=f32)
        rows_ref[6:8, 0:512] = md[9:11]
        lane = (lax.broadcasted_iota(jnp.int32, (8, 768), 1) % 24) // 6
        row = lax.broadcasted_iota(jnp.int32, (8, 768), 0)
        for s in range(4):
            q = lax.dot_general(v[192 * s:192 * s + 192], m4_ref[...], TN, preferred_element_type=f32)
            q = jnp.where(row == lane, q[5:13], 0.0)
            rows_ref[5:6, 768 * s:768 * s + 768] = jnp.sum(q, axis=0, keepdims=True)

    def ln1():
        def body(r):
            n, _ = stats(tok[r, :].astype(f32))
            a_ref[r, :] = (n * rows_ref[0:1, 0:768] + rows_ref[1:2, 0:768]).astype(bf16)
        blocks(body)

    def qkv():
        for h in range(2):
            wt = jnp.concatenate([w(h, u) for u in range(3)], axis=1)
            qkv_ref[:, h * 1152:(h + 1) * 1152] = jnp.dot(a_ref[...], wt, preferred_element_type=f32).astype(bf16)

    ends0 = lens[0] + 2
    ends1 = ends0 + lens[1] + 2
    def seg(shape, axis):
        r = lax.broadcasted_iota(jnp.int32, shape, axis)
        return (r >= ends0).astype(jnp.int32) + (r >= ends1).astype(jnp.int32)

    def attention(lo, hi):
        low = lax.broadcasted_iota(jnp.int32, (1, 128), 1) < 64
        same = seg((ROWS, 1), 0) == seg((1, ROWS), 1)
        bias = jnp.where(same, 0.0, -1e30)
        def pair(i, _):
            q, k, v = (qkv_ref[:, pl.ds(pl.multiple_of(LW * i + 128 * b, 128), 128)] for b in range(3))
            outs_ = []
            for t in range(2):
                keep = low if t == 0 else jnp.logical_not(low)
                s = lax.dot_general(jnp.where(keep, q, jnp.zeros_like(q)), k, NT, preferred_element_type=f32)
                s = jnp.where(same, s * 0.125, -1e30)
                m = jnp.max(s, axis=-1, keepdims=True)
                ex = jnp.exp(s - m)
                pr = (ex / jnp.sum(ex, axis=-1, keepdims=True)).astype(bf16)
                p_out[2 * i + t] = pr
                outs_.append(jnp.dot(pr, v, preferred_element_type=f32))
            o_ref[:, pl.ds(pl.multiple_of(i * 128, 128), 128)] = jnp.where(low, outs_[0], outs_[1]).astype(bf16)
            return 0
        lax.fori_loop(lo, hi, pair, 0)

    def out_proj():
        for h in range(2):
            cs = slice(h * LW, (h + 1) * LW)
            x2_ref[:, cs] = tok[0:ROWS, cs].astype(f32) + jnp.dot(o_ref[...], w(h, 3), preferred_element_type=f32)
        def body(r):
            n, _ = stats(x2_ref[r, :])
            h2_ref[r, :] = (n * rows_ref[2:3, 0:768] + rows_ref[3:4, 0:768]).astype(bf16)
        blocks(body)

    def fc1(first):
        for h in range(2):
            def unit(u, _):
                cs = pl.ds(pl.multiple_of(h * 1536 + u * LW, LW), LW)
                f = jnp.dot(h2_ref[...], w(h, 4 + u), preferred_element_type=f32) + rows_ref[5:6, cs]
                g, dg = gelu_pair(f)
                act_ref[:, cs] = g.astype(bf16)
                dact_ref[:, cs] = dg.astype(bf16)
                return 0
            lax.fori_loop(first, first + 2, unit, 0)

    def fc2():
        for h in range(2):
            cs = slice(h * LW, (h + 1) * LW)
            t = jnp.dot(act_ref[...], g2_ref[h].reshape(3072, LW), preferred_element_type=f32)
            e_ref[:, cs] = (x2_ref[:, cs] + t + rows_ref[4:5, cs]).astype(bf16)

    def dec():
        for h in range(2):
            cs = slice(h * 256, (h + 1) * 256)
            t = jnp.dot(e_ref[...], g_ref[h, 8, :, :, :, 0:256].reshape(768, 256), preferred_element_type=f32)
            z_ref[:, cs] = (t + rows_ref[6:7, cs]).astype(bf16)
        z_ref[:, 512:640] = jnp.ones((ROWS, 128), bf16)
        def block(i, _):
            fill = hits[pl.ds(pl.multiple_of(i * 256, 256), 256), :]
            r = jnp.dot(fill, z_ref[...], preferred_element_type=f32)
            empty = 1.0 - r[:, 512:640]
            for t in range(4):
                cs = slice(128 * t, 128 * t + 128)
                val = r[:, cs] + empty * rows_ref[7:8, cs]
                cells_ref[pl.ds(4 * i, 4), :, cs] = val.astype(bf16).reshape(4, 64, 128)
            return 0
        lax.fori_loop(0, 5, block, 0)

    def fills():
        p_ = pos[0:1, 0:ROWS]
        large = seg((1, ROWS), 1) == jnp.where(first_small, 1, 0)
        target = jnp.where(p_ >= 0, jnp.where(large, p_, 1024 + p_), -1)
        def block(i, _):
            cell = i * 256 + lax.broadcasted_iota(jnp.int32, (256, 1), 0)
            hits[pl.ds(pl.multiple_of(i * 256, 256), 256), :] = (cell == target).astype(f32).astype(bf16)
            return 0
        lax.fori_loop(0, 5, block, 0)

    def cell_grads():
        get_cotangents()
        d = dc[...].reshape(1280, 512)
        dz[...] = lax.dot_general(hits[...], d, TN, preferred_element_type=f32).astype(bf16)
        covered = lax.dot_general(jnp.ones((16, ROWS), bf16), hits[...], NT, preferred_element_type=f32)
        vs[10:11, :] = jnp.dot((1.0 - covered).astype(bf16), d, preferred_element_type=f32)[0:1]
        vs[9:10, :] = jnp.sum(dz[...].astype(f32), axis=0, keepdims=True)
        for n in range(2):
            rs = slice(n * 384, (n + 1) * 384)
            wt = [g_ref[h, 8, :, :, :, 0:256].reshape(768, 256)[rs] for h in range(2)]
            t = lax.dot_general(dz[:, 0:256], wt[0], NT, preferred_element_type=f32)
            t = t + lax.dot_general(dz[:, 256:512], wt[1], NT, preferred_element_type=f32)
            dx[:, rs] = t
            dm[:, rs] = t.astype(bf16)

    kept = dict(rows=(rows_ref, rows_hbm), a=(a_ref, a_hbm), qkv=(qkv_ref, qkv_hbm), p=(p_out, p_hbm), o=(o_ref, o_hbm),
                x2=(x2_ref, x2_hbm), h2=(h2_ref, h2_hbm), act=(act_ref, act_hbm), dact=(dact_ref, dact_hbm), e=(e_ref, e_hbm),
                cells=(cells_ref, cells_hbm), dz=(dz, dz_hbm), dx=(dx, dx_hbm), dm=(dm, dm_hbm), vs=(vs, vs_hbm), inv=(inv, inv_hbm))
    def keep(*names):
        for n in names:
            cp = pltpu.make_async_copy(*kept[n], osem.at[list(kept).index(n)])
            cp.start(); outs.append(cp)

    vs[...] = jnp.zeros_like(vs)
    rows_ref[...] = jnp.zeros_like(rows_ref)
    half = lambda u: ((u, u + 2, 0, LW), (u, u + 1, 0, LW), (u + 1, u + 2, 0, LW))
    pieces = {
        3: [unit_chunk(0, "xz", (8, 9, 0, LW), (8, 9, 0, 256), (8, 9, 256, LW))],
        2: [fc2_chunk(1)],
        0: [unit_chunk(2, "xz", *half(0)), unit_chunk(3, "zx", *half(2))],
        "1a": [unit_chunk(4, "xz", *half(4))],
        "1b": [unit_chunk(5, "zx", *half(6))],
    }
    def go(step, *names):
        for p in names:
            for ch in pieces[p]: ch[step]()
    place(2); go(0, 2)
    shards(0)
    place(3); place(0); go(0, 0, 3)
    go(1, 2, 0, 3)
    shards(1)
    place(1); go(0, "1a", "1b")
    go(2, 0, 3, 2)
    sort_cotangents(); keep("inv")
    go(1, "1a", "1b")
    go(3, 2, 0, 3)
    go(2, "1a", "1b")
    go(4, 2)
    send_cotangents()
    fills()
    go(4, 0, 3)
    go(5, 3); to_hbm(3)
    rows_of(); ln1(); keep("rows", "a")
    go(5, 0); to_hbm(0)
    qkv(); keep("qkv")
    go(3, "1a", "1b")
    go(5, 2)
    attention(0, 3)
    go(4, "1a", "1b")
    attention(3, 6)
    keep("p")
    go(6, 2)
    out_proj(); keep("o", "x2", "h2")
    cell_grads(); keep("dz", "dx", "dm", "vs")
    go(5, "1a"); fc1(0)
    go(5, "1b"); to_hbm(1)
    fc1(2); keep("act", "dact")
    go(7, 2); to_hbm(2)
    fc2(); keep("e")
    dec(); keep("cells")
    for _, got in firsts:
        for cp, _ in got: cp.wait_send()
    for cp in sends: cp.wait_send()
    mate.wait_send()
    for cp in tagged: cp.wait_send()
    finish_cotangents()
    for cp in outs: cp.wait()


def k1_call(*args):
    S = jax.ShapeDtypeStruct
    vm, smem = pl.BlockSpec(memory_space=pltpu.VMEM), pl.BlockSpec(memory_space=pltpu.SMEM)
    anyspec = pl.BlockSpec(memory_space=pl.ANY)
    V, DMA = pltpu.VMEM, pltpu.SemaphoreType.DMA
    outs = (
        S((2, 9, 4, 4, 48, LW), bf16), S((2, 4, 4, 4, 48, LW), bf16), S((8, 3072), f32), S((ROWS, 768), bf16),
        S((ROWS, 2304), bf16), S((12, ROWS, ROWS), bf16), S((ROWS, 768), bf16), S((ROWS, 768), f32),
        S((ROWS, 768), bf16), S((ROWS, 3072), bf16), S((ROWS, 3072), bf16), S((ROWS, 768), bf16), S((20, 64, 512), bf16),
        S((ROWS, 512), bf16), S((ROWS, 768), f32), S((ROWS, 768), bf16), S((16, 512), f32), S((8, 128), jnp.int32),
    )
    return pl.pallas_call(
        k1_kernel,
        out_shape=outs,
        in_specs=[smem, smem] + [vm] * 15 + [anyspec] + [vm] * 4,
        out_specs=[anyspec] * 18,
        scratch_shapes=[V(t.shape, t.dtype) for t in outs] + [
            V((2, SROWS, LW), f32), V((2, SROWS, LW), bf16), V((8, YROWS, LW), bf16), V((SROWS - YROWS, LW), bf16), V((ROWS, 640), bf16), V((128, 128), f32),
            V((8, 128), jnp.int32), V((16, 8, 128), jnp.int32), V((32, 128), jnp.int32), pltpu.SMEM((32, 128), jnp.int32),
            V((32, 64, 512), bf16), V((32, 64, 512), bf16), V((20, 64, 512), bf16), V((1280, ROWS), bf16),
            DMA((3, 7)), DMA((3, 7)), DMA((2,)), DMA((6, 16)), DMA((6, 16)), DMA((4,)), DMA((16,)), DMA((16,)), DMA((16,)),
            DMA((16,)), DMA((16,)), DMA((16,)), DMA((4,)), DMA((4,)),
        ],
        compiler_params=pltpu.CompilerParams(collective_id=0, has_side_effects=True, vmem_limit_bytes=60 * 2**20),
        cost_estimate=pl.CostEstimate(flops=6 * 10**9, bytes_accessed=5 * 10**7, transcendentals=0),
        name="forward",
    )(*args, jnp.asarray(spread_matrix((4, 5, 6, 7), 0).T, bf16), jnp.asarray(spread_matrix((0, 1, 2, 3, 8), 32).T, bf16),
      jnp.asarray(cell_spread(), bf16), jnp.asarray(fc1_bias_spread(), bf16))


def k2_kernel(g_hbm, g2_hbm, rows_hbm, a_hbm, qkv_hbm, p_hbm, o_hbm, x2_hbm, h2_hbm, act_hbm, dact_hbm, e_hbm, cells_hbm,
              dz_hbm, dx_hbm, dm_hbm, vs_hbm, tok_hbm, pt1_ref, pt2_ref, m2_ref, m4_ref,
              tg_ref, arr, oq_ref, oo_ref, of1_ref, of2_ref, od_ref, v0_ref, v1_ref, v2_ref, v3_ref, v4_ref, vf_ref, vd_ref, vm_ref,
              rows_ref, a_ref, qkv_ref, o_ref, x2_ref, h2_ref, act_ref, dact_ref, e_ref, dz, dx, dm, vs, tok,
              wa, wb, sta, sta2, stc, sg, sg2, acc, acc2, xa, xa2, xb, xc, xd,
              dh, df, dqkv, vsum, pb, fs, f1, fo, fs2, f2, zb, vt, vout, vin,
              ssem, rsem, ss1, rs1, loc, wsem, psem, tsem, isem, css, csr, csl, vss, vrs):
    z, x, y, c = coords()
    dp, f = lax.axis_index("dp"), lax.axis_index("fsdp")
    o = 1 - c
    bar = pltpu.get_barrier_semaphore()
    rings = ring_places(z, x, y, c)
    targets = [rings[a][1][d] for a in "zx" for d in (1, -1)]
    sib = dev(z, x, y, o)
    group = []
    for dy in range(4):
        for dc in range(2):
            if dy or dc:
                group.append((dy, dc, dev(z, x, (y + dy) % 4, (c + dc) % 2)))
    plane = [(4 * dz_ + dx_, (z + dz_) % 4, (x + dx_) % 4, (z + 4 - dz_) % 4, (x + 4 - dx_) % 4)
             for dz_ in range(4) for dx_ in range(4) if dz_ or dx_]
    greeted = targets + [(dp, g) for _, g in peers(f)] + [dev(zz, xx, y, c) for _, zz, xx, _, _ in plane]
    greet(bar, greeted)
    loads = {}
    def load(name, src, dst):
        loads[name] = pltpu.make_async_copy(src, dst, isem.at[len(loads)])
        return loads[name]
    for name, src, dst in (
        ("dm", dm_hbm, dm), ("act", act_hbm, act_ref), ("e", e_hbm, e_ref), ("dz", dz_hbm, dz), ("fc2", g2_hbm, wa), ("dact", dact_hbm, dact_ref), ("fc1", g_hbm.at[:, 4:8], wb),
        ("h2", h2_hbm, h2_ref), ("x2", x2_hbm, x2_ref), ("dx", dx_hbm, dx), ("rows", rows_hbm, rows_ref), ("o", o_hbm, o_ref),
        ("qkv", qkv_hbm, qkv_ref), ("a", a_hbm, a_ref), ("tok", tok_hbm.at[0:ROWS], tok),
        ("vs", vs_hbm, vs),
    ):
        load(name, src, dst).start()
    def need(*names):
        for n in names: loads[n].wait()
    ld_c = pltpu.make_async_copy(g_hbm.at[:, 0:4], wb, wsem.at[0])
    zb[...] = jnp.zeros_like(zb)
    vt[...] = jnp.zeros_like(vt)
    vsum[...] = jnp.zeros_like(vsum)
    pl.semaphore_wait(bar, len(greeted))

    few = f < 4
    def cells_to(i, g):
        return pltpu.make_async_remote_copy(cells_hbm.at[g], arr.at[f], css.at[i], csr.at[i], device_id=(dp, g), device_id_type=MESH)
    def small_cells_to(i, g):
        return pltpu.make_async_remote_copy(cells_hbm.at[16 + g % 4], arr.at[16 + f], css.at[16 + i], csr.at[16 + i], device_id=(dp, g), device_id_type=MESH)
    locals_ = [pltpu.make_async_copy(cells_hbm.at[f], arr.at[f], csl.at[0]), pltpu.make_async_copy(zb, arr.at[32], csl.at[1])]
    own_small = pltpu.make_async_copy(cells_hbm.at[16 + f % 4], arr.at[16 + f], csl.at[2])
    for l in locals_: l.start()
    for r, g in peers(f):
        cells_to(r, g).start()
        @pl.when(g < 4)
        def _():
            small_cells_to(r, g).start()
    @pl.when(few)
    def _():
        own_small.start()
    def finish_cells():
        for l in locals_: l.wait()
        for r, g in peers(f):
            src = (f + 16 - r) % 16
            pltpu.make_async_remote_copy(cells_hbm.at[g], arr.at[src], css.at[r], csr.at[r], device_id=(dp, g), device_id_type=MESH).wait_recv()
            cells_to(r, g).wait_send()
            @pl.when(g < 4)
            def _():
                small_cells_to(r, g).wait_send()
        @pl.when(few)
        def _():
            own_small.wait()
            for r, g in peers(f):
                src = (f + 16 - r) % 16
                pltpu.make_async_remote_copy(cells_hbm.at[16], arr.at[16 + src], css.at[16 + r], csr.at[16 + r], device_id=(dp, g), device_id_type=MESH).wait_recv()

    sends = {}
    def send(k, i, src, dst, to):
        cp = pltpu.make_async_remote_copy(src, dst, ssem.at[k, i], rsem.at[k, i], device_id=to, device_id_type=MESH)
        cp.start(); sends[k, i] = cp
    def recv(k, i, v):
        pltpu.make_async_remote_copy(v, v, ssem.at[k, i], rsem.at[k, i], device_id=sib, device_id_type=MESH).wait_recv()

    def steps(k, axes, ours, theirs, from_sib, inbox, parts):
        last = len(axes) - 1
        def add(v, *more):
            t = v[...].astype(f32)
            for m in more: t = t + m[...].astype(f32)
            v[...] = t.astype(bf16)
        def opposite(l):
            at, to = rings[axes[l]]
            _, fa, fb = parts[l]
            send(k, 4 * l, ours(l, at[2], fa), inbox(l, 0, fa), to[1])
            if fb is not None: send(k, 4 * l + 1, ours(l, at[2], fb), inbox(l, 0, fb), to[-1])
        def start():
            send(k, 12, theirs, from_sib, sib)
        def join():
            recv(k, 12, from_sib)
            at, _ = rings[axes[last]]
            for d in (2, 1, -1, 0):
                add(ours(last, at[d], parts[last][0]), share(last, at[d]))
                if d == 2: opposite(last)
        def share(l, place):
            return from_sib_view[k](place)
        def near(l):
            at, to = rings[axes[l]]
            full, fa, fb = parts[l]
            recv(k, 4 * l, inbox(l, 0, fa)); add(ours(l, at[1], fa), inbox(l, 0, fa))
            send(k, 4 * l + 2, ours(l, at[1], full), inbox(l, 1, full), to[1])
            if fb is not None:
                recv(k, 4 * l + 1, inbox(l, 0, fb)); add(ours(l, at[-1], fb), inbox(l, 0, fb))
            send(k, 4 * l + 3, ours(l, at[-1], full), inbox(l, 2, full), to[-1])
        def here(l):
            at, to = rings[axes[l]]
            full = parts[l][0]
            recv(k, 4 * l + 2, inbox(l, 1, full)); recv(k, 4 * l + 3, inbox(l, 2, full))
            add(ours(l, at[0], full), inbox(l, 1, full), inbox(l, 2, full))
            if l: opposite(l - 1)
        out = [start, join]
        for l in range(last, -1, -1):
            out += [functools.partial(near, l), functools.partial(here, l)]
        return out

    from_sib_view = {}
    def unit_chunk(k, axes, staged, *parts):
        def at_level(l, at):
            return [(z, at), (at, ALL)][l] if axes == "xz" else [(at, x), (ALL, at)][l]
        def cut(ref, part, l, at):
            u0, u1, l0, l1 = part
            zs, xs = at_level(l, at)
            return ref.at[u0:u1, zs, xs, :, l0:l1]
        def inbox(l, way, part):
            u0, u1, l0, l1 = part
            return xb.at[way, u0:u1, :, l0:l1] if l == 0 else xa.at[way, u0:u1, :, :, l0:l1]
        u0, u1, l0, l1 = parts[0]
        from_sib_view[k] = lambda place: cut(sg, parts[0], 1, place)
        return steps(k, axes, lambda l, at, part: cut(acc, part, l, at), staged, sg.at[u0:u1, :, :, :, l0:l1], inbox, [parts, parts])
    def fc2_chunk(k):
        def ours(l, at, part):
            a, b = part
            if l == 0: return acc2.at[z, at, y, a:b]
            if l == 1: return acc2.at[at, a:b, y]
            return acc2.at[a:b, :, at]
        def inbox(l, way, part):
            a, b = part
            return (xd, xc, xa2)[l].at[way, a:b]
        ring = ((0, 4), (0, 2), (2, 4))
        from_sib_view[k] = lambda place: sg2.at[:, :, place]
        return steps(k, "xzy", ours, sta2, sg2, inbox, [((0, 48), (0, 32), (32, 48)), ring, ring])

    lanes = lambda u, l0, lm, l1: ((u, u + 1, l0, l1), (u, u + 1, l0, lm), (u, u + 1, lm, l1))
    pair = lambda u: ((u, u + 2, 0, LW), (u, u + 1, 0, LW), (u + 1, u + 2, 0, LW))
    table = {
        "fc2": fc2_chunk(0),
        "dec": unit_chunk(1, "xz", stc.at[:, :, :, :, 0:256], *lanes(8, 0, 128, 256)),
        "f1a": unit_chunk(2, "xz", sta.at[0:2], *pair(4)),
        "f1b": unit_chunk(3, "xz", sta.at[2:4], *pair(6)),
        "out": unit_chunk(4, "zx", sta.at[3:4], *lanes(3, 0, 256, LW)),
        "q0": unit_chunk(5, "xz", sta.at[0:1], *lanes(0, 0, 256, LW)),
        "q1": unit_chunk(6, "zx", sta.at[1:2], *lanes(1, 0, 256, LW)),
        "q2": unit_chunk(8, "xz", sta.at[2:3, :, :, :, 0:256], *lanes(2, 0, 128, 256)),
        "q3": unit_chunk(9, "zx", sta.at[2:3, :, :, :, 256:LW], (2, 3, 256, LW), (2, 3, 256, LW), None),
    }
    def st(s, *names):
        for n in names: table[n][s]()

    def send_small(v):
        vout[...] = v.reshape(4, 4, 48, 128)
        vin[4 * z + x] = vout[z, x]
        for i, zz, xx, _, _ in plane:
            cp = pltpu.make_async_remote_copy(vout.at[zz, xx], vin.at[4 * z + x], vss.at[i], vrs.at[i], device_id=dev(zz, xx, y, c), device_id_type=MESH)
            cp.start(); lasts.append(cp)
    def sum_small():
        for i, zz, xx, sz, sx in plane:
            pltpu.make_async_remote_copy(vout.at[zz, xx], vin.at[4 * sz + sx], vss.at[i], vrs.at[i], device_id=dev(zz, xx, y, c), device_id_type=MESH).wait_recv()
        acc[8, z, x, :, 256:LW] = jnp.sum(vin[...].astype(f32), axis=0).astype(bf16)

    lasts = []
    me = 2 * y + c
    def last_exchange(j, pt, units):
        rs_ = slice(32 * j, 32 * j + 32)
        blk = jnp.concatenate([acc[u, z, x] for u in units], axis=0)
        fs[:, rs_] = jnp.dot(pt[...], blk, preferred_element_type=f32).astype(bf16).reshape(8, 32, LW)
        own = pltpu.make_async_copy(fs.at[me, rs_], f1.at[me, rs_], loc.at[j])
        own.start()
        got = []
        for i, (dy, dc, t) in enumerate(group):
            dst = 2 * ((y + dy) % 4) + (c + dc) % 2
            cp = pltpu.make_async_remote_copy(fs.at[dst, rs_], f1.at[me, rs_], ss1.at[j, i], rs1.at[j, i], device_id=t, device_id_type=MESH)
            cp.start()
            src = 2 * ((y + 4 - dy) % 4) + (c + dc) % 2
            rc = pltpu.make_async_remote_copy(fs.at[me, rs_], f1.at[src, rs_], ss1.at[j, i], rs1.at[j, i], device_id=t, device_id_type=MESH)
            lasts.append(cp); got.append(rc)
        def finish():
            own.wait()
            for rc in got: rc.wait_recv()
            for h in range(2):
                t = f1[h, rs_].astype(f32)
                for yy in range(1, 4): t = t + f1[2 * yy + h, rs_].astype(f32)
                fo[h, rs_] = t
        return finish
    def fc2_exchange():
        v = acc2[z, x, y].astype(f32)
        pad = jnp.zeros((8, LW), f32)
        for k in range(2):
            fs2[k] = jnp.concatenate([v[24 * k:24 * k + 24], pad], axis=0).astype(bf16)
        cp = pltpu.make_async_remote_copy(fs2.at[o], f2, ss1.at[0, 7], rs1.at[0, 7], device_id=sib, device_id_type=MESH)
        cp.start(); lasts.append(cp)
        of2_ref[:, pl.ds(pl.multiple_of(c * LW, LW), LW)] = jnp.where(c == 0, v[0:24], v[24:48])
        def finish():
            cp.wait_recv()
            of2_ref[:, pl.ds(pl.multiple_of(o * LW, LW), LW)] = f2[...].astype(f32)[0:24]
        return finish

    def blocks(body, n=7):
        def step(i, _):
            body(pl.ds(pl.multiple_of(i * 48, 48), 48)); return 0
        lax.fori_loop(0, n, step, 0)
    def col(base, width, unit):
        return pl.ds(pl.multiple_of(base, unit), width)

    def grad_fc2(h, dst):
        def part(i, _):
            t = lax.dot_general(act_ref[:, col(i * 768, 768, 768)], dm[:, col(h * LW, LW, LW)], TN, preferred_element_type=f32)
            dst[i] = t.astype(bf16).reshape(4, 4, 48, LW)
            return 0
        lax.fori_loop(0, 4, part, 0)

    def fc2_back():
        def part(i, _):
            cs = col(i * 768, 768, 768)
            t = lax.dot_general(dm[:, 0:LW], wa[0, i].reshape(768, LW), NT, preferred_element_type=f32)
            t = t + lax.dot_general(dm[:, LW:768], wa[1, i].reshape(768, LW), NT, preferred_element_type=f32)
            t = (t * dact_ref[:, cs].astype(f32)).astype(bf16)
            df[:, cs] = t
            vsum[5:6, cs] = jnp.sum(t.astype(f32), axis=0, keepdims=True)
            return 0
        lax.fori_loop(0, 4, part, 0)

    def wunit(h, u):
        return wb[h, u].reshape(768, LW)
    def fc1_back():
        for h in range(2):
            wt = lambda r: jnp.concatenate([wunit(h, u)[r] for u in range(4)], axis=1)
            for n in range(2):
                rs = slice(n * 384, (n + 1) * 384)
                t = lax.dot_general(df[:, h * 1536:(h + 1) * 1536], wt(rs), NT, preferred_element_type=f32)
                dh[:, rs] = t if h == 0 else dh[:, rs] + t

    def grad_fc1(h, dst, base):
        def part(u, _):
            t = lax.dot_general(h2_ref[...], df[:, col(h * 1536 + u * LW, LW, LW)], TN, preferred_element_type=f32)
            dst[base + u] = t.astype(bf16).reshape(4, 4, 48, LW)
            return 0
        lax.fori_loop(0, 4, part, 0)

    def norm_back(src, gain_row, into, out_lo, base):
        gain = rows_ref[gain_row:gain_row + 1, 0:768]
        def body(r):
            n, rstd = stats(src[r, :].astype(f32))
            d = dh[r, :]
            vsum[base:base + 1, 0:768] += jnp.sum(d * n, axis=0, keepdims=True)
            vsum[base + 1:base + 2, 0:768] += jnp.sum(d, axis=0, keepdims=True)
            dn = d * gain
            t = rstd * (dn - jnp.mean(dn, axis=-1, keepdims=True) - n * jnp.mean(dn * n, axis=-1, keepdims=True))
            t = dx[r, :] + t
            into[r, :] = t
            if out_lo is not None: out_lo[r, :] = t.astype(bf16)
        blocks(body)

    def out_back():
        t = lax.dot_general(dm[:, 0:LW], wunit(0, 3), NT, preferred_element_type=f32)
        t = t + lax.dot_general(dm[:, LW:768], wunit(1, 3), NT, preferred_element_type=f32)
        df[:, 0:768] = t.astype(bf16)

    def load_p(i):
        return pltpu.make_async_copy(p_hbm.at[pl.ds(2 * (i // 2 + 3 * (i % 2)), 2)], pb.at[i % 2], psem.at[i % 2])

    def attn_back(u):
        low = lax.broadcasted_iota(jnp.int32, (1, 128), 1) < 64
        def pair(j, _):
            load_p(2 * u + j).wait()
            i = u + 3 * j
            def cols(b):
                return qkv_ref[:, col(LW * i + 128 * b, 128, 128)]
            q, kk, v, do = cols(0), cols(1), cols(2), df[:, col(i * 128, 128, 128)]
            r = []
            for t in range(2):
                keep = low if t == 0 else jnp.logical_not(low)
                pr = pb[j, t]
                dp = lax.dot_general(jnp.where(keep, do, jnp.zeros_like(do)), v, NT, preferred_element_type=f32)
                p32 = pr.astype(f32)
                ds = (p32 * (dp - jnp.sum(dp * p32, axis=-1, keepdims=True))).astype(bf16)
                dv = lax.dot_general(pr, do, TN, preferred_element_type=f32)
                dq = jnp.dot(ds, kk, preferred_element_type=f32)
                dk = lax.dot_general(ds, q, TN, preferred_element_type=f32)
                r.append((0.125 * dq, 0.125 * dk, dv))
            for b in range(3):
                dqkv[:, col(LW * i + 128 * b, 128, 128)] = jnp.where(low, r[0][b], r[1][b]).astype(bf16)
            if u < 2: load_p(2 * u + j + 2).start()
            return 0
        lax.fori_loop(0, 2, pair, 0)

    def qkv_back():
        for h in range(2):
            wt = lambda r: jnp.concatenate([wunit(h, u)[r] for u in range(3)], axis=1)
            for n in range(2):
                rs = slice(n * 384, (n + 1) * 384)
                t = lax.dot_general(dqkv[:, h * 1152:(h + 1) * 1152], wt(rs), NT, preferred_element_type=f32)
                dh[:, rs] = t if h == 0 else dh[:, rs] + t

    def grad_qkv(u, h, dst):
        t = lax.dot_general(a_ref[...], dqkv[:, col(h * 1152 + u * LW, LW, LW)], TN, preferred_element_type=f32)
        dst[u] = t.astype(bf16).reshape(4, 4, 48, LW)
    def grad_out(h, dst):
        t = lax.dot_general(o_ref[...], dm[:, col(h * LW, LW, LW)], TN, preferred_element_type=f32)
        dst[3] = t.astype(bf16).reshape(4, 4, 48, LW)

    def vec_cols():
        rt = jnp.concatenate([vsum[0:8, 0:768], jnp.zeros((120, 768), f32)], axis=0)
        srow = lax.broadcasted_iota(jnp.int32, (128, 768), 0)
        rt = jnp.where(srow < 5, rt, 0.0)
        v = rt.T
        r2 = jnp.concatenate([vsum[0:16, 0:512], jnp.zeros((112, 512), f32)], axis=0)
        srow2 = lax.broadcasted_iota(jnp.int32, (128, 512), 0)
        r2 = jnp.where((srow2 == 9) | (srow2 == 10), r2, 0.0).astype(bf16)
        v = v + lax.dot_general(m2_ref[...], r2, NT, preferred_element_type=f32)
        lane = (lax.broadcasted_iota(jnp.int32, (128, 768), 1) % 24) // 6
        parts = []
        for s in range(4):
            wrow = jnp.broadcast_to(vsum[5:6, 768 * s:768 * s + 768], (128, 768))
            wt = jnp.where(srow - 5 == lane, wrow, 0.0).astype(bf16)
            parts.append(lax.dot_general(m4_ref[...], wt, NT, preferred_element_type=f32))
        return (v + jnp.concatenate(parts, axis=0)).astype(bf16)

    def grad_dec(h, dst_store):
        t = lax.dot_general(e_ref[...], dz[:, col(h * 256, 256, 256)], TN, preferred_element_type=f32)
        dst_store(t.astype(bf16).reshape(4, 4, 48, 256), slice(0, 256))

    def acc8(v, cs): acc[8, :, :, :, cs] = v
    def stc8(v, cs): stc[0, :, :, :, cs] = v

    need("dm", "act")
    grad_fc2(o, sta2); st(0, "fc2")
    grad_fc2(c, acc2)
    vsum[4:5, 0:768] = jnp.sum(dm[...].astype(f32), axis=0, keepdims=True)
    need("e", "dz")
    grad_dec(o, stc8); st(0, "dec")
    grad_dec(c, acc8)
    need("fc2", "dact")
    fc2_back()
    st(1, "fc2", "dec")
    need("h2")
    grad_fc1(o, sta, 0); st(0, "f1a", "f1b")
    grad_fc1(c, acc, 4)
    st(2, "dec")
    need("fc1")
    fc1_back()
    ld_c.start()
    load_p(0).start(); load_p(1).start()
    st(1, "f1a", "f1b")
    need("x2", "dx", "rows")
    norm_back(x2_ref, 2, dx, dm, 2)
    ld_c.wait()
    for kk in (2, 3): sends[kk, 12].wait_send(); del sends[kk, 12]
    need("o", "qkv")
    grad_out(o, sta); st(0, "out")
    grad_out(c, acc)
    out_back()
    st(3, "dec"); st(1, "out")
    need("a")
    attn_back(0)
    st(2, "f1a", "f1b")
    grad_qkv(0, o, sta); st(0, "q0"); grad_qkv(0, c, acc)
    st(2, "fc2"); st(2, "out"); st(4, "dec")
    attn_back(1)
    st(3, "out"); st(5, "dec"); st(1, "q0")
    grad_qkv(1, o, sta); st(0, "q1"); grad_qkv(1, c, acc)
    st(3, "f1a", "f1b")
    attn_back(2)
    st(2, "q0"); st(1, "q1"); st(3, "fc2")
    grad_qkv(2, o, sta); st(0, "q2", "q3"); grad_qkv(2, c, acc)
    st(4, "out", "f1a", "f1b"); st(3, "q0"); st(4, "fc2")
    qkv_back()
    st(1, "q2", "q3"); st(2, "q1"); st(5, "out", "f1a", "f1b", "fc2")
    finish_first = last_exchange(0, pt1_ref, (4, 5, 6, 7))
    need("tok", "vs")
    vsum[9:11, 0:512] = vs[9:11, :]
    norm_back(tok, 0, dx, None, 0)
    st(2, "q2", "q3")
    send_small(vec_cols())
    dh[0:512 - ROWS, :] = jnp.zeros((512 - ROWS, 768), f32)
    tgs = [pltpu.make_async_copy(dx, tg_ref.at[0:ROWS], tsem.at[0]), pltpu.make_async_copy(dh.at[0:512 - ROWS], tg_ref.at[ROWS:512], tsem.at[1])]
    for t in tgs: t.start()
    st(3, "q1"); st(4, "q0"); st(6, "fc2")
    st(3, "q2", "q3"); st(5, "q0"); st(4, "q1"); st(7, "fc2")
    finish_fc2 = fc2_exchange()
    st(4, "q2", "q3"); st(5, "q1")
    sum_small()
    finish_fc2(); finish_first()
    st(5, "q2", "q3")
    finish_second = last_exchange(1, pt2_ref, (0, 1, 2, 3, 8))
    for h in range(2):
        for u in range(4):
            of1_ref[:, h * 1536 + u * LW:h * 1536 + (u + 1) * LW] = fo[h, 6 * u:6 * u + 6, :]
    finish_second()
    for h in range(2):
        for u in range(3):
            for b in range(3):
                first = 768 * b + 128 * (3 * h + u)
                oq_ref[:, first:first + 128] = fo[h, 32 + 6 * u:38 + 6 * u, 128 * b:128 * b + 128]
        oo_ref[:, h * LW:(h + 1) * LW] = fo[h, 50:56, :]
        od_ref[:, h * 256:(h + 1) * 256] = fo[h, 56:62, 0:256]
    vt[0:6, :] = fo[0, 56:62, 256:384] + fo[1, 56:62, 256:384]
    vrows = vt[...].T
    for i, r in enumerate((v0_ref, v1_ref, v2_ref, v3_ref, v4_ref)):
        r[...] = vrows[i:i + 1, 0:6]
    for q in range(4):
        vf_ref[:, 6 * q:6 * q + 6] = vrows[5 + q:6 + q, 0:6]
    vd_ref[...] = vrows[9:10, 0:4]
    vm_ref[...] = vrows[10:11, 0:4]
    finish_cells()
    for t in tgs: t.wait()
    for cp in lasts: cp.wait_send()
    for cp in sends.values(): cp.wait_send()


def k2_call(*args):
    S = jax.ShapeDtypeStruct
    vm = pl.BlockSpec(memory_space=pltpu.VMEM)
    anyspec = pl.BlockSpec(memory_space=pl.ANY)
    V, DMA = pltpu.VMEM, pltpu.SemaphoreType.DMA
    outs = (S((512, 768), f32), S((33, 64, 512), bf16), S((6, 2304), f32), S((6, 768), f32), S((6, 3072), f32), S((24, 768), f32),
            S((6, 512), f32)) + (S((1, 6), f32),) * 5 + (S((1, 24), f32), S((1, 4), f32), S((1, 4), f32))
    return pl.pallas_call(
        k2_kernel,
        out_shape=outs,
        in_specs=[anyspec] * 18 + [vm] * 4,
        out_specs=[anyspec] * 2 + [vm] * 13,
        scratch_shapes=[
            V((8, 3072), f32), V((ROWS, 768), bf16), V((ROWS, 2304), bf16), V((ROWS, 768), bf16), V((ROWS, 768), f32),
            V((ROWS, 768), bf16), V((ROWS, 3072), bf16), V((ROWS, 3072), bf16), V((ROWS, 768), bf16), V((ROWS, 512), bf16),
            V((ROWS, 768), f32), V((ROWS, 768), bf16), V((16, 512), f32), V((ROWS, 768), bf16),
            V((2, 4, 4, 4, 48, LW), bf16), V((2, 4, 4, 4, 48, LW), bf16),
            V((4, 4, 4, 48, LW), bf16), V((4, 4, 4, 48, LW), bf16), V((1, 4, 4, 48, LW), bf16),
            V((9, 4, 4, 48, LW), bf16), V((4, 4, 4, 48, LW), bf16),
            V((9, 4, 4, 48, LW), bf16), V((4, 4, 4, 48, LW), bf16),
            V((3, 9, 4, 48, LW), bf16), V((3, 4, 4, 48, LW), bf16),
            V((3, 9, 48, LW), bf16), V((3, 4, 48, LW), bf16), V((3, 48, LW), bf16),
            V((ROWS, 768), f32), V((ROWS, 3072), bf16), V((ROWS, 2304), bf16), V((16, 3072), f32), V((2, 2, ROWS, ROWS), bf16),
            V((8, YROWS, LW), bf16), V((8, YROWS, LW), bf16), V((2, YROWS, LW), f32), V((2, 32, LW), bf16), V((32, LW), bf16), V((64, 512), bf16), V((128, 128), f32), V((4, 4, 48, 128), bf16), V((16, 48, 128), bf16),
            DMA((10, 13)), DMA((10, 13)), DMA((2, 8)), DMA((2, 8)), DMA((2,)), DMA((1,)), DMA((2,)), DMA((2,)), DMA((16,)),
            DMA((32,)), DMA((32,)), DMA((3,)), DMA((16,)), DMA((16,)),
        ],
        compiler_params=pltpu.CompilerParams(collective_id=1, has_side_effects=True, vmem_limit_bytes=60 * 2**20),
        cost_estimate=pl.CostEstimate(flops=12 * 10**9, bytes_accessed=5 * 10**7, transcendentals=0),
        name="backward",
    )(*args, jnp.asarray(spread_matrix((4, 5, 6, 7), 0), bf16), jnp.asarray(spread_matrix((0, 1, 2, 3, 8), 32), bf16),
      jnp.asarray(cell_spread(), bf16), jnp.asarray(fc1_bias_spread(), bf16))


def k3_kernel(inv, arr, tg, *refs):
    n = len(refs) - 3
    small, (grid, tg_out, *outs), (gv, tv, sem) = refs[:13], refs[13:n], refs[n:]
    ins = [pltpu.make_async_copy(tg, tv, sem.at[0])]
    ins += [pltpu.make_async_copy(arr.at[inv[0, r]], gv.at[r], sem.at[1 + r]) for r in range(32)]
    for cp in ins: cp.start()
    for a, b in zip(small, outs): b[...] = a[...]
    back = [pltpu.make_async_copy(tv, tg_out, sem.at[33])]
    back += [pltpu.make_async_copy(gv.at[pl.ds(8 * i, 8)], grid.at[pl.ds(8 * i, 8)], sem.at[34 + i]) for i in range(4)]
    ins[0].wait()
    back[0].start()
    for i in range(4):
        for r in range(8): ins[1 + 8 * i + r].wait()
        back[1 + i].start()
    for cp in back: cp.wait()


def k3_call(inv, arr, tg, *small):
    S = jax.ShapeDtypeStruct
    vm = pl.BlockSpec(memory_space=pltpu.VMEM)
    anyspec = pl.BlockSpec(memory_space=pl.ANY)
    return pl.pallas_call(
        k3_kernel,
        out_shape=(S((32, 64, 512), bf16), S((512, 768), f32)) + tuple(S(t.shape, t.dtype) for t in small),
        in_specs=[pl.BlockSpec(memory_space=pltpu.SMEM), anyspec, anyspec] + [vm] * 13,
        out_specs=[anyspec, anyspec] + [vm] * 13,
        scratch_shapes=[pltpu.VMEM((32, 64, 512), bf16), pltpu.VMEM((512, 768), f32), pltpu.SemaphoreType.DMA((38,))],
        name="results",
    )(inv, arr, tg, *small)


def body(tokens, chip_lengths, chip_ids, positions, ln1_gain, ln1_bias, qkv_weight, out_weight, ln2_gain, ln2_bias, fc1_weight,
         fc1_bias, fc2_weight, fc2_bias, dec_weight, dec_bias, mask_token, grid_cotangent):
    row = lambda v: v.reshape(1, -1)
    *saved, inv = k1_call(chip_ids, chip_lengths, row(positions), tokens, row(ln1_gain), row(ln1_bias), qkv_weight, out_weight,
                          row(ln2_gain), row(ln2_bias), fc1_weight, row(fc1_bias), fc2_weight, row(fc2_bias), dec_weight,
                          row(dec_bias), row(mask_token), grid_cotangent)
    tg, arrived, *small = k2_call(*saved, tokens)
    grid, tg, dq, do, df1, df2, dd, *v = k3_call(inv, arrived, tg, *small)
    v = [t.reshape(-1) for t in v]
    return (grid, tg, v[0], v[1], dq, do, v[2], v[3], df1, v[5], df2, v[4], dd, v[6], v[7])


def solution(mesh):
    both = ("dp", "fsdp")
    r1, r2, grid = P(both), P(both, None), P("dp", "fsdp", None)
    weights = (r1, r1, r2, r2, r1, r1, r2, r1, r2, r1, r2, r1, r1)
    return jax.shard_map(body, mesh=mesh, in_specs=(r2, r1, r1, r1) + weights + (grid,), out_specs=(grid, r2) + weights,
                         check_vma=False)
```

```python
import functools
import numpy as np
import jax, jax.numpy as jnp
from jax import lax
from jax.experimental import pallas as pl
from jax.experimental.pallas import tpu as pltpu
from jax.sharding import PartitionSpec as P

MESH = pl.DeviceIdType.MESH
LW = 384
SROWS = 96
YROWS = 64

def coords():
    dp = lax.axis_index("dp"); fs = lax.axis_index("fsdp")
    z = dp // 2
    x = (dp % 2) * 2 + fs // 8
    y = (fs % 8) // 2
    c = fs % 2
    return z, x, y, c

def dev(z, x, y, c):
    return (z * 2 + x // 2, (x % 2) * 8 + y * 2 + c)

UNIT_ROWS = (32, 38, 44, 50, 0, 6, 12, 18, 56)
FC2_ROWS = 64


def perm_matrix():
    m = np.zeros((432, 512), np.float32)
    for u, base in enumerate(UNIT_ROWS):
        for d in range(8):
            for j in range(6):
                m[48 * u + 6 * d + j, d * 64 + base + j] = 1
    return m


def spread_matrix(units, first):
    m = perm_matrix().reshape(9, 48, 8, 64)[list(units), :, :, first:first + 32]
    return m.reshape(48 * len(units), 256).T


ALL = slice(None)


def ring_places(z, x, y, c):
    out = {}
    for name, v in (("z", z), ("x", x), ("y", y)):
        at = {0: v, 1: (v + 1) % 4, -1: (v + 3) % 4, 2: (v + 2) % 4}
        to = {k: dev(*(at[k] if n == name else w for n, w in (("z", z), ("x", x), ("y", y))), c) for k in (1, -1)}
        out[name] = (at, to)
    return out


ROWS = 336
HEADS_PAIRS = 6
D = 768
NT = (((1,), (1,)), ((), ()))
TN = (((0,), (0,)), ((), ()))
f32, bf16 = jnp.float32, jnp.bfloat16


def cell_spread():
    m = np.zeros((768, 512), np.float32)
    for d in range(128):
        for j in range(4):
            m[6 * d + j, 4 * d + j] = 1
    return m


def fc1_bias_spread():
    m = np.zeros((192, 768), np.float32)
    n = np.arange(768)
    m[6 * (n // 24) + n % 6, n] = 1
    return m


def peers(f):
    return [(r, (f + r) % 16) for r in range(1, 16)]


def greet(bar, devices):
    for t in devices:
        pl.semaphore_signal(bar, inc=1, device_id=t, device_id_type=MESH)


def stats(v):
    mean = jnp.mean(v, axis=-1, keepdims=True)
    center = v - mean
    rstd = lax.rsqrt(jnp.mean(center * center, axis=-1, keepdims=True) + 1e-6)
    return center * rstd, rstd


def gelu_pair(f):
    cdf = 0.5 * (1.0 + lax.erf(f * 0.7071067811865476))
    pdf = 0.3989422804014327 * jnp.exp(-0.5 * f * f)
    return f * cdf, cdf + f * pdf


def k1_kernel(ids, lens, pos, tok, l1g, l1b, qkv_s, out_s, l2g, l2b, fc1_s, fc1b, fc2_s, fc2b, dec_s, decb, maskt, cot_hbm,
              p1_ref, p2_ref, m2_ref, m4_ref,
              g_hbm, g2_hbm, rows_hbm, a_hbm, qkv_hbm, p_hbm, o_hbm, x2_hbm, h2_hbm, act_hbm, dact_hbm, e_hbm, cells_hbm,
              dz_hbm, dx_hbm, dm_hbm, vs_hbm, inv_hbm,
              g_ref, g2_ref, rows_ref, a_ref, qkv_ref, p_out, o_ref, x2_ref, h2_ref, act_ref, dact_ref, e_ref, cells_ref,
              dz, dx, dm, vs, inv,
              sp, s_ref, s1, s2, z_ref, vrow, tag, tags, idv, idm, cot, cotsend, dc, hits,
              ss1, rs1, loc, ssem, rsem, wsem, osem, tss, tsr, bss, bsr, mss, msr, lsem):
    z, x, y, c = coords()
    dp, f = lax.axis_index("dp"), lax.axis_index("fsdp")
    o = 1 - c
    bar = pltpu.get_barrier_semaphore()
    rings = ring_places(z, x, y, c)
    targets = [rings[a][1][d] for a in "zx" for d in (1, -1)]
    group = []
    for dy in range(4):
        for dc_ in range(2):
            if dy or dc_:
                group.append((dy, dc_, dev(z, x, (y + dy) % 4, (c + dc_) % 2)))
    greeted = targets + [(dp, g) for _, g in peers(f)]
    greet(bar, greeted)
    ld_cot = pltpu.make_async_copy(cot_hbm, cot, lsem.at[0])
    ld_cot.start()

    sp[...] = jnp.zeros_like(sp)
    for h in range(2):
        for u in range(3):
            for b in range(3):
                first = 768 * b + 128 * (3 * h + u)
                sp[h, 32 + 6 * u:38 + 6 * u, 128 * b:128 * b + 128] = qkv_s[:, first:first + 128].astype(f32)
        sp[h, 50:56, :] = out_s[:, h * LW:(h + 1) * LW].astype(f32)
        for u in range(4):
            sp[h, 6 * u:6 * u + 6, :] = fc1_s[:, h * 1536 + u * LW:h * 1536 + (u + 1) * LW].astype(f32)
        sp[h, 64:88, :] = fc2_s[:, h * LW:(h + 1) * LW].astype(f32)
        sp[h, 56:62, 0:256] = dec_s[:, h * 256:(h + 1) * 256].astype(f32)
    vrow[...] = jnp.zeros_like(vrow)
    for i, r in enumerate((l1g, l1b, l2g, l2b, fc2b)):
        vrow[i:i + 1, 0:6] = r[...].astype(f32)
    for q in range(4):
        vrow[5 + q:6 + q, 0:6] = fc1b[:, 6 * q:6 * q + 6].astype(f32)
    vrow[9:10, 0:4] = decb[...].astype(f32)
    vrow[10:11, 0:4] = maskt[...].astype(f32)
    sp[0, 56:62, 256:384] = vrow[...].T[0:6]
    s_ref[...] = sp[...].astype(bf16)
    first_small = lens[0] < lens[1]
    trow = lax.broadcasted_iota(jnp.int32, (8, 128), 0)
    tag[...] = jnp.where(trow == 0, jnp.where(first_small, ids[1], ids[0]), jnp.where(first_small, ids[0], ids[1]))
    pl.semaphore_wait(bar, len(greeted))

    me = 2 * y + c
    sib = dev(z, x, y, o)
    mate = pltpu.make_async_remote_copy(s_ref.at[o, YROWS:SROWS], s2, ss1.at[2, 0], rs1.at[2, 0], device_id=sib, device_id_type=MESH)
    mate.start()
    firsts = []
    for j, rows in enumerate((slice(32, 64), slice(0, 32))):
        own = pltpu.make_async_copy(s_ref.at[c, rows], s1.at[me, rows], loc.at[j])
        own.start()
        got = []
        for i, (dy, dc_, t) in enumerate(group):
            cp = pltpu.make_async_remote_copy(s_ref.at[(c + dc_) % 2, rows], s1.at[me, rows], ss1.at[j, i], rs1.at[j, i], device_id=t, device_id_type=MESH)
            cp.start()
            src = 2 * ((y + 4 - dy) % 4) + (c + dc_) % 2
            rc = pltpu.make_async_remote_copy(s_ref.at[c, rows], s1.at[src, rows], ss1.at[j, i], rs1.at[j, i], device_id=t, device_id_type=MESH)
            got.append((cp, rc))
        firsts.append((own, got))
    def shards(j):
        own, got = firsts[j]
        own.wait()
        for _, rc in got: rc.wait_recv()
    tagged = []
    tags[f] = tag[...]
    for r, g in peers(f):
        cp = pltpu.make_async_remote_copy(tag, tags.at[f], tss.at[r], tsr.at[r], device_id=(dp, g), device_id_type=MESH)
        cp.start(); tagged.append(cp)
    def sort_cotangents():
        for r, g in peers(f):
            src = (f + 16 - r) % 16
            pltpu.make_async_remote_copy(tag, tags.at[src], tss.at[r], tsr.at[r], device_id=(dp, g), device_id_type=MESH).wait_recv()
        for s in range(16):
            idv[s:s + 1, :] = tags[s, 0:1, :]
            idv[16 + s:17 + s, :] = tags[s, 1:2, :]
        ld_ids = pltpu.make_async_copy(idv, idm, lsem.at[1])
        ld_ids.start()
        srow = lax.broadcasted_iota(jnp.int32, (32, 128), 0)
        hit = idv[...] == lax.broadcasted_iota(jnp.int32, (32, 128), 1)
        place_of = jnp.where((srow >= 16) & (f >= 4), 32, srow)
        inv[...] = jnp.broadcast_to(jnp.sum(jnp.where(hit, place_of, 0), axis=0, keepdims=True), (8, 128))
        ld_ids.wait()
        ld_cot.wait()
        for s in range(32):
            cotsend[s] = cot[idm[s, 0]]

    few = f < 4
    def to_peer(i, g):
        big = pltpu.make_async_remote_copy(cotsend.at[g], dc.at[f], bss.at[i], bsr.at[i], device_id=(dp, g), device_id_type=MESH)
        return big
    def small_to_peer(i, g):
        return pltpu.make_async_remote_copy(cotsend.at[16 + g], dc.at[16 + f % 4], mss.at[i], msr.at[f % 4], device_id=(dp, g), device_id_type=MESH)
    own_dc = pltpu.make_async_copy(cotsend.at[f], dc.at[f], lsem.at[2])
    own_small = pltpu.make_async_copy(cotsend.at[16 + f], dc.at[16 + f % 4], lsem.at[3])
    def send_cotangents():
        own_dc.start()
        for r, g in peers(f):
            to_peer(r, g).start()
    def send_small_cotangents():
        @pl.when(few)
        def _():
            own_small.start()
            for r, g in peers(f):
                small_to_peer(r, g).start()
    def get_cotangents():
        own_dc.wait()
        for r, g in peers(f):
            src = (f + 16 - r) % 16
            pltpu.make_async_remote_copy(cotsend.at[g], dc.at[src], bss.at[r], bsr.at[r], device_id=(dp, g), device_id_type=MESH).wait_recv()
        for s in range(4):
            @pl.when(f != s)
            def _():
                pltpu.make_async_remote_copy(cotsend.at[16], dc.at[16 + s], mss.at[0], msr.at[s], device_id=(dp, s), device_id_type=MESH).wait_recv()
        @pl.when(few)
        def _():
            own_small.wait()
    def finish_cotangents():
        for r, g in peers(f):
            to_peer(r, g).wait_send()
        @pl.when(few)
        def _():
            for r, g in peers(f):
                small_to_peer(r, g).wait_send()

    def relay(perm, rows, lo, hi):
        flat = s1[:, rows].reshape(256, LW)
        r = jnp.dot(perm[lo:hi, :], flat, preferred_element_type=f32)
        return r.astype(bf16)

    def place(p):
        if p == 0: g_ref[c, 0:4, z, x] = relay(p2_ref, slice(32, 64), 0, 192).reshape(4, 48, LW)
        if p == 1: g_ref[c, 4:8, z, x] = relay(p1_ref, slice(0, 32), 0, 192).reshape(4, 48, LW)
        if p == 2:
            mate.wait_recv()
            both = [s_ref[c, YROWS:SROWS].astype(f32)[0:24], s2[...].astype(f32)[0:24]]
            both = [jnp.where(c == k, both[0], both[1]) for k in range(2)]
            g2_ref[c, z, x, y] = jnp.concatenate(both, axis=0).astype(bf16)
        if p == 3: g_ref[c, 8, z, x] = relay(p2_ref, slice(32, 64), 192, 240)

    sends = []
    def mk(k, i, v, to):
        return pltpu.make_async_remote_copy(v, v, ssem.at[k, i], rsem.at[k, i], device_id=to, device_id_type=MESH)
    def send(k, i, v, to):
        cp = mk(k, i, v, to); cp.start(); sends.append(cp)
    def recv(k, i, v):
        mk(k, i, v, sib).wait_recv()

    def steps(k, axes, view, parts):
        last = len(axes) - 1
        def opposite(l):
            at, _ = rings[axes[l]]
            _, fa, fb = parts[l]
            recv(k, 4 * l + 2, view(l, at[2], fa, c))
            if fb is not None: recv(k, 4 * l + 3, view(l, at[2], fb, c))
        def first(l):
            at, to = rings[axes[l]]
            full = parts[l][0]
            if l: opposite(l - 1)
            for i, d in enumerate((1, -1)): send(k, 4 * l + i, view(l, at[0], full, c), to[d])
            if l == last: send(k, 12, view(l, at[0], full, c), sib)
        def second(l):
            at, to = rings[axes[l]]
            full, fa, fb = parts[l]
            recv(k, 4 * l, view(l, at[-1], full, c))
            send(k, 4 * l + 2, view(l, at[-1], fa, c), to[1])
            if l == last: send(k, 13, view(l, at[-1], full, c), sib)
            recv(k, 4 * l + 1, view(l, at[1], full, c))
            if fb is not None: send(k, 4 * l + 3, view(l, at[1], fb, c), to[-1])
            if l == last: send(k, 14, view(l, at[1], full, c), sib)
        def third():
            at, _ = rings[axes[last]]
            opposite(last)
            send(k, 15, view(last, at[2], parts[last][0], c), sib)
        def fourth():
            at, _ = rings[axes[last]]
            for i, d in enumerate((0, -1, 1, 2)): recv(k, 12 + i, view(last, at[d], parts[last][0], o))
        out = []
        for l in range(last + 1):
            out += [functools.partial(first, l), functools.partial(second, l)]
        return out + [third, fourth]

    def unit_chunk(k, axes, *parts):
        def view(l, at, part, h):
            u0, u1, l0, l1 = part
            zs, xs = [(z, at), (at, ALL)][l] if axes == "xz" else [(at, x), (ALL, at)][l]
            return g_ref.at[h, u0:u1, zs, xs, :, l0:l1]
        return steps(k, axes, view, [parts, parts])
    def fc2_chunk(k):
        def view(l, at, part, h):
            a, b = part
            if l == 0: return g2_ref.at[h, z, at, y, a:b]
            if l == 1: return g2_ref.at[h, at, a:b, y]
            return g2_ref.at[h, a:b, :, at]
        ring = ((0, 4), (0, 2), (2, 4))
        return steps(k, "xzy", view, [((0, 48), (0, 32), (32, 48)), ring, ring])

    outs = []
    def to_hbm(p):
        if p == 2: cp = pltpu.make_async_copy(g2_ref, g2_hbm, wsem.at[p])
        else:
            u0, u1 = ((0, 4), (4, 8), None, (8, 9))[p]
            cp = pltpu.make_async_copy(g_ref.at[:, u0:u1], g_hbm.at[:, u0:u1], wsem.at[p])
        cp.start(); outs.append(cp)

    def blocks(body, n=7):
        def step(i, _):
            body(pl.ds(pl.multiple_of(i * 48, 48), 48)); return 0
        lax.fori_loop(0, n, step, 0)

    def w(h, u):
        return g_ref[h, u].reshape(768, LW)

    def rows_of():
        v = jnp.concatenate([g_ref[0, 8, zz, xx, :, 256:384] for zz in range(4) for xx in range(4)], axis=0)
        vt = v.astype(f32).T
        rows_ref[0:5, 0:768] = vt[0:5]
        md = lax.dot_general(v, m2_ref[...], TN, preferred_element_type=f32)
        rows_ref[6:8, 0:512] = md[9:11]
        lane = (lax.broadcasted_iota(jnp.int32, (8, 768), 1) % 24) // 6
        row = lax.broadcasted_iota(jnp.int32, (8, 768), 0)
        for s in range(4):
            q = lax.dot_general(v[192 * s:192 * s + 192], m4_ref[...], TN, preferred_element_type=f32)
            q = jnp.where(row == lane, q[5:13], 0.0)
            rows_ref[5:6, 768 * s:768 * s + 768] = jnp.sum(q, axis=0, keepdims=True)

    def ln1():
        def body(r):
            n, _ = stats(tok[r, :].astype(f32))
            a_ref[r, :] = (n * rows_ref[0:1, 0:768] + rows_ref[1:2, 0:768]).astype(bf16)
        blocks(body)

    def qkv():
        for h in range(2):
            wt = jnp.concatenate([w(h, u) for u in range(3)], axis=1)
            qkv_ref[:, h * 1152:(h + 1) * 1152] = jnp.dot(a_ref[...], wt, preferred_element_type=f32).astype(bf16)

    ends0 = lens[0] + 2
    ends1 = ends0 + lens[1] + 2
    def seg(shape, axis):
        r = lax.broadcasted_iota(jnp.int32, shape, axis)
        return (r >= ends0).astype(jnp.int32) + (r >= ends1).astype(jnp.int32)

    def attention(lo, hi):
        low = lax.broadcasted_iota(jnp.int32, (1, 128), 1) < 64
        same = seg((ROWS, 1), 0) == seg((1, ROWS), 1)
        bias = jnp.where(same, 0.0, -1e30)
        def pair(i, _):
            q, k, v = (qkv_ref[:, pl.ds(pl.multiple_of(LW * i + 128 * b, 128), 128)] for b in range(3))
            outs_ = []
            for t in range(2):
                keep = low if t == 0 else jnp.logical_not(low)
                s = lax.dot_general(jnp.where(keep, q, jnp.zeros_like(q)), k, NT, preferred_element_type=f32)
                s = jnp.where(same, s * 0.125, -1e30)
                m = jnp.max(s, axis=-1, keepdims=True)
                ex = jnp.exp(s - m)
                pr = (ex / jnp.sum(ex, axis=-1, keepdims=True)).astype(bf16)
                p_out[2 * i + t] = pr
                outs_.append(jnp.dot(pr, v, preferred_element_type=f32))
            o_ref[:, pl.ds(pl.multiple_of(i * 128, 128), 128)] = jnp.where(low, outs_[0], outs_[1]).astype(bf16)
            return 0
        lax.fori_loop(lo, hi, pair, 0)

    def out_proj():
        for h in range(2):
            cs = slice(h * LW, (h + 1) * LW)
            x2_ref[:, cs] = tok[0:ROWS, cs].astype(f32) + jnp.dot(o_ref[...], w(h, 3), preferred_element_type=f32)
        def body(r):
            n, _ = stats(x2_ref[r, :])
            h2_ref[r, :] = (n * rows_ref[2:3, 0:768] + rows_ref[3:4, 0:768]).astype(bf16)
        blocks(body)

    def fc1(first):
        for h in range(2):
            def unit(u, _):
                cs = pl.ds(pl.multiple_of(h * 1536 + u * LW, LW), LW)
                f = jnp.dot(h2_ref[...], w(h, 4 + u), preferred_element_type=f32) + rows_ref[5:6, cs]
                g, dg = gelu_pair(f)
                act_ref[:, cs] = g.astype(bf16)
                dact_ref[:, cs] = dg.astype(bf16)
                return 0
            lax.fori_loop(first, first + 2, unit, 0)

    def fc2():
        for h in range(2):
            cs = slice(h * LW, (h + 1) * LW)
            t = jnp.dot(act_ref[...], g2_ref[h].reshape(3072, LW), preferred_element_type=f32)
            e_ref[:, cs] = (x2_ref[:, cs] + t + rows_ref[4:5, cs]).astype(bf16)

    def dec():
        for h in range(2):
            cs = slice(h * 256, (h + 1) * 256)
            t = jnp.dot(e_ref[...], g_ref[h, 8, :, :, :, 0:256].reshape(768, 256), preferred_element_type=f32)
            z_ref[:, cs] = (t + rows_ref[6:7, cs]).astype(bf16)
        z_ref[:, 512:640] = jnp.ones((ROWS, 128), bf16)
        def block(i, _):
            fill = hits[pl.ds(pl.multiple_of(i * 256, 256), 256), :]
            r = jnp.dot(fill, z_ref[...], preferred_element_type=f32)
            empty = 1.0 - r[:, 512:640]
            for t in range(4):
                cs = slice(128 * t, 128 * t + 128)
                val = r[:, cs] + empty * rows_ref[7:8, cs]
                cells_ref[pl.ds(4 * i, 4), :, cs] = val.astype(bf16).reshape(4, 64, 128)
            return 0
        lax.fori_loop(0, 5, block, 0)

    def fills():
        p_ = pos[0:1, 0:ROWS]
        large = seg((1, ROWS), 1) == jnp.where(first_small, 1, 0)
        target = jnp.where(p_ >= 0, jnp.where(large, p_, 1024 + p_), -1)
        def block(i, _):
            cell = i * 256 + lax.broadcasted_iota(jnp.int32, (256, 1), 0)
            hits[pl.ds(pl.multiple_of(i * 256, 256), 256), :] = (cell == target).astype(f32).astype(bf16)
            return 0
        lax.fori_loop(0, 5, block, 0)

    def cell_grads():
        get_cotangents()
        d = dc[...].reshape(1280, 512)
        dz[...] = lax.dot_general(hits[...], d, TN, preferred_element_type=f32).astype(bf16)
        covered = lax.dot_general(jnp.ones((16, ROWS), bf16), hits[...], NT, preferred_element_type=f32)
        vs[10:11, :] = jnp.dot((1.0 - covered).astype(bf16), d, preferred_element_type=f32)[0:1]
        vs[9:10, :] = jnp.sum(dz[...].astype(f32), axis=0, keepdims=True)
        for n in range(2):
            rs = slice(n * 384, (n + 1) * 384)
            wt = [g_ref[h, 8, :, :, :, 0:256].reshape(768, 256)[rs] for h in range(2)]
            t = lax.dot_general(dz[:, 0:256], wt[0], NT, preferred_element_type=f32)
            t = t + lax.dot_general(dz[:, 256:512], wt[1], NT, preferred_element_type=f32)
            dx[:, rs] = t
            dm[:, rs] = t.astype(bf16)

    kept = dict(rows=(rows_ref, rows_hbm), a=(a_ref, a_hbm), qkv=(qkv_ref, qkv_hbm), p=(p_out, p_hbm), o=(o_ref, o_hbm),
                x2=(x2_ref, x2_hbm), h2=(h2_ref, h2_hbm), act=(act_ref, act_hbm), dact=(dact_ref, dact_hbm), e=(e_ref, e_hbm),
                cells=(cells_ref, cells_hbm), dz=(dz, dz_hbm), dx=(dx, dx_hbm), dm=(dm, dm_hbm), vs=(vs, vs_hbm), inv=(inv, inv_hbm))
    def keep(*names):
        for n in names:
            cp = pltpu.make_async_copy(*kept[n], osem.at[list(kept).index(n)])
            cp.start(); outs.append(cp)

    vs[...] = jnp.zeros_like(vs)
    rows_ref[...] = jnp.zeros_like(rows_ref)
    half = lambda u: ((u, u + 2, 0, LW), (u, u + 1, 0, LW), (u + 1, u + 2, 0, LW))
    pieces = {
        3: [unit_chunk(0, "xz", (8, 9, 0, LW), (8, 9, 0, 256), (8, 9, 256, LW))],
        2: [fc2_chunk(1)],
        0: [unit_chunk(2, "xz", *half(0)), unit_chunk(3, "zx", *half(2))],
        "1a": [unit_chunk(4, "xz", *half(4))],
        "1b": [unit_chunk(5, "zx", *half(6))],
    }
    def go(step, *names):
        for p in names:
            for ch in pieces[p]: ch[step]()
    place(2); go(0, 2)
    shards(0)
    place(3); place(0); go(0, 0, 3)
    go(1, 2, 0, 3)
    shards(1)
    place(1); go(0, "1a", "1b")
    go(2, 0, 3, 2)
    sort_cotangents(); keep("inv")
    send_small_cotangents()
    go(1, "1a", "1b")
    go(3, 2, 0, 3)
    go(2, "1a", "1b")
    go(4, 2)
    send_cotangents()
    fills()
    go(4, 0, 3)
    go(5, 3); to_hbm(3)
    rows_of(); ln1(); keep("rows", "a")
    go(5, 0); to_hbm(0)
    qkv(); keep("qkv")
    go(3, "1a", "1b")
    go(5, 2)
    attention(0, 3)
    go(4, "1a", "1b")
    attention(3, 6)
    keep("p")
    go(6, 2)
    out_proj(); keep("o", "x2", "h2")
    cell_grads(); keep("dz", "dx", "dm", "vs")
    go(5, "1a"); fc1(0)
    go(5, "1b"); to_hbm(1)
    fc1(2); keep("act", "dact")
    go(7, 2); to_hbm(2)
    fc2(); keep("e")
    dec(); keep("cells")
    for _, got in firsts:
        for cp, _ in got: cp.wait_send()
    for cp in sends: cp.wait_send()
    mate.wait_send()
    for cp in tagged: cp.wait_send()
    finish_cotangents()
    for cp in outs: cp.wait()


def k1_call(*args):
    S = jax.ShapeDtypeStruct
    vm, smem = pl.BlockSpec(memory_space=pltpu.VMEM), pl.BlockSpec(memory_space=pltpu.SMEM)
    anyspec = pl.BlockSpec(memory_space=pl.ANY)
    V, DMA = pltpu.VMEM, pltpu.SemaphoreType.DMA
    outs = (
        S((2, 9, 4, 4, 48, LW), bf16), S((2, 4, 4, 4, 48, LW), bf16), S((8, 3072), f32), S((ROWS, 768), bf16),
        S((ROWS, 2304), bf16), S((12, ROWS, ROWS), bf16), S((ROWS, 768), bf16), S((ROWS, 768), f32),
        S((ROWS, 768), bf16), S((ROWS, 3072), bf16), S((ROWS, 3072), bf16), S((ROWS, 768), bf16), S((20, 64, 512), bf16),
        S((ROWS, 512), bf16), S((ROWS, 768), f32), S((ROWS, 768), bf16), S((16, 512), f32), S((8, 128), jnp.int32),
    )
    return pl.pallas_call(
        k1_kernel,
        out_shape=outs,
        in_specs=[smem, smem] + [vm] * 15 + [anyspec] + [vm] * 4,
        out_specs=[anyspec] * 18,
        scratch_shapes=[V(t.shape, t.dtype) for t in outs] + [
            V((2, SROWS, LW), f32), V((2, SROWS, LW), bf16), V((8, YROWS, LW), bf16), V((SROWS - YROWS, LW), bf16), V((ROWS, 640), bf16), V((128, 128), f32),
            V((8, 128), jnp.int32), V((16, 8, 128), jnp.int32), V((32, 128), jnp.int32), pltpu.SMEM((32, 128), jnp.int32),
            V((32, 64, 512), bf16), V((32, 64, 512), bf16), V((20, 64, 512), bf16), V((1280, ROWS), bf16),
            DMA((3, 7)), DMA((3, 7)), DMA((2,)), DMA((6, 16)), DMA((6, 16)), DMA((4,)), DMA((16,)), DMA((16,)), DMA((16,)),
            DMA((16,)), DMA((16,)), DMA((16,)), DMA((4,)), DMA((4,)),
        ],
        compiler_params=pltpu.CompilerParams(collective_id=0, has_side_effects=True, vmem_limit_bytes=60 * 2**20),
        cost_estimate=pl.CostEstimate(flops=6 * 10**9, bytes_accessed=5 * 10**7, transcendentals=0),
        name="forward",
    )(*args, jnp.asarray(spread_matrix((4, 5, 6, 7), 0).T, bf16), jnp.asarray(spread_matrix((0, 1, 2, 3, 8), 32).T, bf16),
      jnp.asarray(cell_spread(), bf16), jnp.asarray(fc1_bias_spread(), bf16))


def k2_kernel(g_hbm, g2_hbm, rows_hbm, a_hbm, qkv_hbm, p_hbm, o_hbm, x2_hbm, h2_hbm, act_hbm, dact_hbm, e_hbm, cells_hbm,
              dz_hbm, dx_hbm, dm_hbm, vs_hbm, tok_hbm, pt1_ref, pt2_ref, m2_ref, m4_ref,
              tg_ref, arr, oq_ref, oo_ref, of1_ref, of2_ref, od_ref, v0_ref, v1_ref, v2_ref, v3_ref, v4_ref, vf_ref, vd_ref, vm_ref,
              rows_ref, a_ref, qkv_ref, o_ref, x2_ref, h2_ref, act_ref, dact_ref, e_ref, dz, dx, dm, vs, tok,
              wa, wb, sta, sta2, stc, sg, sg2, acc, acc2, xa, xa2, xb, xc, xd,
              dh, df, dqkv, vsum, pb, fs, f1, fo, fs2, f2, zb, vt, vout, vin,
              ssem, rsem, ss1, rs1, loc, wsem, psem, tsem, isem, css, csr, csl, vss, vrs):
    z, x, y, c = coords()
    dp, f = lax.axis_index("dp"), lax.axis_index("fsdp")
    o = 1 - c
    bar = pltpu.get_barrier_semaphore()
    rings = ring_places(z, x, y, c)
    targets = [rings[a][1][d] for a in "zx" for d in (1, -1)]
    sib = dev(z, x, y, o)
    group = []
    for dy in range(4):
        for dc in range(2):
            if dy or dc:
                group.append((dy, dc, dev(z, x, (y + dy) % 4, (c + dc) % 2)))
    plane = [(4 * dz_ + dx_, (z + dz_) % 4, (x + dx_) % 4, (z + 4 - dz_) % 4, (x + 4 - dx_) % 4)
             for dz_ in range(4) for dx_ in range(4) if dz_ or dx_]
    greeted = targets + [(dp, g) for _, g in peers(f)] + [dev(zz, xx, y, c) for _, zz, xx, _, _ in plane]
    greet(bar, greeted)
    loads = {}
    def load(name, src, dst):
        loads[name] = pltpu.make_async_copy(src, dst, isem.at[len(loads)])
        return loads[name]
    for name, src, dst in (
        ("dm", dm_hbm, dm), ("act", act_hbm, act_ref), ("e", e_hbm, e_ref), ("dz", dz_hbm, dz), ("fc2", g2_hbm, wa), ("dact", dact_hbm, dact_ref), ("fc1", g_hbm.at[:, 4:8], wb),
        ("h2", h2_hbm, h2_ref), ("x2", x2_hbm, x2_ref), ("dx", dx_hbm, dx), ("rows", rows_hbm, rows_ref), ("o", o_hbm, o_ref),
        ("qkv", qkv_hbm, qkv_ref), ("a", a_hbm, a_ref), ("tok", tok_hbm.at[0:ROWS], tok),
        ("vs", vs_hbm, vs),
    ):
        load(name, src, dst).start()
    def need(*names):
        for n in names: loads[n].wait()
    ld_c = pltpu.make_async_copy(g_hbm.at[:, 0:4], wb, wsem.at[0])
    zb[...] = jnp.zeros_like(zb)
    vt[...] = jnp.zeros_like(vt)
    vsum[...] = jnp.zeros_like(vsum)
    pl.semaphore_wait(bar, len(greeted))

    few = f < 4
    def cells_to(i, g):
        return pltpu.make_async_remote_copy(cells_hbm.at[g], arr.at[f], css.at[i], csr.at[i], device_id=(dp, g), device_id_type=MESH)
    def small_cells_to(i, g):
        return pltpu.make_async_remote_copy(cells_hbm.at[16 + g % 4], arr.at[16 + f], css.at[16 + i], csr.at[16 + i], device_id=(dp, g), device_id_type=MESH)
    locals_ = [pltpu.make_async_copy(cells_hbm.at[f], arr.at[f], csl.at[0]), pltpu.make_async_copy(zb, arr.at[32], csl.at[1])]
    own_small = pltpu.make_async_copy(cells_hbm.at[16 + f % 4], arr.at[16 + f], csl.at[2])
    for l in locals_: l.start()
    for r, g in peers(f):
        cells_to(r, g).start()
        @pl.when(g < 4)
        def _():
            small_cells_to(r, g).start()
    @pl.when(few)
    def _():
        own_small.start()
    def finish_cells():
        for l in locals_: l.wait()
        for r, g in peers(f):
            src = (f + 16 - r) % 16
            pltpu.make_async_remote_copy(cells_hbm.at[g], arr.at[src], css.at[r], csr.at[r], device_id=(dp, g), device_id_type=MESH).wait_recv()
            cells_to(r, g).wait_send()
            @pl.when(g < 4)
            def _():
                small_cells_to(r, g).wait_send()
        @pl.when(few)
        def _():
            own_small.wait()
            for r, g in peers(f):
                src = (f + 16 - r) % 16
                pltpu.make_async_remote_copy(cells_hbm.at[16], arr.at[16 + src], css.at[16 + r], csr.at[16 + r], device_id=(dp, g), device_id_type=MESH).wait_recv()

    sends = {}
    def send(k, i, src, dst, to):
        cp = pltpu.make_async_remote_copy(src, dst, ssem.at[k, i], rsem.at[k, i], device_id=to, device_id_type=MESH)
        cp.start(); sends[k, i] = cp
    def recv(k, i, v):
        pltpu.make_async_remote_copy(v, v, ssem.at[k, i], rsem.at[k, i], device_id=sib, device_id_type=MESH).wait_recv()

    def steps(k, axes, ours, theirs, from_sib, inbox, parts):
        last = len(axes) - 1
        def add(v, *more):
            t = v[...].astype(f32)
            for m in more: t = t + m[...].astype(f32)
            v[...] = t.astype(bf16)
        def opposite(l):
            at, to = rings[axes[l]]
            _, fa, fb = parts[l]
            send(k, 4 * l, ours(l, at[2], fa), inbox(l, 0, fa), to[1])
            if fb is not None: send(k, 4 * l + 1, ours(l, at[2], fb), inbox(l, 0, fb), to[-1])
        def start():
            send(k, 12, theirs, from_sib, sib)
        def join():
            recv(k, 12, from_sib)
            at, _ = rings[axes[last]]
            for d in (2, 1, -1, 0):
                add(ours(last, at[d], parts[last][0]), share(last, at[d]))
                if d == 2: opposite(last)
        def share(l, place):
            return from_sib_view[k](place)
        def near(l):
            at, to = rings[axes[l]]
            full, fa, fb = parts[l]
            recv(k, 4 * l, inbox(l, 0, fa)); add(ours(l, at[1], fa), inbox(l, 0, fa))
            send(k, 4 * l + 2, ours(l, at[1], full), inbox(l, 1, full), to[1])
            if fb is not None:
                recv(k, 4 * l + 1, inbox(l, 0, fb)); add(ours(l, at[-1], fb), inbox(l, 0, fb))
            send(k, 4 * l + 3, ours(l, at[-1], full), inbox(l, 2, full), to[-1])
        def here(l):
            at, to = rings[axes[l]]
            full = parts[l][0]
            recv(k, 4 * l + 2, inbox(l, 1, full)); recv(k, 4 * l + 3, inbox(l, 2, full))
            add(ours(l, at[0], full), inbox(l, 1, full), inbox(l, 2, full))
            if l: opposite(l - 1)
        out = [start, join]
        for l in range(last, -1, -1):
            out += [functools.partial(near, l), functools.partial(here, l)]
        return out

    from_sib_view = {}
    def unit_chunk(k, axes, staged, *parts):
        def at_level(l, at):
            return [(z, at), (at, ALL)][l] if axes == "xz" else [(at, x), (ALL, at)][l]
        def cut(ref, part, l, at):
            u0, u1, l0, l1 = part
            zs, xs = at_level(l, at)
            return ref.at[u0:u1, zs, xs, :, l0:l1]
        def inbox(l, way, part):
            u0, u1, l0, l1 = part
            return xb.at[way, u0:u1, :, l0:l1] if l == 0 else xa.at[way, u0:u1, :, :, l0:l1]
        u0, u1, l0, l1 = parts[0]
        from_sib_view[k] = lambda place: cut(sg, parts[0], 1, place)
        return steps(k, axes, lambda l, at, part: cut(acc, part, l, at), staged, sg.at[u0:u1, :, :, :, l0:l1], inbox, [parts, parts])
    def fc2_chunk(k):
        def ours(l, at, part):
            a, b = part
            if l == 0: return acc2.at[z, at, y, a:b]
            if l == 1: return acc2.at[at, a:b, y]
            return acc2.at[a:b, :, at]
        def inbox(l, way, part):
            a, b = part
            return (xd, xc, xa2)[l].at[way, a:b]
        ring = ((0, 4), (0, 2), (2, 4))
        from_sib_view[k] = lambda place: sg2.at[:, :, place]
        return steps(k, "xzy", ours, sta2, sg2, inbox, [((0, 48), (0, 32), (32, 48)), ring, ring])

    lanes = lambda u, l0, lm, l1: ((u, u + 1, l0, l1), (u, u + 1, l0, lm), (u, u + 1, lm, l1))
    pair = lambda u: ((u, u + 2, 0, LW), (u, u + 1, 0, LW), (u + 1, u + 2, 0, LW))
    table = {
        "fc2": fc2_chunk(0),
        "dec": unit_chunk(1, "xz", stc.at[:, :, :, :, 0:256], *lanes(8, 0, 128, 256)),
        "f1a": unit_chunk(2, "xz", sta.at[0:2], *pair(4)),
        "f1b": unit_chunk(3, "xz", sta.at[2:4], *pair(6)),
        "out": unit_chunk(4, "zx", sta.at[3:4], *lanes(3, 0, 256, LW)),
        "q0": unit_chunk(5, "xz", sta.at[0:1], *lanes(0, 0, 256, LW)),
        "q1": unit_chunk(6, "zx", sta.at[1:2], *lanes(1, 0, 256, LW)),
        "q2": unit_chunk(8, "xz", sta.at[2:3, :, :, :, 0:256], *lanes(2, 0, 128, 256)),
        "q3": unit_chunk(9, "zx", sta.at[2:3, :, :, :, 256:LW], (2, 3, 256, LW), (2, 3, 256, LW), None),
    }
    def st(s, *names):
        for n in names: table[n][s]()

    def send_small(v):
        vout[...] = v.reshape(4, 4, 48, 128)
        vin[4 * z + x] = vout[z, x]
        for i, zz, xx, _, _ in plane:
            cp = pltpu.make_async_remote_copy(vout.at[zz, xx], vin.at[4 * z + x], vss.at[i], vrs.at[i], device_id=dev(zz, xx, y, c), device_id_type=MESH)
            cp.start(); lasts.append(cp)
    def sum_small():
        for i, zz, xx, sz, sx in plane:
            pltpu.make_async_remote_copy(vout.at[zz, xx], vin.at[4 * sz + sx], vss.at[i], vrs.at[i], device_id=dev(zz, xx, y, c), device_id_type=MESH).wait_recv()
        acc[8, z, x, :, 256:LW] = jnp.sum(vin[...].astype(f32), axis=0).astype(bf16)

    lasts = []
    me = 2 * y + c
    def last_exchange(j, pt, units):
        rs_ = slice(32 * j, 32 * j + 32)
        blk = jnp.concatenate([acc[u, z, x] for u in units], axis=0)
        fs[:, rs_] = jnp.dot(pt[...], blk, preferred_element_type=f32).astype(bf16).reshape(8, 32, LW)
        own = pltpu.make_async_copy(fs.at[me, rs_], f1.at[me, rs_], loc.at[j])
        own.start()
        got = []
        for i, (dy, dc, t) in enumerate(group):
            dst = 2 * ((y + dy) % 4) + (c + dc) % 2
            cp = pltpu.make_async_remote_copy(fs.at[dst, rs_], f1.at[me, rs_], ss1.at[j, i], rs1.at[j, i], device_id=t, device_id_type=MESH)
            cp.start()
            src = 2 * ((y + 4 - dy) % 4) + (c + dc) % 2
            rc = pltpu.make_async_remote_copy(fs.at[me, rs_], f1.at[src, rs_], ss1.at[j, i], rs1.at[j, i], device_id=t, device_id_type=MESH)
            lasts.append(cp); got.append(rc)
        def finish():
            own.wait()
            for rc in got: rc.wait_recv()
            for h in range(2):
                t = f1[h, rs_].astype(f32)
                for yy in range(1, 4): t = t + f1[2 * yy + h, rs_].astype(f32)
                fo[h, rs_] = t
        return finish
    def fc2_exchange():
        v = acc2[z, x, y].astype(f32)
        pad = jnp.zeros((8, LW), f32)
        for k in range(2):
            fs2[k] = jnp.concatenate([v[24 * k:24 * k + 24], pad], axis=0).astype(bf16)
        cp = pltpu.make_async_remote_copy(fs2.at[o], f2, ss1.at[0, 7], rs1.at[0, 7], device_id=sib, device_id_type=MESH)
        cp.start(); lasts.append(cp)
        of2_ref[:, pl.ds(pl.multiple_of(c * LW, LW), LW)] = jnp.where(c == 0, v[0:24], v[24:48])
        def finish():
            cp.wait_recv()
            of2_ref[:, pl.ds(pl.multiple_of(o * LW, LW), LW)] = f2[...].astype(f32)[0:24]
        return finish

    def blocks(body, n=7):
        def step(i, _):
            body(pl.ds(pl.multiple_of(i * 48, 48), 48)); return 0
        lax.fori_loop(0, n, step, 0)
    def col(base, width, unit):
        return pl.ds(pl.multiple_of(base, unit), width)

    def grad_fc2(h, dst):
        def part(i, _):
            t = lax.dot_general(act_ref[:, col(i * 768, 768, 768)], dm[:, col(h * LW, LW, LW)], TN, preferred_element_type=f32)
            dst[i] = t.astype(bf16).reshape(4, 4, 48, LW)
            return 0
        lax.fori_loop(0, 4, part, 0)

    def fc2_back():
        def part(i, _):
            cs = col(i * 768, 768, 768)
            t = lax.dot_general(dm[:, 0:LW], wa[0, i].reshape(768, LW), NT, preferred_element_type=f32)
            t = t + lax.dot_general(dm[:, LW:768], wa[1, i].reshape(768, LW), NT, preferred_element_type=f32)
            t = (t * dact_ref[:, cs].astype(f32)).astype(bf16)
            df[:, cs] = t
            vsum[5:6, cs] = jnp.sum(t.astype(f32), axis=0, keepdims=True)
            return 0
        lax.fori_loop(0, 4, part, 0)

    def wunit(h, u):
        return wb[h, u].reshape(768, LW)
    def fc1_back():
        for h in range(2):
            wt = lambda r: jnp.concatenate([wunit(h, u)[r] for u in range(4)], axis=1)
            for n in range(2):
                rs = slice(n * 384, (n + 1) * 384)
                t = lax.dot_general(df[:, h * 1536:(h + 1) * 1536], wt(rs), NT, preferred_element_type=f32)
                dh[:, rs] = t if h == 0 else dh[:, rs] + t

    def grad_fc1(h, dst, base):
        def part(u, _):
            t = lax.dot_general(h2_ref[...], df[:, col(h * 1536 + u * LW, LW, LW)], TN, preferred_element_type=f32)
            dst[base + u] = t.astype(bf16).reshape(4, 4, 48, LW)
            return 0
        lax.fori_loop(0, 4, part, 0)

    def norm_back(src, gain_row, into, out_lo, base):
        gain = rows_ref[gain_row:gain_row + 1, 0:768]
        def body(r):
            n, rstd = stats(src[r, :].astype(f32))
            d = dh[r, :]
            vsum[base:base + 1, 0:768] += jnp.sum(d * n, axis=0, keepdims=True)
            vsum[base + 1:base + 2, 0:768] += jnp.sum(d, axis=0, keepdims=True)
            dn = d * gain
            t = rstd * (dn - jnp.mean(dn, axis=-1, keepdims=True) - n * jnp.mean(dn * n, axis=-1, keepdims=True))
            t = dx[r, :] + t
            into[r, :] = t
            if out_lo is not None: out_lo[r, :] = t.astype(bf16)
        blocks(body)

    def out_back():
        t = lax.dot_general(dm[:, 0:LW], wunit(0, 3), NT, preferred_element_type=f32)
        t = t + lax.dot_general(dm[:, LW:768], wunit(1, 3), NT, preferred_element_type=f32)
        df[:, 0:768] = t.astype(bf16)

    def load_p(i):
        return pltpu.make_async_copy(p_hbm.at[pl.ds(2 * (i // 2 + 3 * (i % 2)), 2)], pb.at[i % 2], psem.at[i % 2])

    def attn_back(u):
        low = lax.broadcasted_iota(jnp.int32, (1, 128), 1) < 64
        def pair(j, _):
            load_p(2 * u + j).wait()
            i = u + 3 * j
            def cols(b):
                return qkv_ref[:, col(LW * i + 128 * b, 128, 128)]
            q, kk, v, do = cols(0), cols(1), cols(2), df[:, col(i * 128, 128, 128)]
            r = []
            for t in range(2):
                keep = low if t == 0 else jnp.logical_not(low)
                pr = pb[j, t]
                dp = lax.dot_general(jnp.where(keep, do, jnp.zeros_like(do)), v, NT, preferred_element_type=f32)
                p32 = pr.astype(f32)
                ds = (p32 * (dp - jnp.sum(dp * p32, axis=-1, keepdims=True))).astype(bf16)
                dv = lax.dot_general(pr, do, TN, preferred_element_type=f32)
                dq = jnp.dot(ds, kk, preferred_element_type=f32)
                dk = lax.dot_general(ds, q, TN, preferred_element_type=f32)
                r.append((0.125 * dq, 0.125 * dk, dv))
            for b in range(3):
                dqkv[:, col(LW * i + 128 * b, 128, 128)] = jnp.where(low, r[0][b], r[1][b]).astype(bf16)
            if u < 2: load_p(2 * u + j + 2).start()
            return 0
        lax.fori_loop(0, 2, pair, 0)

    def qkv_back():
        for h in range(2):
            wt = lambda r: jnp.concatenate([wunit(h, u)[r] for u in range(3)], axis=1)
            for n in range(2):
                rs = slice(n * 384, (n + 1) * 384)
                t = lax.dot_general(dqkv[:, h * 1152:(h + 1) * 1152], wt(rs), NT, preferred_element_type=f32)
                dh[:, rs] = t if h == 0 else dh[:, rs] + t

    def grad_qkv(u, h, dst):
        t = lax.dot_general(a_ref[...], dqkv[:, col(h * 1152 + u * LW, LW, LW)], TN, preferred_element_type=f32)
        dst[u] = t.astype(bf16).reshape(4, 4, 48, LW)
    def grad_out(h, dst):
        t = lax.dot_general(o_ref[...], dm[:, col(h * LW, LW, LW)], TN, preferred_element_type=f32)
        dst[3] = t.astype(bf16).reshape(4, 4, 48, LW)

    def vec_cols():
        rt = jnp.concatenate([vsum[0:8, 0:768], jnp.zeros((120, 768), f32)], axis=0)
        srow = lax.broadcasted_iota(jnp.int32, (128, 768), 0)
        rt = jnp.where(srow < 5, rt, 0.0)
        v = rt.T
        r2 = jnp.concatenate([vsum[0:16, 0:512], jnp.zeros((112, 512), f32)], axis=0)
        srow2 = lax.broadcasted_iota(jnp.int32, (128, 512), 0)
        r2 = jnp.where((srow2 == 9) | (srow2 == 10), r2, 0.0).astype(bf16)
        v = v + lax.dot_general(m2_ref[...], r2, NT, preferred_element_type=f32)
        lane = (lax.broadcasted_iota(jnp.int32, (128, 768), 1) % 24) // 6
        parts = []
        for s in range(4):
            wrow = jnp.broadcast_to(vsum[5:6, 768 * s:768 * s + 768], (128, 768))
            wt = jnp.where(srow - 5 == lane, wrow, 0.0).astype(bf16)
            parts.append(lax.dot_general(m4_ref[...], wt, NT, preferred_element_type=f32))
        return (v + jnp.concatenate(parts, axis=0)).astype(bf16)

    def grad_dec(h, dst_store):
        t = lax.dot_general(e_ref[...], dz[:, col(h * 256, 256, 256)], TN, preferred_element_type=f32)
        dst_store(t.astype(bf16).reshape(4, 4, 48, 256), slice(0, 256))

    def acc8(v, cs): acc[8, :, :, :, cs] = v
    def stc8(v, cs): stc[0, :, :, :, cs] = v

    need("dm", "act")
    grad_fc2(o, sta2); st(0, "fc2")
    grad_fc2(c, acc2)
    vsum[4:5, 0:768] = jnp.sum(dm[...].astype(f32), axis=0, keepdims=True)
    need("e", "dz")
    grad_dec(o, stc8); st(0, "dec")
    grad_dec(c, acc8)
    need("fc2", "dact")
    fc2_back()
    st(1, "fc2", "dec")
    need("h2")
    grad_fc1(o, sta, 0); st(0, "f1a", "f1b")
    grad_fc1(c, acc, 4)
    st(2, "dec")
    need("fc1")
    fc1_back()
    ld_c.start()
    load_p(0).start(); load_p(1).start()
    st(1, "f1a", "f1b")
    need("x2", "dx", "rows")
    norm_back(x2_ref, 2, dx, dm, 2)
    ld_c.wait()
    for kk in (2, 3): sends[kk, 12].wait_send(); del sends[kk, 12]
    need("o", "qkv")
    grad_out(o, sta); st(0, "out")
    grad_out(c, acc)
    out_back()
    st(3, "dec"); st(1, "out")
    need("a")
    attn_back(0)
    st(2, "f1a", "f1b")
    grad_qkv(0, o, sta); st(0, "q0"); grad_qkv(0, c, acc)
    st(2, "fc2"); st(2, "out"); st(4, "dec")
    attn_back(1)
    st(3, "out"); st(5, "dec"); st(1, "q0")
    grad_qkv(1, o, sta); st(0, "q1"); grad_qkv(1, c, acc)
    st(3, "f1a", "f1b")
    attn_back(2)
    st(2, "q0"); st(1, "q1"); st(3, "fc2")
    grad_qkv(2, o, sta); st(0, "q2", "q3"); grad_qkv(2, c, acc)
    st(4, "out", "f1a", "f1b"); st(3, "q0"); st(4, "fc2")
    qkv_back()
    st(1, "q2", "q3"); st(2, "q1"); st(5, "out", "f1a", "f1b", "fc2")
    finish_first = last_exchange(0, pt1_ref, (4, 5, 6, 7))
    need("tok", "vs")
    vsum[9:11, 0:512] = vs[9:11, :]
    norm_back(tok, 0, dx, None, 0)
    st(2, "q2", "q3")
    send_small(vec_cols())
    dh[0:512 - ROWS, :] = jnp.zeros((512 - ROWS, 768), f32)
    tgs = [pltpu.make_async_copy(dx, tg_ref.at[0:ROWS], tsem.at[0]), pltpu.make_async_copy(dh.at[0:512 - ROWS], tg_ref.at[ROWS:512], tsem.at[1])]
    for t in tgs: t.start()
    st(3, "q1"); st(4, "q0"); st(6, "fc2")
    st(3, "q2", "q3"); st(5, "q0"); st(4, "q1"); st(7, "fc2")
    finish_fc2 = fc2_exchange()
    st(4, "q2", "q3"); st(5, "q1")
    sum_small()
    finish_fc2(); finish_first()
    st(5, "q2", "q3")
    finish_second = last_exchange(1, pt2_ref, (0, 1, 2, 3, 8))
    for h in range(2):
        for u in range(4):
            of1_ref[:, h * 1536 + u * LW:h * 1536 + (u + 1) * LW] = fo[h, 6 * u:6 * u + 6, :]
    finish_second()
    for h in range(2):
        for u in range(3):
            for b in range(3):
                first = 768 * b + 128 * (3 * h + u)
                oq_ref[:, first:first + 128] = fo[h, 32 + 6 * u:38 + 6 * u, 128 * b:128 * b + 128]
        oo_ref[:, h * LW:(h + 1) * LW] = fo[h, 50:56, :]
        od_ref[:, h * 256:(h + 1) * 256] = fo[h, 56:62, 0:256]
    vt[0:6, :] = fo[0, 56:62, 256:384] + fo[1, 56:62, 256:384]
    vrows = vt[...].T
    for i, r in enumerate((v0_ref, v1_ref, v2_ref, v3_ref, v4_ref)):
        r[...] = vrows[i:i + 1, 0:6]
    for q in range(4):
        vf_ref[:, 6 * q:6 * q + 6] = vrows[5 + q:6 + q, 0:6]
    vd_ref[...] = vrows[9:10, 0:4]
    vm_ref[...] = vrows[10:11, 0:4]
    finish_cells()
    for t in tgs: t.wait()
    for cp in lasts: cp.wait_send()
    for cp in sends.values(): cp.wait_send()


def k2_call(*args):
    S = jax.ShapeDtypeStruct
    vm = pl.BlockSpec(memory_space=pltpu.VMEM)
    anyspec = pl.BlockSpec(memory_space=pl.ANY)
    V, DMA = pltpu.VMEM, pltpu.SemaphoreType.DMA
    outs = (S((512, 768), f32), S((33, 64, 512), bf16), S((6, 2304), f32), S((6, 768), f32), S((6, 3072), f32), S((24, 768), f32),
            S((6, 512), f32)) + (S((1, 6), f32),) * 5 + (S((1, 24), f32), S((1, 4), f32), S((1, 4), f32))
    return pl.pallas_call(
        k2_kernel,
        out_shape=outs,
        in_specs=[anyspec] * 18 + [vm] * 4,
        out_specs=[anyspec] * 2 + [vm] * 13,
        scratch_shapes=[
            V((8, 3072), f32), V((ROWS, 768), bf16), V((ROWS, 2304), bf16), V((ROWS, 768), bf16), V((ROWS, 768), f32),
            V((ROWS, 768), bf16), V((ROWS, 3072), bf16), V((ROWS, 3072), bf16), V((ROWS, 768), bf16), V((ROWS, 512), bf16),
            V((ROWS, 768), f32), V((ROWS, 768), bf16), V((16, 512), f32), V((ROWS, 768), bf16),
            V((2, 4, 4, 4, 48, LW), bf16), V((2, 4, 4, 4, 48, LW), bf16),
            V((4, 4, 4, 48, LW), bf16), V((4, 4, 4, 48, LW), bf16), V((1, 4, 4, 48, LW), bf16),
            V((9, 4, 4, 48, LW), bf16), V((4, 4, 4, 48, LW), bf16),
            V((9, 4, 4, 48, LW), bf16), V((4, 4, 4, 48, LW), bf16),
            V((3, 9, 4, 48, LW), bf16), V((3, 4, 4, 48, LW), bf16),
            V((3, 9, 48, LW), bf16), V((3, 4, 48, LW), bf16), V((3, 48, LW), bf16),
            V((ROWS, 768), f32), V((ROWS, 3072), bf16), V((ROWS, 2304), bf16), V((16, 3072), f32), V((2, 2, ROWS, ROWS), bf16),
            V((8, YROWS, LW), bf16), V((8, YROWS, LW), bf16), V((2, YROWS, LW), f32), V((2, 32, LW), bf16), V((32, LW), bf16), V((64, 512), bf16), V((128, 128), f32), V((4, 4, 48, 128), bf16), V((16, 48, 128), bf16),
            DMA((10, 13)), DMA((10, 13)), DMA((2, 8)), DMA((2, 8)), DMA((2,)), DMA((1,)), DMA((2,)), DMA((2,)), DMA((16,)),
            DMA((32,)), DMA((32,)), DMA((3,)), DMA((16,)), DMA((16,)),
        ],
        compiler_params=pltpu.CompilerParams(collective_id=1, has_side_effects=True, vmem_limit_bytes=60 * 2**20),
        cost_estimate=pl.CostEstimate(flops=12 * 10**9, bytes_accessed=5 * 10**7, transcendentals=0),
        name="backward",
    )(*args, jnp.asarray(spread_matrix((4, 5, 6, 7), 0), bf16), jnp.asarray(spread_matrix((0, 1, 2, 3, 8), 32), bf16),
      jnp.asarray(cell_spread(), bf16), jnp.asarray(fc1_bias_spread(), bf16))


def k3_kernel(inv, arr, tg, *refs):
    n = len(refs) - 3
    small, (grid, tg_out, *outs), (gv, tv, sem) = refs[:13], refs[13:n], refs[n:]
    ins = [pltpu.make_async_copy(tg, tv, sem.at[0])]
    ins += [pltpu.make_async_copy(arr.at[inv[0, r]], gv.at[r], sem.at[1 + r]) for r in range(32)]
    for cp in ins: cp.start()
    for a, b in zip(small, outs): b[...] = a[...]
    back = [pltpu.make_async_copy(tv, tg_out, sem.at[33])]
    back += [pltpu.make_async_copy(gv.at[pl.ds(8 * i, 8)], grid.at[pl.ds(8 * i, 8)], sem.at[34 + i]) for i in range(4)]
    ins[0].wait()
    back[0].start()
    for i in range(4):
        for r in range(8): ins[1 + 8 * i + r].wait()
        back[1 + i].start()
    for cp in back: cp.wait()


def k3_call(inv, arr, tg, *small):
    S = jax.ShapeDtypeStruct
    vm = pl.BlockSpec(memory_space=pltpu.VMEM)
    anyspec = pl.BlockSpec(memory_space=pl.ANY)
    return pl.pallas_call(
        k3_kernel,
        out_shape=(S((32, 64, 512), bf16), S((512, 768), f32)) + tuple(S(t.shape, t.dtype) for t in small),
        in_specs=[pl.BlockSpec(memory_space=pltpu.SMEM), anyspec, anyspec] + [vm] * 13,
        out_specs=[anyspec, anyspec] + [vm] * 13,
        scratch_shapes=[pltpu.VMEM((32, 64, 512), bf16), pltpu.VMEM((512, 768), f32), pltpu.SemaphoreType.DMA((38,))],
        name="results",
    )(inv, arr, tg, *small)


def body(tokens, chip_lengths, chip_ids, positions, ln1_gain, ln1_bias, qkv_weight, out_weight, ln2_gain, ln2_bias, fc1_weight,
         fc1_bias, fc2_weight, fc2_bias, dec_weight, dec_bias, mask_token, grid_cotangent):
    row = lambda v: v.reshape(1, -1)
    *saved, inv = k1_call(chip_ids, chip_lengths, row(positions), tokens, row(ln1_gain), row(ln1_bias), qkv_weight, out_weight,
                          row(ln2_gain), row(ln2_bias), fc1_weight, row(fc1_bias), fc2_weight, row(fc2_bias), dec_weight,
                          row(dec_bias), row(mask_token), grid_cotangent)
    tg, arrived, *small = k2_call(*saved, tokens)
    grid, tg, dq, do, df1, df2, dd, *v = k3_call(inv, arrived, tg, *small)
    v = [t.reshape(-1) for t in v]
    return (grid, tg, v[0], v[1], dq, do, v[2], v[3], df1, v[5], df2, v[4], dd, v[6], v[7])


def solution(mesh):
    both = ("dp", "fsdp")
    r1, r2, grid = P(both), P(both, None), P("dp", "fsdp", None)
    weights = (r1, r1, r2, r2, r1, r1, r2, r1, r2, r1, r2, r1, r1)
    return jax.shard_map(body, mesh=mesh, in_specs=(r2, r1, r1, r1) + weights + (grid,), out_specs=(grid, r2) + weights,
                         check_vma=False)
```

```python
import functools
import numpy as np
import jax, jax.numpy as jnp
from jax import lax
from jax.experimental import pallas as pl
from jax.experimental.pallas import tpu as pltpu
from jax.sharding import PartitionSpec as P

MESH = pl.DeviceIdType.MESH
LW = 384
SROWS = 96
YROWS = 64

def coords():
    dp = lax.axis_index("dp"); fs = lax.axis_index("fsdp")
    z = dp // 2
    x = (dp % 2) * 2 + fs // 8
    y = (fs % 8) // 2
    c = fs % 2
    return z, x, y, c

def dev(z, x, y, c):
    return (z * 2 + x // 2, (x % 2) * 8 + y * 2 + c)

UNIT_ROWS = (32, 38, 44, 50, 0, 6, 12, 18, 56)
FC2_ROWS = 64


def perm_matrix():
    m = np.zeros((432, 512), np.float32)
    for u, base in enumerate(UNIT_ROWS):
        for d in range(8):
            for j in range(6):
                m[48 * u + 6 * d + j, d * 64 + base + j] = 1
    return m


def spread_matrix(units, first):
    m = perm_matrix().reshape(9, 48, 8, 64)[list(units), :, :, first:first + 32]
    return m.reshape(48 * len(units), 256).T


ALL = slice(None)


def ring_places(z, x, y, c):
    out = {}
    for name, v in (("z", z), ("x", x), ("y", y)):
        at = {0: v, 1: (v + 1) % 4, -1: (v + 3) % 4, 2: (v + 2) % 4}
        to = {k: dev(*(at[k] if n == name else w for n, w in (("z", z), ("x", x), ("y", y))), c) for k in (1, -1)}
        out[name] = (at, to)
    return out


ROWS = 336
HEADS_PAIRS = 6
D = 768
NT = (((1,), (1,)), ((), ()))
TN = (((0,), (0,)), ((), ()))
f32, bf16 = jnp.float32, jnp.bfloat16


def cell_spread():
    m = np.zeros((768, 512), np.float32)
    for d in range(128):
        for j in range(4):
            m[6 * d + j, 4 * d + j] = 1
    return m


def fc1_bias_spread():
    m = np.zeros((192, 768), np.float32)
    n = np.arange(768)
    m[6 * (n // 24) + n % 6, n] = 1
    return m


def peers(f):
    return [(r, (f + r) % 16) for r in range(1, 16)]


def greet(bar, devices):
    for t in devices:
        pl.semaphore_signal(bar, inc=1, device_id=t, device_id_type=MESH)


def stats(v):
    mean = jnp.mean(v, axis=-1, keepdims=True)
    center = v - mean
    rstd = lax.rsqrt(jnp.mean(center * center, axis=-1, keepdims=True) + 1e-6)
    return center * rstd, rstd


def gelu_pair(f):
    cdf = 0.5 * (1.0 + lax.erf(f * 0.7071067811865476))
    pdf = 0.3989422804014327 * jnp.exp(-0.5 * f * f)
    return f * cdf, cdf + f * pdf


def k1_kernel(ids, lens, pos, tok, l1g, l1b, qkv_s, out_s, l2g, l2b, fc1_s, fc1b, fc2_s, fc2b, dec_s, decb, maskt, cot_hbm,
              p1_ref, p2_ref, m2_ref, m4_ref,
              g_hbm, g2_hbm, rows_hbm, a_hbm, qkv_hbm, p_hbm, o_hbm, x2_hbm, h2_hbm, act_hbm, dact_hbm, e_hbm, cells_hbm,
              dz_hbm, dx_hbm, dm_hbm, vs_hbm, inv_hbm,
              g_ref, g2_ref, rows_ref, a_ref, qkv_ref, p_out, o_ref, x2_ref, h2_ref, act_ref, dact_ref, e_ref, cells_ref,
              dz, dx, dm, vs, inv,
              sp, s_ref, s1, s2, z_ref, vrow, tag, tags, idv, idm, cot, cotsend, dc, hits,
              ss1, rs1, loc, ssem, rsem, wsem, osem, tss, tsr, bss, bsr, mss, msr, lsem):
    z, x, y, c = coords()
    dp, f = lax.axis_index("dp"), lax.axis_index("fsdp")
    o = 1 - c
    bar = pltpu.get_barrier_semaphore()
    rings = ring_places(z, x, y, c)
    targets = [rings[a][1][d] for a in "zx" for d in (1, -1)]
    group = []
    for dy in range(4):
        for dc_ in range(2):
            if dy or dc_:
                group.append((dy, dc_, dev(z, x, (y + dy) % 4, (c + dc_) % 2)))
    greeted = targets + [(dp, g) for _, g in peers(f)]
    greet(bar, greeted)
    ld_cot = pltpu.make_async_copy(cot_hbm, cot, lsem.at[0])
    ld_cot.start()

    sp[...] = jnp.zeros_like(sp)
    for h in range(2):
        for u in range(3):
            for b in range(3):
                first = 768 * b + 128 * (3 * h + u)
                sp[h, 32 + 6 * u:38 + 6 * u, 128 * b:128 * b + 128] = qkv_s[:, first:first + 128].astype(f32)
        sp[h, 50:56, :] = out_s[:, h * LW:(h + 1) * LW].astype(f32)
        for u in range(4):
            sp[h, 6 * u:6 * u + 6, :] = fc1_s[:, h * 1536 + u * LW:h * 1536 + (u + 1) * LW].astype(f32)
        sp[h, 64:88, :] = fc2_s[:, h * LW:(h + 1) * LW].astype(f32)
        sp[h, 56:62, 0:256] = dec_s[:, h * 256:(h + 1) * 256].astype(f32)
    vrow[...] = jnp.zeros_like(vrow)
    for i, r in enumerate((l1g, l1b, l2g, l2b, fc2b)):
        vrow[i:i + 1, 0:6] = r[...].astype(f32)
    for q in range(4):
        vrow[5 + q:6 + q, 0:6] = fc1b[:, 6 * q:6 * q + 6].astype(f32)
    vrow[9:10, 0:4] = decb[...].astype(f32)
    vrow[10:11, 0:4] = maskt[...].astype(f32)
    sp[0, 56:62, 256:384] = vrow[...].T[0:6]
    s_ref[...] = sp[...].astype(bf16)
    first_small = lens[0] < lens[1]
    trow = lax.broadcasted_iota(jnp.int32, (8, 128), 0)
    tag[...] = jnp.where(trow == 0, jnp.where(first_small, ids[1], ids[0]), jnp.where(first_small, ids[0], ids[1]))
    pl.semaphore_wait(bar, len(greeted))

    me = 2 * y + c
    sib = dev(z, x, y, o)
    mate = pltpu.make_async_remote_copy(s_ref.at[o, YROWS:SROWS], s2, ss1.at[2, 0], rs1.at[2, 0], device_id=sib, device_id_type=MESH)
    mate.start()
    firsts = []
    for j, rows in enumerate((slice(32, 64), slice(0, 32))):
        own = pltpu.make_async_copy(s_ref.at[c, rows], s1.at[me, rows], loc.at[j])
        own.start()
        got = []
        for i, (dy, dc_, t) in enumerate(group):
            cp = pltpu.make_async_remote_copy(s_ref.at[(c + dc_) % 2, rows], s1.at[me, rows], ss1.at[j, i], rs1.at[j, i], device_id=t, device_id_type=MESH)
            cp.start()
            src = 2 * ((y + 4 - dy) % 4) + (c + dc_) % 2
            rc = pltpu.make_async_remote_copy(s_ref.at[c, rows], s1.at[src, rows], ss1.at[j, i], rs1.at[j, i], device_id=t, device_id_type=MESH)
            got.append((cp, rc))
        firsts.append((own, got))
    def shards(j):
        own, got = firsts[j]
        own.wait()
        for _, rc in got: rc.wait_recv()
    tagged = []
    tags[f] = tag[...]
    for r, g in peers(f):
        cp = pltpu.make_async_remote_copy(tag, tags.at[f], tss.at[r], tsr.at[r], device_id=(dp, g), device_id_type=MESH)
        cp.start(); tagged.append(cp)
    def sort_cotangents():
        for r, g in peers(f):
            src = (f + 16 - r) % 16
            pltpu.make_async_remote_copy(tag, tags.at[src], tss.at[r], tsr.at[r], device_id=(dp, g), device_id_type=MESH).wait_recv()
        for s in range(16):
            idv[s:s + 1, :] = tags[s, 0:1, :]
            idv[16 + s:17 + s, :] = tags[s, 1:2, :]
        ld_ids = pltpu.make_async_copy(idv, idm, lsem.at[1])
        ld_ids.start()
        srow = lax.broadcasted_iota(jnp.int32, (32, 128), 0)
        hit = idv[...] == lax.broadcasted_iota(jnp.int32, (32, 128), 1)
        place_of = jnp.where((srow >= 16) & (f >= 4), 32, srow)
        inv[...] = jnp.broadcast_to(jnp.sum(jnp.where(hit, place_of, 0), axis=0, keepdims=True), (8, 128))
        ld_ids.wait()
        ld_cot.wait()
        for s in range(32):
            cotsend[s] = cot[idm[s, 0]]

    few = f < 4
    def to_peer(i, g):
        big = pltpu.make_async_remote_copy(cotsend.at[g], dc.at[f], bss.at[i], bsr.at[i], device_id=(dp, g), device_id_type=MESH)
        return big
    def small_to_peer(i, g):
        return pltpu.make_async_remote_copy(cotsend.at[16 + g], dc.at[16 + f % 4], mss.at[i], msr.at[f % 4], device_id=(dp, g), device_id_type=MESH)
    own_dc = pltpu.make_async_copy(cotsend.at[f], dc.at[f], lsem.at[2])
    own_small = pltpu.make_async_copy(cotsend.at[16 + f], dc.at[16 + f % 4], lsem.at[3])
    def send_cotangents():
        own_dc.start()
        for r, g in peers(f):
            to_peer(r, g).start()
    def send_small_cotangents():
        @pl.when(few)
        def _():
            own_small.start()
            for r, g in peers(f):
                small_to_peer(r, g).start()
    def get_cotangents():
        own_dc.wait()
        for r, g in peers(f):
            src = (f + 16 - r) % 16
            pltpu.make_async_remote_copy(cotsend.at[g], dc.at[src], bss.at[r], bsr.at[r], device_id=(dp, g), device_id_type=MESH).wait_recv()
        for s in range(4):
            @pl.when(f != s)
            def _():
                pltpu.make_async_remote_copy(cotsend.at[16], dc.at[16 + s], mss.at[0], msr.at[s], device_id=(dp, s), device_id_type=MESH).wait_recv()
        @pl.when(few)
        def _():
            own_small.wait()
    def finish_cotangents():
        for r, g in peers(f):
            to_peer(r, g).wait_send()
        @pl.when(few)
        def _():
            for r, g in peers(f):
                small_to_peer(r, g).wait_send()

    def relay(perm, rows, lo, hi):
        flat = s1[:, rows].reshape(256, LW)
        r = jnp.dot(perm[lo:hi, :], flat, preferred_element_type=f32)
        return r.astype(bf16)

    def place(p):
        if p == 0: g_ref[c, 0:4, z, x] = relay(p2_ref, slice(32, 64), 0, 192).reshape(4, 48, LW)
        if p == 1: g_ref[c, 4:8, z, x] = relay(p1_ref, slice(0, 32), 0, 192).reshape(4, 48, LW)
        if p == 2:
            mate.wait_recv()
            both = [s_ref[c, YROWS:SROWS].astype(f32)[0:24], s2[...].astype(f32)[0:24]]
            both = [jnp.where(c == k, both[0], both[1]) for k in range(2)]
            g2_ref[c, z, x, y] = jnp.concatenate(both, axis=0).astype(bf16)
        if p == 3: g_ref[c, 8, z, x] = relay(p2_ref, slice(32, 64), 192, 240)

    sends = []
    def mk(k, i, v, to):
        return pltpu.make_async_remote_copy(v, v, ssem.at[k, i], rsem.at[k, i], device_id=to, device_id_type=MESH)
    def send(k, i, v, to):
        cp = mk(k, i, v, to); cp.start(); sends.append(cp)
    def recv(k, i, v):
        mk(k, i, v, sib).wait_recv()

    def steps(k, axes, view, parts):
        last = len(axes) - 1
        def opposite(l):
            at, _ = rings[axes[l]]
            _, fa, fb = parts[l]
            recv(k, 4 * l + 2, view(l, at[2], fa, c))
            if fb is not None: recv(k, 4 * l + 3, view(l, at[2], fb, c))
        def first(l):
            at, to = rings[axes[l]]
            full = parts[l][0]
            if l: opposite(l - 1)
            for i, d in enumerate((1, -1)): send(k, 4 * l + i, view(l, at[0], full, c), to[d])
            if l == last: send(k, 12, view(l, at[0], full, c), sib)
        def second(l):
            at, to = rings[axes[l]]
            full, fa, fb = parts[l]
            recv(k, 4 * l, view(l, at[-1], full, c))
            send(k, 4 * l + 2, view(l, at[-1], fa, c), to[1])
            if l == last: send(k, 13, view(l, at[-1], full, c), sib)
            recv(k, 4 * l + 1, view(l, at[1], full, c))
            if fb is not None: send(k, 4 * l + 3, view(l, at[1], fb, c), to[-1])
            if l == last: send(k, 14, view(l, at[1], full, c), sib)
        def third():
            at, _ = rings[axes[last]]
            opposite(last)
            send(k, 15, view(last, at[2], parts[last][0], c), sib)
        def fourth():
            at, _ = rings[axes[last]]
            for i, d in enumerate((0, -1, 1, 2)): recv(k, 12 + i, view(last, at[d], parts[last][0], o))
        out = []
        for l in range(last + 1):
            out += [functools.partial(first, l), functools.partial(second, l)]
        return out + [third, fourth]

    def unit_chunk(k, axes, *parts):
        def view(l, at, part, h):
            u0, u1, l0, l1 = part
            zs, xs = [(z, at), (at, ALL)][l] if axes == "xz" else [(at, x), (ALL, at)][l]
            return g_ref.at[h, u0:u1, zs, xs, :, l0:l1]
        return steps(k, axes, view, [parts, parts])
    def fc2_chunk(k):
        def view(l, at, part, h):
            a, b = part
            if l == 0: return g2_ref.at[h, z, at, y, a:b]
            if l == 1: return g2_ref.at[h, at, a:b, y]
            return g2_ref.at[h, a:b, :, at]
        ring = ((0, 4), (0, 2), (2, 4))
        return steps(k, "xzy", view, [((0, 48), (0, 32), (32, 48)), ring, ring])

    outs = []
    def to_hbm(p):
        if p == 2: cp = pltpu.make_async_copy(g2_ref, g2_hbm, wsem.at[p])
        else:
            u0, u1 = ((0, 4), (4, 8), None, (8, 9))[p]
            cp = pltpu.make_async_copy(g_ref.at[:, u0:u1], g_hbm.at[:, u0:u1], wsem.at[p])
        cp.start(); outs.append(cp)

    def blocks(body, n=7):
        def step(i, _):
            body(pl.ds(pl.multiple_of(i * 48, 48), 48)); return 0
        lax.fori_loop(0, n, step, 0)

    def w(h, u):
        return g_ref[h, u].reshape(768, LW)

    def rows_of():
        v = jnp.concatenate([g_ref[0, 8, zz, xx, :, 256:384] for zz in range(4) for xx in range(4)], axis=0)
        vt = v.astype(f32).T
        rows_ref[0:5, 0:768] = vt[0:5]
        md = lax.dot_general(v, m2_ref[...], TN, preferred_element_type=f32)
        rows_ref[6:8, 0:512] = md[9:11]
        lane = (lax.broadcasted_iota(jnp.int32, (8, 768), 1) % 24) // 6
        row = lax.broadcasted_iota(jnp.int32, (8, 768), 0)
        for s in range(4):
            q = lax.dot_general(v[192 * s:192 * s + 192], m4_ref[...], TN, preferred_element_type=f32)
            q = jnp.where(row == lane, q[5:13], 0.0)
            rows_ref[5:6, 768 * s:768 * s + 768] = jnp.sum(q, axis=0, keepdims=True)

    def ln1():
        def body(r):
            n, _ = stats(tok[r, :].astype(f32))
            a_ref[r, :] = (n * rows_ref[0:1, 0:768] + rows_ref[1:2, 0:768]).astype(bf16)
        blocks(body)

    def qkv():
        for h in range(2):
            wt = jnp.concatenate([w(h, u) for u in range(3)], axis=1)
            qkv_ref[:, h * 1152:(h + 1) * 1152] = jnp.dot(a_ref[...], wt, preferred_element_type=f32).astype(bf16)

    ends0 = lens[0] + 2
    ends1 = ends0 + lens[1] + 2
    def seg(shape, axis):
        r = lax.broadcasted_iota(jnp.int32, shape, axis)
        return (r >= ends0).astype(jnp.int32) + (r >= ends1).astype(jnp.int32)

    def attention(lo, hi):
        low = lax.broadcasted_iota(jnp.int32, (1, 128), 1) < 64
        same = seg((ROWS, 1), 0) == seg((1, ROWS), 1)
        bias = jnp.where(same, 0.0, -1e30)
        def pair(i, _):
            q, k, v = (qkv_ref[:, pl.ds(pl.multiple_of(LW * i + 128 * b, 128), 128)] for b in range(3))
            outs_ = []
            for t in range(2):
                keep = low if t == 0 else jnp.logical_not(low)
                s = lax.dot_general(jnp.where(keep, q, jnp.zeros_like(q)), k, NT, preferred_element_type=f32)
                s = jnp.where(same, s * 0.125, -1e30)
                m = jnp.max(s, axis=-1, keepdims=True)
                ex = jnp.exp(s - m)
                pr = (ex / jnp.sum(ex, axis=-1, keepdims=True)).astype(bf16)
                p_out[2 * i + t] = pr
                outs_.append(jnp.dot(pr, v, preferred_element_type=f32))
            o_ref[:, pl.ds(pl.multiple_of(i * 128, 128), 128)] = jnp.where(low, outs_[0], outs_[1]).astype(bf16)
            return 0
        lax.fori_loop(lo, hi, pair, 0)

    def out_proj():
        for h in range(2):
            cs = slice(h * LW, (h + 1) * LW)
            x2_ref[:, cs] = tok[0:ROWS, cs].astype(f32) + jnp.dot(o_ref[...], w(h, 3), preferred_element_type=f32)
        def body(r):
            n, _ = stats(x2_ref[r, :])
            h2_ref[r, :] = (n * rows_ref[2:3, 0:768] + rows_ref[3:4, 0:768]).astype(bf16)
        blocks(body)

    def fc1(first):
        for h in range(2):
            def unit(u, _):
                cs = pl.ds(pl.multiple_of(h * 1536 + u * LW, LW), LW)
                f = jnp.dot(h2_ref[...], w(h, 4 + u), preferred_element_type=f32) + rows_ref[5:6, cs]
                g, dg = gelu_pair(f)
                act_ref[:, cs] = g.astype(bf16)
                dact_ref[:, cs] = dg.astype(bf16)
                return 0
            lax.fori_loop(first, first + 2, unit, 0)

    def fc2():
        for h in range(2):
            cs = slice(h * LW, (h + 1) * LW)
            t = jnp.dot(act_ref[...], g2_ref[h].reshape(3072, LW), preferred_element_type=f32)
            e_ref[:, cs] = (x2_ref[:, cs] + t + rows_ref[4:5, cs]).astype(bf16)

    def dec():
        for h in range(2):
            cs = slice(h * 256, (h + 1) * 256)
            t = jnp.dot(e_ref[...], g_ref[h, 8, :, :, :, 0:256].reshape(768, 256), preferred_element_type=f32)
            z_ref[:, cs] = (t + rows_ref[6:7, cs]).astype(bf16)
        z_ref[:, 512:640] = jnp.ones((ROWS, 128), bf16)
        def block(i, _):
            fill = hits[pl.ds(pl.multiple_of(i * 256, 256), 256), :]
            r = jnp.dot(fill, z_ref[...], preferred_element_type=f32)
            empty = 1.0 - r[:, 512:640]
            for t in range(4):
                cs = slice(128 * t, 128 * t + 128)
                val = r[:, cs] + empty * rows_ref[7:8, cs]
                cells_ref[pl.ds(4 * i, 4), :, cs] = val.astype(bf16).reshape(4, 64, 128)
            return 0
        lax.fori_loop(0, 5, block, 0)

    def fills():
        p_ = pos[0:1, 0:ROWS]
        large = seg((1, ROWS), 1) == jnp.where(first_small, 1, 0)
        target = jnp.where(p_ >= 0, jnp.where(large, p_, 1024 + p_), -1)
        def block(i, _):
            cell = i * 256 + lax.broadcasted_iota(jnp.int32, (256, 1), 0)
            hits[pl.ds(pl.multiple_of(i * 256, 256), 256), :] = (cell == target).astype(f32).astype(bf16)
            return 0
        lax.fori_loop(0, 5, block, 0)

    def cell_grads():
        get_cotangents()
        d = dc[...].reshape(1280, 512)
        dz[...] = lax.dot_general(hits[...], d, TN, preferred_element_type=f32).astype(bf16)
        covered = lax.dot_general(jnp.ones((16, ROWS), bf16), hits[...], NT, preferred_element_type=f32)
        vs[10:11, :] = jnp.dot((1.0 - covered).astype(bf16), d, preferred_element_type=f32)[0:1]
        vs[9:10, :] = jnp.sum(dz[...].astype(f32), axis=0, keepdims=True)
        for n in range(2):
            rs = slice(n * 384, (n + 1) * 384)
            wt = [g_ref[h, 8, :, :, :, 0:256].reshape(768, 256)[rs] for h in range(2)]
            t = lax.dot_general(dz[:, 0:256], wt[0], NT, preferred_element_type=f32)
            t = t + lax.dot_general(dz[:, 256:512], wt[1], NT, preferred_element_type=f32)
            dx[:, rs] = t
            dm[:, rs] = t.astype(bf16)

    kept = dict(rows=(rows_ref, rows_hbm), a=(a_ref, a_hbm), qkv=(qkv_ref, qkv_hbm), p=(p_out, p_hbm), o=(o_ref, o_hbm),
                x2=(x2_ref, x2_hbm), h2=(h2_ref, h2_hbm), act=(act_ref, act_hbm), dact=(dact_ref, dact_hbm), e=(e_ref, e_hbm),
                cells=(cells_ref, cells_hbm), dz=(dz, dz_hbm), dx=(dx, dx_hbm), dm=(dm, dm_hbm), vs=(vs, vs_hbm), inv=(inv, inv_hbm))
    def keep(*names):
        for n in names:
            cp = pltpu.make_async_copy(*kept[n], osem.at[list(kept).index(n)])
            cp.start(); outs.append(cp)

    vs[...] = jnp.zeros_like(vs)
    rows_ref[...] = jnp.zeros_like(rows_ref)
    half = lambda u: ((u, u + 2, 0, LW), (u, u + 1, 0, LW), (u + 1, u + 2, 0, LW))
    pieces = {
        3: [unit_chunk(0, "xz", (8, 9, 0, LW), (8, 9, 0, 256), (8, 9, 256, LW))],
        2: [fc2_chunk(1)],
        0: [unit_chunk(2, "xz", *half(0)), unit_chunk(3, "zx", *half(2))],
        "1a": [unit_chunk(4, "xz", *half(4))],
        "1b": [unit_chunk(5, "zx", *half(6))],
    }
    def go(step, *names):
        for p in names:
            for ch in pieces[p]: ch[step]()
    place(2); go(0, 2)
    shards(0)
    place(3); place(0); go(0, 0, 3)
    go(1, 2, 0, 3)
    shards(1)
    place(1); go(0, "1a", "1b")
    go(2, 0, 3, 2)
    sort_cotangents(); keep("inv")
    send_small_cotangents()
    go(1, "1a", "1b")
    go(3, 2, 0, 3)
    go(2, "1a", "1b")
    go(4, 2)
    send_cotangents()
    fills()
    go(4, 0, 3)
    go(5, 3); to_hbm(3)
    rows_of(); ln1(); keep("rows", "a")
    go(5, 0); to_hbm(0)
    qkv(); keep("qkv")
    go(3, "1a", "1b")
    go(5, 2)
    attention(0, 3)
    go(4, "1a", "1b")
    attention(3, 6)
    keep("p")
    go(6, 2)
    out_proj(); keep("o", "x2", "h2")
    cell_grads(); keep("dz", "dx", "dm", "vs")
    go(5, "1a"); fc1(0)
    go(5, "1b"); to_hbm(1)
    fc1(2); keep("act", "dact")
    go(7, 2); to_hbm(2)
    fc2(); keep("e")
    dec(); keep("cells")
    for _, got in firsts:
        for cp, _ in got: cp.wait_send()
    for cp in sends: cp.wait_send()
    mate.wait_send()
    for cp in tagged: cp.wait_send()
    finish_cotangents()
    for cp in outs: cp.wait()


def k1_call(*args):
    S = jax.ShapeDtypeStruct
    vm, smem = pl.BlockSpec(memory_space=pltpu.VMEM), pl.BlockSpec(memory_space=pltpu.SMEM)
    anyspec = pl.BlockSpec(memory_space=pl.ANY)
    V, DMA = pltpu.VMEM, pltpu.SemaphoreType.DMA
    outs = (
        S((2, 9, 4, 4, 48, LW), bf16), S((2, 4, 4, 4, 48, LW), bf16), S((8, 3072), f32), S((ROWS, 768), bf16),
        S((ROWS, 2304), bf16), S((12, ROWS, ROWS), bf16), S((ROWS, 768), bf16), S((ROWS, 768), f32),
        S((ROWS, 768), bf16), S((ROWS, 3072), bf16), S((ROWS, 3072), bf16), S((ROWS, 768), bf16), S((20, 64, 512), bf16),
        S((ROWS, 512), bf16), S((ROWS, 768), f32), S((ROWS, 768), bf16), S((16, 512), f32), S((8, 128), jnp.int32),
    )
    return pl.pallas_call(
        k1_kernel,
        out_shape=outs,
        in_specs=[smem, smem] + [vm] * 15 + [anyspec] + [vm] * 4,
        out_specs=[anyspec] * 18,
        scratch_shapes=[V(t.shape, t.dtype) for t in outs] + [
            V((2, SROWS, LW), f32), V((2, SROWS, LW), bf16), V((8, YROWS, LW), bf16), V((SROWS - YROWS, LW), bf16), V((ROWS, 640), bf16), V((128, 128), f32),
            V((8, 128), jnp.int32), V((16, 8, 128), jnp.int32), V((32, 128), jnp.int32), pltpu.SMEM((32, 128), jnp.int32),
            V((32, 64, 512), bf16), V((32, 64, 512), bf16), V((20, 64, 512), bf16), V((1280, ROWS), bf16),
            DMA((3, 7)), DMA((3, 7)), DMA((2,)), DMA((6, 16)), DMA((6, 16)), DMA((4,)), DMA((16,)), DMA((16,)), DMA((16,)),
            DMA((16,)), DMA((16,)), DMA((16,)), DMA((4,)), DMA((4,)),
        ],
        compiler_params=pltpu.CompilerParams(collective_id=0, has_side_effects=True, vmem_limit_bytes=60 * 2**20),
        cost_estimate=pl.CostEstimate(flops=6 * 10**9, bytes_accessed=5 * 10**7, transcendentals=0),
        name="forward",
    )(*args, jnp.asarray(spread_matrix((4, 5, 6, 7), 0).T, bf16), jnp.asarray(spread_matrix((0, 1, 2, 3, 8), 32).T, bf16),
      jnp.asarray(cell_spread(), bf16), jnp.asarray(fc1_bias_spread(), bf16))


def k2_kernel(g_hbm, g2_hbm, rows_hbm, a_hbm, qkv_hbm, p_hbm, o_hbm, x2_hbm, h2_hbm, act_hbm, dact_hbm, e_hbm, cells_hbm,
              dz_hbm, dx_hbm, dm_hbm, vs_hbm, tok_hbm, pt1_ref, pt2_ref, m2_ref, m4_ref,
              tg_ref, arr, oq_ref, oo_ref, of1_ref, of2_ref, od_ref, v0_ref, v1_ref, v2_ref, v3_ref, v4_ref, vf_ref, vd_ref, vm_ref,
              rows_ref, a_ref, qkv_ref, o_ref, x2_ref, h2_ref, act_ref, dact_ref, e_ref, dz, dx, dm, vs, tok,
              wa, wb, sta, sta2, stc, sg, sg2, acc, acc2, xa, xa2, xb, xc, xd,
              dh, df, dqkv, vsum, pb, fs, f1, fo, fs2, f2, zb, vt, vout, vin,
              ssem, rsem, ss1, rs1, loc, wsem, psem, tsem, isem, css, csr, csl, vss, vrs):
    z, x, y, c = coords()
    dp, f = lax.axis_index("dp"), lax.axis_index("fsdp")
    o = 1 - c
    bar = pltpu.get_barrier_semaphore()
    rings = ring_places(z, x, y, c)
    targets = [rings[a][1][d] for a in "zx" for d in (1, -1)]
    sib = dev(z, x, y, o)
    group = []
    for dy in range(4):
        for dc in range(2):
            if dy or dc:
                group.append((dy, dc, dev(z, x, (y + dy) % 4, (c + dc) % 2)))
    plane = [(4 * dz_ + dx_, (z + dz_) % 4, (x + dx_) % 4, (z + 4 - dz_) % 4, (x + 4 - dx_) % 4)
             for dz_ in range(4) for dx_ in range(4) if dz_ or dx_]
    greeted = targets + [(dp, g) for _, g in peers(f)] + [dev(zz, xx, y, c) for _, zz, xx, _, _ in plane]
    greet(bar, greeted)
    loads = {}
    def load(name, src, dst):
        loads[name] = pltpu.make_async_copy(src, dst, isem.at[len(loads)])
        return loads[name]
    for name, src, dst in (
        ("dm", dm_hbm, dm), ("act", act_hbm, act_ref), ("e", e_hbm, e_ref), ("dz", dz_hbm, dz), ("fc2", g2_hbm, wa), ("dact", dact_hbm, dact_ref), ("fc1", g_hbm.at[:, 4:8], wb),
        ("h2", h2_hbm, h2_ref), ("x2", x2_hbm, x2_ref), ("dx", dx_hbm, dx), ("rows", rows_hbm, rows_ref), ("o", o_hbm, o_ref),
        ("qkv", qkv_hbm, qkv_ref), ("a", a_hbm, a_ref), ("tok", tok_hbm.at[0:ROWS], tok),
        ("vs", vs_hbm, vs),
    ):
        load(name, src, dst).start()
    def need(*names):
        for n in names: loads[n].wait()
    ld_c = pltpu.make_async_copy(g_hbm.at[:, 0:4], wb, wsem.at[0])
    zb[...] = jnp.zeros_like(zb)
    vt[...] = jnp.zeros_like(vt)
    vsum[...] = jnp.zeros_like(vsum)
    pl.semaphore_wait(bar, len(greeted))

    few = f < 4
    def cells_to(i, g):
        return pltpu.make_async_remote_copy(cells_hbm.at[g], arr.at[f], css.at[i], csr.at[i], device_id=(dp, g), device_id_type=MESH)
    def small_cells_to(i, g):
        return pltpu.make_async_remote_copy(cells_hbm.at[16 + g % 4], arr.at[16 + f], css.at[16 + i], csr.at[16 + i], device_id=(dp, g), device_id_type=MESH)
    locals_ = [pltpu.make_async_copy(cells_hbm.at[f], arr.at[f], csl.at[0]), pltpu.make_async_copy(zb, arr.at[32], csl.at[1])]
    own_small = pltpu.make_async_copy(cells_hbm.at[16 + f % 4], arr.at[16 + f], csl.at[2])
    for l in locals_: l.start()
    for r, g in peers(f):
        cells_to(r, g).start()
        @pl.when(g < 4)
        def _():
            small_cells_to(r, g).start()
    @pl.when(few)
    def _():
        own_small.start()
    def finish_cells():
        for l in locals_: l.wait()
        for r, g in peers(f):
            src = (f + 16 - r) % 16
            pltpu.make_async_remote_copy(cells_hbm.at[g], arr.at[src], css.at[r], csr.at[r], device_id=(dp, g), device_id_type=MESH).wait_recv()
            cells_to(r, g).wait_send()
            @pl.when(g < 4)
            def _():
                small_cells_to(r, g).wait_send()
        @pl.when(few)
        def _():
            own_small.wait()
            for r, g in peers(f):
                src = (f + 16 - r) % 16
                pltpu.make_async_remote_copy(cells_hbm.at[16], arr.at[16 + src], css.at[16 + r], csr.at[16 + r], device_id=(dp, g), device_id_type=MESH).wait_recv()

    sends = {}
    def send(k, i, src, dst, to):
        cp = pltpu.make_async_remote_copy(src, dst, ssem.at[k, i], rsem.at[k, i], device_id=to, device_id_type=MESH)
        cp.start(); sends[k, i] = cp
    def recv(k, i, v):
        pltpu.make_async_remote_copy(v, v, ssem.at[k, i], rsem.at[k, i], device_id=sib, device_id_type=MESH).wait_recv()

    def steps(k, axes, ours, theirs, from_sib, inbox, parts):
        last = len(axes) - 1
        def add(v, *more):
            t = v[...].astype(f32)
            for m in more: t = t + m[...].astype(f32)
            v[...] = t.astype(bf16)
        def opposite(l):
            at, to = rings[axes[l]]
            _, fa, fb = parts[l]
            send(k, 4 * l, ours(l, at[2], fa), inbox(l, 0, fa), to[1])
            if fb is not None: send(k, 4 * l + 1, ours(l, at[2], fb), inbox(l, 0, fb), to[-1])
        def start():
            send(k, 12, theirs, from_sib, sib)
        def join():
            recv(k, 12, from_sib)
            at, _ = rings[axes[last]]
            for d in (2, 1, -1, 0):
                add(ours(last, at[d], parts[last][0]), share(last, at[d]))
                if d == 2: opposite(last)
        def share(l, place):
            return from_sib_view[k](place)
        def near(l):
            at, to = rings[axes[l]]
            full, fa, fb = parts[l]
            recv(k, 4 * l, inbox(l, 0, fa)); add(ours(l, at[1], fa), inbox(l, 0, fa))
            send(k, 4 * l + 2, ours(l, at[1], full), inbox(l, 1, full), to[1])
            if fb is not None:
                recv(k, 4 * l + 1, inbox(l, 0, fb)); add(ours(l, at[-1], fb), inbox(l, 0, fb))
            send(k, 4 * l + 3, ours(l, at[-1], full), inbox(l, 2, full), to[-1])
        def here(l):
            at, to = rings[axes[l]]
            full = parts[l][0]
            recv(k, 4 * l + 2, inbox(l, 1, full)); recv(k, 4 * l + 3, inbox(l, 2, full))
            add(ours(l, at[0], full), inbox(l, 1, full), inbox(l, 2, full))
            if l: opposite(l - 1)
        out = [start, join]
        for l in range(last, -1, -1):
            out += [functools.partial(near, l), functools.partial(here, l)]
        return out

    from_sib_view = {}
    def unit_chunk(k, axes, staged, *parts):
        def at_level(l, at):
            return [(z, at), (at, ALL)][l] if axes == "xz" else [(at, x), (ALL, at)][l]
        def cut(ref, part, l, at):
            u0, u1, l0, l1 = part
            zs, xs = at_level(l, at)
            return ref.at[u0:u1, zs, xs, :, l0:l1]
        def inbox(l, way, part):
            u0, u1, l0, l1 = part
            return xb.at[way, u0:u1, :, l0:l1] if l == 0 else xa.at[way, u0:u1, :, :, l0:l1]
        u0, u1, l0, l1 = parts[0]
        from_sib_view[k] = lambda place: cut(sg, parts[0], 1, place)
        return steps(k, axes, lambda l, at, part: cut(acc, part, l, at), staged, sg.at[u0:u1, :, :, :, l0:l1], inbox, [parts, parts])
    def fc2_chunk(k):
        def ours(l, at, part):
            a, b = part
            if l == 0: return acc2.at[z, at, y, a:b]
            if l == 1: return acc2.at[at, a:b, y]
            return acc2.at[a:b, :, at]
        def inbox(l, way, part):
            a, b = part
            return (xd, xc, xa2)[l].at[way, a:b]
        ring = ((0, 4), (0, 2), (2, 4))
        from_sib_view[k] = lambda place: sg2.at[:, :, place]
        return steps(k, "xzy", ours, sta2, sg2, inbox, [((0, 48), (0, 32), (32, 48)), ring, ring])

    lanes = lambda u, l0, lm, l1: ((u, u + 1, l0, l1), (u, u + 1, l0, lm), (u, u + 1, lm, l1))
    pair = lambda u: ((u, u + 2, 0, LW), (u, u + 1, 0, LW), (u + 1, u + 2, 0, LW))
    table = {
        "fc2": fc2_chunk(0),
        "dec": unit_chunk(1, "xz", stc.at[:, :, :, :, 0:256], *lanes(8, 0, 128, 256)),
        "f1a": unit_chunk(2, "xz", sta.at[0:2], *pair(4)),
        "f1b": unit_chunk(3, "xz", sta.at[2:4], *pair(6)),
        "out": unit_chunk(4, "zx", sta.at[3:4], *lanes(3, 0, 256, LW)),
        "q0": unit_chunk(5, "xz", sta.at[0:1], *lanes(0, 0, 256, LW)),
        "q1": unit_chunk(6, "zx", sta.at[1:2], *lanes(1, 0, 256, LW)),
        "q2": unit_chunk(8, "xz", sta.at[2:3, :, :, :, 0:256], *lanes(2, 0, 128, 256)),
        "q3": unit_chunk(9, "zx", sta.at[2:3, :, :, :, 256:LW], (2, 3, 256, LW), (2, 3, 256, LW), None),
    }
    def st(s, *names):
        for n in names: table[n][s]()

    def send_small(v):
        vout[...] = v.reshape(4, 4, 48, 128)
        vin[4 * z + x] = vout[z, x]
        for i, zz, xx, _, _ in plane:
            cp = pltpu.make_async_remote_copy(vout.at[zz, xx], vin.at[4 * z + x], vss.at[i], vrs.at[i], device_id=dev(zz, xx, y, c), device_id_type=MESH)
            cp.start(); lasts.append(cp)
    def sum_small():
        for i, zz, xx, sz, sx in plane:
            pltpu.make_async_remote_copy(vout.at[zz, xx], vin.at[4 * sz + sx], vss.at[i], vrs.at[i], device_id=dev(zz, xx, y, c), device_id_type=MESH).wait_recv()
        acc[8, z, x, :, 256:LW] = jnp.sum(vin[...].astype(f32), axis=0).astype(bf16)

    lasts = []
    me = 2 * y + c
    def last_exchange(j, pt, units):
        rs_ = slice(32 * j, 32 * j + 32)
        blk = jnp.concatenate([acc[u, z, x] for u in units], axis=0)
        fs[:, rs_] = jnp.dot(pt[...], blk, preferred_element_type=f32).astype(bf16).reshape(8, 32, LW)
        own = pltpu.make_async_copy(fs.at[me, rs_], f1.at[me, rs_], loc.at[j])
        own.start()
        got = []
        for i, (dy, dc, t) in enumerate(group):
            dst = 2 * ((y + dy) % 4) + (c + dc) % 2
            cp = pltpu.make_async_remote_copy(fs.at[dst, rs_], f1.at[me, rs_], ss1.at[j, i], rs1.at[j, i], device_id=t, device_id_type=MESH)
            cp.start()
            src = 2 * ((y + 4 - dy) % 4) + (c + dc) % 2
            rc = pltpu.make_async_remote_copy(fs.at[me, rs_], f1.at[src, rs_], ss1.at[j, i], rs1.at[j, i], device_id=t, device_id_type=MESH)
            lasts.append(cp); got.append(rc)
        def finish():
            own.wait()
            for rc in got: rc.wait_recv()
            for h in range(2):
                t = f1[h, rs_].astype(f32)
                for yy in range(1, 4): t = t + f1[2 * yy + h, rs_].astype(f32)
                fo[h, rs_] = t
        return finish
    def fc2_exchange():
        v = acc2[z, x, y].astype(f32)
        pad = jnp.zeros((8, LW), f32)
        for k in range(2):
            fs2[k] = jnp.concatenate([v[24 * k:24 * k + 24], pad], axis=0).astype(bf16)
        cp = pltpu.make_async_remote_copy(fs2.at[o], f2, ss1.at[0, 7], rs1.at[0, 7], device_id=sib, device_id_type=MESH)
        cp.start(); lasts.append(cp)
        of2_ref[:, pl.ds(pl.multiple_of(c * LW, LW), LW)] = jnp.where(c == 0, v[0:24], v[24:48])
        def finish():
            cp.wait_recv()
            of2_ref[:, pl.ds(pl.multiple_of(o * LW, LW), LW)] = f2[...].astype(f32)[0:24]
        return finish

    def blocks(body, n=7):
        def step(i, _):
            body(pl.ds(pl.multiple_of(i * 48, 48), 48)); return 0
        lax.fori_loop(0, n, step, 0)
    def col(base, width, unit):
        return pl.ds(pl.multiple_of(base, unit), width)

    def grad_fc2(h, dst):
        def part(i, _):
            t = lax.dot_general(act_ref[:, col(i * 768, 768, 768)], dm[:, col(h * LW, LW, LW)], TN, preferred_element_type=f32)
            dst[i] = t.astype(bf16).reshape(4, 4, 48, LW)
            return 0
        lax.fori_loop(0, 4, part, 0)

    def fc2_back():
        def part(i, _):
            cs = col(i * 768, 768, 768)
            t = lax.dot_general(dm[:, 0:LW], wa[0, i].reshape(768, LW), NT, preferred_element_type=f32)
            t = t + lax.dot_general(dm[:, LW:768], wa[1, i].reshape(768, LW), NT, preferred_element_type=f32)
            t = (t * dact_ref[:, cs].astype(f32)).astype(bf16)
            df[:, cs] = t
            vsum[5:6, cs] = jnp.sum(t.astype(f32), axis=0, keepdims=True)
            return 0
        lax.fori_loop(0, 4, part, 0)

    def wunit(h, u):
        return wb[h, u].reshape(768, LW)
    def fc1_back():
        for h in range(2):
            wt = lambda r: jnp.concatenate([wunit(h, u)[r] for u in range(4)], axis=1)
            for n in range(2):
                rs = slice(n * 384, (n + 1) * 384)
                t = lax.dot_general(df[:, h * 1536:(h + 1) * 1536], wt(rs), NT, preferred_element_type=f32)
                dh[:, rs] = t if h == 0 else dh[:, rs] + t

    def grad_fc1(h, dst, base):
        def part(u, _):
            t = lax.dot_general(h2_ref[...], df[:, col(h * 1536 + u * LW, LW, LW)], TN, preferred_element_type=f32)
            dst[base + u] = t.astype(bf16).reshape(4, 4, 48, LW)
            return 0
        lax.fori_loop(0, 4, part, 0)

    def norm_back(src, gain_row, into, out_lo, base):
        gain = rows_ref[gain_row:gain_row + 1, 0:768]
        def body(r):
            n, rstd = stats(src[r, :].astype(f32))
            d = dh[r, :]
            vsum[base:base + 1, 0:768] += jnp.sum(d * n, axis=0, keepdims=True)
            vsum[base + 1:base + 2, 0:768] += jnp.sum(d, axis=0, keepdims=True)
            dn = d * gain
            t = rstd * (dn - jnp.mean(dn, axis=-1, keepdims=True) - n * jnp.mean(dn * n, axis=-1, keepdims=True))
            t = dx[r, :] + t
            into[r, :] = t
            if out_lo is not None: out_lo[r, :] = t.astype(bf16)
        blocks(body)

    def out_back():
        t = lax.dot_general(dm[:, 0:LW], wunit(0, 3), NT, preferred_element_type=f32)
        t = t + lax.dot_general(dm[:, LW:768], wunit(1, 3), NT, preferred_element_type=f32)
        df[:, 0:768] = t.astype(bf16)

    def load_p(i):
        return pltpu.make_async_copy(p_hbm.at[pl.ds(2 * (i // 2 + 3 * (i % 2)), 2)], pb.at[i % 2], psem.at[i % 2])

    def attn_back(u):
        low = lax.broadcasted_iota(jnp.int32, (1, 128), 1) < 64
        def pair(j, _):
            load_p(2 * u + j).wait()
            i = u + 3 * j
            def cols(b):
                return qkv_ref[:, col(LW * i + 128 * b, 128, 128)]
            q, kk, v, do = cols(0), cols(1), cols(2), df[:, col(i * 128, 128, 128)]
            r = []
            for t in range(2):
                keep = low if t == 0 else jnp.logical_not(low)
                pr = pb[j, t]
                dp = lax.dot_general(jnp.where(keep, do, jnp.zeros_like(do)), v, NT, preferred_element_type=f32)
                p32 = pr.astype(f32)
                ds = (p32 * (dp - jnp.sum(dp * p32, axis=-1, keepdims=True))).astype(bf16)
                dv = lax.dot_general(pr, do, TN, preferred_element_type=f32)
                dq = jnp.dot(ds, kk, preferred_element_type=f32)
                dk = lax.dot_general(ds, q, TN, preferred_element_type=f32)
                r.append((0.125 * dq, 0.125 * dk, dv))
            for b in range(3):
                dqkv[:, col(LW * i + 128 * b, 128, 128)] = jnp.where(low, r[0][b], r[1][b]).astype(bf16)
            if u < 2: load_p(2 * u + j + 2).start()
            return 0
        lax.fori_loop(0, 2, pair, 0)

    def qkv_back():
        for h in range(2):
            wt = lambda r: jnp.concatenate([wunit(h, u)[r] for u in range(3)], axis=1)
            for n in range(2):
                rs = slice(n * 384, (n + 1) * 384)
                t = lax.dot_general(dqkv[:, h * 1152:(h + 1) * 1152], wt(rs), NT, preferred_element_type=f32)
                dh[:, rs] = t if h == 0 else dh[:, rs] + t

    def grad_qkv(u, h, dst):
        t = lax.dot_general(a_ref[...], dqkv[:, col(h * 1152 + u * LW, LW, LW)], TN, preferred_element_type=f32)
        dst[u] = t.astype(bf16).reshape(4, 4, 48, LW)
    def grad_out(h, dst):
        t = lax.dot_general(o_ref[...], dm[:, col(h * LW, LW, LW)], TN, preferred_element_type=f32)
        dst[3] = t.astype(bf16).reshape(4, 4, 48, LW)

    def vec_cols():
        rt = jnp.concatenate([vsum[0:8, 0:768], jnp.zeros((120, 768), f32)], axis=0)
        srow = lax.broadcasted_iota(jnp.int32, (128, 768), 0)
        rt = jnp.where(srow < 5, rt, 0.0)
        v = rt.T
        r2 = jnp.concatenate([vsum[0:16, 0:512], jnp.zeros((112, 512), f32)], axis=0)
        srow2 = lax.broadcasted_iota(jnp.int32, (128, 512), 0)
        r2 = jnp.where((srow2 == 9) | (srow2 == 10), r2, 0.0).astype(bf16)
        v = v + lax.dot_general(m2_ref[...], r2, NT, preferred_element_type=f32)
        lane = (lax.broadcasted_iota(jnp.int32, (128, 768), 1) % 24) // 6
        parts = []
        for s in range(4):
            wrow = jnp.broadcast_to(vsum[5:6, 768 * s:768 * s + 768], (128, 768))
            wt = jnp.where(srow - 5 == lane, wrow, 0.0).astype(bf16)
            parts.append(lax.dot_general(m4_ref[...], wt, NT, preferred_element_type=f32))
        return (v + jnp.concatenate(parts, axis=0)).astype(bf16)

    def grad_dec(h, dst_store):
        t = lax.dot_general(e_ref[...], dz[:, col(h * 256, 256, 256)], TN, preferred_element_type=f32)
        dst_store(t.astype(bf16).reshape(4, 4, 48, 256), slice(0, 256))

    def acc8(v, cs): acc[8, :, :, :, cs] = v
    def stc8(v, cs): stc[0, :, :, :, cs] = v

    need("dm", "act")
    grad_fc2(o, sta2); st(0, "fc2")
    grad_fc2(c, acc2)
    vsum[4:5, 0:768] = jnp.sum(dm[...].astype(f32), axis=0, keepdims=True)
    need("e", "dz")
    grad_dec(o, stc8); st(0, "dec")
    grad_dec(c, acc8)
    need("fc2", "dact")
    fc2_back()
    st(1, "fc2", "dec")
    need("h2")
    grad_fc1(o, sta, 0); st(0, "f1a", "f1b")
    grad_fc1(c, acc, 4)
    st(2, "dec")
    need("fc1")
    fc1_back()
    ld_c.start()
    load_p(0).start(); load_p(1).start()
    st(1, "f1a", "f1b")
    need("x2", "dx", "rows")
    norm_back(x2_ref, 2, dx, dm, 2)
    ld_c.wait()
    for kk in (2, 3): sends[kk, 12].wait_send(); del sends[kk, 12]
    need("o", "qkv")
    grad_out(o, sta); st(0, "out")
    grad_out(c, acc)
    out_back()
    st(3, "dec"); st(1, "out")
    need("a")
    attn_back(0)
    st(2, "f1a", "f1b")
    grad_qkv(0, o, sta); st(0, "q0"); grad_qkv(0, c, acc)
    st(2, "fc2"); st(2, "out"); st(4, "dec")
    attn_back(1)
    st(3, "out"); st(5, "dec"); st(1, "q0")
    grad_qkv(1, o, sta); st(0, "q1"); grad_qkv(1, c, acc)
    st(3, "f1a", "f1b")
    attn_back(2)
    st(2, "q0"); st(1, "q1"); st(3, "fc2")
    grad_qkv(2, o, sta); st(0, "q2", "q3"); grad_qkv(2, c, acc)
    st(4, "out", "f1a", "f1b"); st(3, "q0"); st(4, "fc2")
    qkv_back()
    st(1, "q2", "q3"); st(2, "q1"); st(5, "out", "f1a", "f1b", "fc2")
    finish_first = last_exchange(0, pt1_ref, (4, 5, 6, 7))
    need("tok", "vs")
    vsum[9:11, 0:512] = vs[9:11, :]
    norm_back(tok, 0, dx, None, 0)
    st(2, "q2", "q3")
    send_small(vec_cols())
    dh[0:512 - ROWS, :] = jnp.zeros((512 - ROWS, 768), f32)
    tgs = [pltpu.make_async_copy(dx, tg_ref.at[0:ROWS], tsem.at[0]), pltpu.make_async_copy(dh.at[0:512 - ROWS], tg_ref.at[ROWS:512], tsem.at[1])]
    for t in tgs: t.start()
    st(3, "q1"); st(4, "q0"); st(6, "fc2")
    st(3, "q2", "q3"); st(5, "q0"); st(4, "q1"); st(7, "fc2")
    finish_fc2 = fc2_exchange()
    st(4, "q2", "q3"); st(5, "q1")
    sum_small()
    finish_fc2(); finish_first()
    st(5, "q2", "q3")
    finish_second = last_exchange(1, pt2_ref, (0, 1, 2, 3, 8))
    for h in range(2):
        for u in range(4):
            of1_ref[:, h * 1536 + u * LW:h * 1536 + (u + 1) * LW] = fo[h, 6 * u:6 * u + 6, :]
    finish_second()
    for h in range(2):
        for u in range(3):
            for b in range(3):
                first = 768 * b + 128 * (3 * h + u)
                oq_ref[:, first:first + 128] = fo[h, 32 + 6 * u:38 + 6 * u, 128 * b:128 * b + 128]
        oo_ref[:, h * LW:(h + 1) * LW] = fo[h, 50:56, :]
        od_ref[:, h * 256:(h + 1) * 256] = fo[h, 56:62, 0:256]
    vt[0:6, :] = fo[0, 56:62, 256:384] + fo[1, 56:62, 256:384]
    vrows = vt[...].T
    for i, r in enumerate((v0_ref, v1_ref, v2_ref, v3_ref, v4_ref)):
        r[...] = vrows[i:i + 1, 0:6]
    for q in range(4):
        vf_ref[:, 6 * q:6 * q + 6] = vrows[5 + q:6 + q, 0:6]
    vd_ref[...] = vrows[9:10, 0:4]
    vm_ref[...] = vrows[10:11, 0:4]
    finish_cells()
    for t in tgs: t.wait()
    for cp in lasts: cp.wait_send()
    for cp in sends.values(): cp.wait_send()


def k2_call(*args):
    S = jax.ShapeDtypeStruct
    vm = pl.BlockSpec(memory_space=pltpu.VMEM)
    anyspec = pl.BlockSpec(memory_space=pl.ANY)
    V, DMA = pltpu.VMEM, pltpu.SemaphoreType.DMA
    outs = (S((512, 768), f32), S((33, 64, 512), bf16), S((6, 2304), f32), S((6, 768), f32), S((6, 3072), f32), S((24, 768), f32),
            S((6, 512), f32)) + (S((1, 6), f32),) * 5 + (S((1, 24), f32), S((1, 4), f32), S((1, 4), f32))
    return pl.pallas_call(
        k2_kernel,
        out_shape=outs,
        in_specs=[anyspec] * 18 + [vm] * 4,
        out_specs=[anyspec] * 2 + [vm] * 13,
        scratch_shapes=[
            V((8, 3072), f32), V((ROWS, 768), bf16), V((ROWS, 2304), bf16), V((ROWS, 768), bf16), V((ROWS, 768), f32),
            V((ROWS, 768), bf16), V((ROWS, 3072), bf16), V((ROWS, 3072), bf16), V((ROWS, 768), bf16), V((ROWS, 512), bf16),
            V((ROWS, 768), f32), V((ROWS, 768), bf16), V((16, 512), f32), V((ROWS, 768), bf16),
            V((2, 4, 4, 4, 48, LW), bf16), V((2, 4, 4, 4, 48, LW), bf16),
            V((4, 4, 4, 48, LW), bf16), V((4, 4, 4, 48, LW), bf16), V((1, 4, 4, 48, LW), bf16),
            V((9, 4, 4, 48, LW), bf16), V((4, 4, 4, 48, LW), bf16),
            V((9, 4, 4, 48, LW), bf16), V((4, 4, 4, 48, LW), bf16),
            V((3, 9, 4, 48, LW), bf16), V((3, 4, 4, 48, LW), bf16),
            V((3, 9, 48, LW), bf16), V((3, 4, 48, LW), bf16), V((3, 48, LW), bf16),
            V((ROWS, 768), f32), V((ROWS, 3072), bf16), V((ROWS, 2304), bf16), V((16, 3072), f32), V((2, 2, ROWS, ROWS), bf16),
            V((8, YROWS, LW), bf16), V((8, YROWS, LW), bf16), V((2, YROWS, LW), f32), V((2, 32, LW), bf16), V((32, LW), bf16), V((64, 512), bf16), V((128, 128), f32), V((4, 4, 48, 128), bf16), V((16, 48, 128), bf16),
            DMA((10, 13)), DMA((10, 13)), DMA((2, 8)), DMA((2, 8)), DMA((2,)), DMA((1,)), DMA((2,)), DMA((2,)), DMA((16,)),
            DMA((32,)), DMA((32,)), DMA((3,)), DMA((16,)), DMA((16,)),
        ],
        compiler_params=pltpu.CompilerParams(collective_id=1, has_side_effects=True, vmem_limit_bytes=60 * 2**20),
        cost_estimate=pl.CostEstimate(flops=12 * 10**9, bytes_accessed=5 * 10**7, transcendentals=0),
        name="backward",
    )(*args, jnp.asarray(spread_matrix((4, 5, 6, 7), 0), bf16), jnp.asarray(spread_matrix((0, 1, 2, 3, 8), 32), bf16),
      jnp.asarray(cell_spread(), bf16), jnp.asarray(fc1_bias_spread(), bf16))


def k3_kernel(inv, arr, tg, *refs):
    n = len(refs) - 3
    small, (grid, tg_out, *outs), (gv, tv, sem) = refs[:13], refs[13:n], refs[n:]
    part = lambda i: pl.ds(128 * i, 128)
    ins = [pltpu.make_async_copy(tg.at[part(i)], tv.at[part(i)], sem.at[i]) for i in range(4)]
    ins += [pltpu.make_async_copy(arr.at[inv[0, r]], gv.at[r], sem.at[4 + r]) for r in range(32)]
    for cp in ins: cp.start()
    for a, b in zip(small, outs): b[...] = a[...]
    back = [pltpu.make_async_copy(tv.at[part(i)], tg_out.at[part(i)], sem.at[36 + i]) for i in range(4)]
    back += [pltpu.make_async_copy(gv.at[pl.ds(4 * i, 4)], grid.at[pl.ds(4 * i, 4)], sem.at[40 + i]) for i in range(8)]
    for i in range(4):
        ins[i].wait()
        back[i].start()
    for i in range(8):
        for r in range(4): ins[4 + 4 * i + r].wait()
        back[4 + i].start()
    for cp in back: cp.wait()


def k3_call(inv, arr, tg, *small):
    S = jax.ShapeDtypeStruct
    vm = pl.BlockSpec(memory_space=pltpu.VMEM)
    anyspec = pl.BlockSpec(memory_space=pl.ANY)
    return pl.pallas_call(
        k3_kernel,
        out_shape=(S((32, 64, 512), bf16), S((512, 768), f32)) + tuple(S(t.shape, t.dtype) for t in small),
        in_specs=[pl.BlockSpec(memory_space=pltpu.SMEM), anyspec, anyspec] + [vm] * 13,
        out_specs=[anyspec, anyspec] + [vm] * 13,
        scratch_shapes=[pltpu.VMEM((32, 64, 512), bf16), pltpu.VMEM((512, 768), f32), pltpu.SemaphoreType.DMA((48,))],
        name="results",
    )(inv, arr, tg, *small)


def body(tokens, chip_lengths, chip_ids, positions, ln1_gain, ln1_bias, qkv_weight, out_weight, ln2_gain, ln2_bias, fc1_weight,
         fc1_bias, fc2_weight, fc2_bias, dec_weight, dec_bias, mask_token, grid_cotangent):
    row = lambda v: v.reshape(1, -1)
    *saved, inv = k1_call(chip_ids, chip_lengths, row(positions), tokens, row(ln1_gain), row(ln1_bias), qkv_weight, out_weight,
                          row(ln2_gain), row(ln2_bias), fc1_weight, row(fc1_bias), fc2_weight, row(fc2_bias), dec_weight,
                          row(dec_bias), row(mask_token), grid_cotangent)
    tg, arrived, *small = k2_call(*saved, tokens)
    grid, tg, dq, do, df1, df2, dd, *v = k3_call(inv, arrived, tg, *small)
    v = [t.reshape(-1) for t in v]
    return (grid, tg, v[0], v[1], dq, do, v[2], v[3], df1, v[5], df2, v[4], dd, v[6], v[7])


def solution(mesh):
    both = ("dp", "fsdp")
    r1, r2, grid = P(both), P(both, None), P("dp", "fsdp", None)
    weights = (r1, r1, r2, r2, r1, r1, r2, r1, r2, r1, r2, r1, r1)
    return jax.shard_map(body, mesh=mesh, in_specs=(r2, r1, r1, r1) + weights + (grid,), out_specs=(grid, r2) + weights,
                         check_vma=False)
```
